128 devices in a mesh: bulk: 16 (over y, x), coarse: 8 (over z, core).
Axes of the slice: x: 4, y: 4, z: 4, core: 2. Of those that a mesh axis runs over, the one named last changes fastest.
Arguments:
- diag_blocks: bfloat16 [2048, 128, 128], P(('bulk', 'coarse')), as said below
- off_blocks: bfloat16 [2048, 3, 128, 128], P(('bulk', 'coarse')), may hold values from -0.125 to 0.125
- off_columns: int32 [2048, 3], P(('bulk', 'coarse')), may hold values from 0 to 31
- tentative: bfloat16 [2048, 128, 128], P(('bulk', 'coarse')), may hold values from -2 to 2
- aggregate: int32 [2048], P(('bulk', 'coarse')), may hold values from 0 to 1
- send_rows: int32 [512, 4], P(('bulk', 'coarse')), may hold values from 0 to 15
Outputs:
- coarse_op: float32 [256, 128, 3328], P(('bulk', 'coarse'))
The draws below stay inside these ranges and needn't reach their ends.
Inputs may be any that keep to these rules, and one draw needn't show every extreme that they name: `diag_blocks`: every block's diagonal entries lie between 1 and 2.
All inputs are finite; a program needn't handle non-finite values.
Results may differ from the reference program's by a relative error of at most 0.0017.
Values may be sent and summed in bfloat16 or wider, within the bound.
No kernel may reach another device: no remote copies, remote signals or barrier semaphores. Data moves between devices by JAX's collectives and lax.ppermute only.
A program may use at most 256 MiB of HBM per device.

```python
import jax
import jax.numpy as jnp
from jax import lax

BLOCK = 128
CWIDTH = 128
BLK_DEV = 16
CB_DEV = 2
OFFDIAG = 3
GHOSTS = 4
BLOCKS = 2048
CBLKS = 256
N_BULK = 16
N_COARSE = 8


def draw_diag_blocks(key, part):
    first_key, second_key = jax.random.split(key, 2)
    spread = (4.0 * BLOCK * (OFFDIAG + 1)) ** (-0.5)
    noise = jax.random.normal(first_key, (BLOCKS, BLOCK, BLOCK), jnp.float32) * spread
    diagonal = jax.random.uniform(second_key, (BLOCKS, BLOCK), jnp.float32, 1.0, 2.0)
    identity = jnp.eye(BLOCK, dtype=jnp.float32)
    return (noise * (1.0 - identity) + identity * diagonal[:, :, None]).astype(jnp.bfloat16)


def place_ends(entries, rng, least, top_value):
    index_at = [jax.random.randint(jax.random.fold_in(rng, axis), (), 0, length) for axis, length in enumerate(entries.shape)]
    main_axis = entries.shape.index(max(entries.shape))
    beside = index_at[:main_axis] + [(index_at[main_axis] + 1) % entries.shape[main_axis]] + index_at[main_axis + 1:]
    return entries.at[tuple(index_at)].set(least).at[tuple(beside)].set(top_value)


def shard_levels(key, shape, cuts, least, largest):
    level = 1.0
    for position, parts in cuts:
        draws = jax.random.uniform(jax.random.fold_in(jax.random.fold_in(key, 6), position), (parts,), jnp.float32, least / len(cuts), largest / len(cuts))
        level = level * jnp.repeat(jnp.exp(draws), shape[position] // parts).reshape((-1,) + (1,) * (len(shape) - 1 - position))
    return level


def scatter_about(own_key, extent, deviation, limit, cuts=(), kind=jnp.bfloat16):
    values = jax.random.normal(own_key, extent, jnp.float32) * deviation
    if len(cuts) > 0:
        values = shard_levels(own_key, extent, cuts, -0.22, 0.18) * values
    return jnp.clip(values, min=-limit, max=limit).astype(kind)


def setup_inputs(seed: int = 0) -> dict:
    streams_of = jax.random.split(jax.random.key(seed), 7)
    diag_blocks = draw_diag_blocks(jax.random.fold_in(streams_of[6], 71), 0)
    off_blocks = scatter_about(streams_of[1], (BLOCKS, OFFDIAG, BLOCK, BLOCK), (4 * BLOCK * (OFFDIAG + 1)) ** -0.5, 0.125, ((0, 128),))
    off_columns = place_ends(jax.random.randint(streams_of[2], (BLOCKS, OFFDIAG), 0, BLK_DEV + 4 * GHOSTS), jax.random.fold_in(streams_of[2], 1), 0, (BLK_DEV + 4 * GHOSTS) - 1).astype(jnp.int32)
    tentative = scatter_about(streams_of[3], (BLOCKS, BLOCK, CWIDTH), (2.0 / (BLK_DEV * BLOCK // CB_DEV) ** 0.25), 2.0, ((0, 128),))
    aggregate = place_ends(jax.random.randint(streams_of[4], (BLOCKS,), 0, CB_DEV), jax.random.fold_in(streams_of[4], 1), 0, CB_DEV - 1).astype(jnp.int32)
    send_rows = place_ends(jax.random.randint(streams_of[5], (4 * N_BULK * N_COARSE, GHOSTS), 0, BLK_DEV), jax.random.fold_in(streams_of[5], 1), 0, BLK_DEV - 1).astype(jnp.int32)
    return {"diag_blocks": diag_blocks, "off_blocks": off_blocks, "off_columns": off_columns, "tentative": tentative, "aggregate": aggregate, "send_rows": send_rows}


damping = 0.6


def expand_window(slot_values, slot_labels, width_blocks):
    select = (slot_labels[:, :, None] == jnp.arange(width_blocks, dtype=jnp.int32)[None, None, :]).astype(jnp.float32)
    dense_rows = jnp.einsum('rkw,rkic->riwc', select, slot_values, precision=lax.Precision.HIGHEST)
    return dense_rows.reshape(slot_values.shape[0], slot_values.shape[2], width_blocks * CWIDTH)


def column_map(off_columns, send_rows):
    devices = N_BULK * N_COARSE
    block_ids = jnp.arange(BLOCKS, dtype=jnp.int32)
    partition = (block_ids // BLK_DEV)[:, None]
    is_local = off_columns < BLK_DEV
    ghost_index = jnp.maximum(off_columns - BLK_DEV, 0)
    neighbour = ghost_index // GHOSTS
    within = ghost_index % GHOSTS
    offsets = jnp.array([1, -1, 2, -2], dtype=jnp.int32)
    source = partition - offsets[neighbour]
    present = (source >= 0) & (source < devices)
    source_safe = jnp.clip(source, 0, devices - 1).astype(jnp.int32)
    remote_row = send_rows[source_safe * 4 + neighbour, within]
    global_col = jnp.where(is_local, partition * BLK_DEV + off_columns, source_safe * BLK_DEV + remote_row)
    has_column = is_local | present
    return global_col.astype(jnp.int32), has_column


def smooth_rows(row_ids, anchor, diag_blocks, off_blocks, tentative, labels, global_col, has_column):
    own_diag = diag_blocks[row_ids].astype(jnp.float32)
    inv_diag = 1.0 / jnp.diagonal(own_diag, axis1=1, axis2=2)
    own_tent = tentative[row_ids].astype(jnp.float32)
    near_cols = global_col[row_ids]
    alive_mask = has_column[row_ids].astype(jnp.float32)
    near_tent = tentative[near_cols].astype(jnp.float32) * alive_mask[:, :, None, None]
    own_term = jnp.einsum('rij,rjc->ric', own_diag, own_tent, precision=lax.Precision.HIGHEST)
    off_term = jnp.einsum('rkij,rkjc->rkic', off_blocks[row_ids].astype(jnp.float32), near_tent, precision=lax.Precision.HIGHEST)
    first_slot = own_tent - damping * inv_diag[:, :, None] * own_term
    others = -damping * inv_diag[:, None, :, None] * off_term
    slot_values = jnp.concatenate([first_slot[:, None], others], axis=1).astype(jnp.bfloat16)
    slot_labels = jnp.concatenate([labels[row_ids][:, None], labels[near_cols]], axis=1) - anchor * CB_DEV
    return slot_values, slot_labels.astype(jnp.int32)


def reference(diag_blocks, off_blocks, off_columns, tentative, aggregate, send_rows):
    global_col, has_column = column_map(off_columns, send_rows)
    labels = ((jnp.arange(BLOCKS, dtype=jnp.int32) // BLK_DEV) * CB_DEV + aggregate).astype(jnp.int32)
    row_span = CB_DEV * CWIDTH
    frame_width = 9 * row_span
    band_width = 13 * row_span

    def one_part(summed, partition):
        row_ids = (partition * BLK_DEV + jnp.arange(BLK_DEV, dtype=jnp.int32)).astype(jnp.int32)
        anchor = partition - 4
        own_slots, own_labels = smooth_rows(row_ids, anchor, diag_blocks, off_blocks, tentative, labels, global_col, has_column)
        prolong = expand_window(own_slots.astype(jnp.float32), own_labels, 9 * CB_DEV)
        near_cols = global_col[row_ids].reshape(-1)
        near_slots, near_labels = smooth_rows(near_cols, anchor, diag_blocks, off_blocks, tentative, labels, global_col, has_column)
        near_prol = expand_window(near_slots.astype(jnp.float32), near_labels, 9 * CB_DEV)
        near_prol = near_prol.reshape(BLK_DEV, OFFDIAG, BLOCK, frame_width)
        alive_mask = has_column[row_ids].astype(jnp.float32)
        near_float = near_prol * alive_mask[:, :, None, None]
        applied = jnp.einsum('rij,rjc->ric', diag_blocks[row_ids].astype(jnp.float32), prolong, precision=lax.Precision.HIGHEST)
        applied = applied + jnp.einsum('rkij,rkjc->ric', off_blocks[row_ids].astype(jnp.float32), near_float, precision=lax.Precision.HIGHEST)
        applied = applied.astype(jnp.bfloat16)
        compact = prolong[:, :, 2 * row_span:7 * row_span].reshape(-1, 5 * row_span)
        flat_applied = applied.astype(jnp.float32).reshape(-1, frame_width)
        partial_value = jnp.dot(compact.T, flat_applied, precision=lax.Precision.HIGHEST)
        pieces = []
        for level in range(5):
            row_piece = partial_value[level * row_span:(level + 1) * row_span]
            pieces.append(jnp.pad(row_piece, ((0, 0), ((4 - level) * row_span, level * row_span))))
        banded = jnp.concatenate(pieces, axis=0)
        row_start = (partition * row_span).astype(jnp.int32)
        zero_index = jnp.zeros((), jnp.int32)
        current = lax.dynamic_slice(summed, (row_start, zero_index), (5 * row_span, band_width))
        summed = lax.dynamic_update_slice(summed, current + banded, (row_start, zero_index))
        return summed, None

    devices = N_BULK * N_COARSE
    start_sum = jnp.zeros(((devices + 4) * row_span, band_width), jnp.float32)
    summed, _ = lax.scan(one_part, start_sum, jnp.arange(devices, dtype=jnp.int32))
    return summed[2 * row_span:2 * row_span + CBLKS * CWIDTH].reshape(CBLKS, CWIDTH, band_width)
```

```python
import jax
import jax.numpy as jnp
from jax import lax
from jax.experimental import pallas as pl
from jax.experimental.pallas import tpu as pltpu
from jax.sharding import PartitionSpec as P

AXES = ("bulk", "coarse")
OFFSETS = (1, -1, 2, -2)
BS = 128
NB = 16
NG = 4
NT = NB + 4 * NG
FRAME = 18
WIDE = FRAME * BS
SLOTW = 4 * BS
EXTRA = 16
BF = jnp.bfloat16
F32 = jnp.float32
SMEM = pltpu.SMEM
ANY = pl.ANY
VMEM_LIMIT = 56 * 1024 * 1024


def spec(space):
    return pl.BlockSpec(memory_space=space)


def shift(value, steps):
    count = lax.axis_size(AXES)
    first, last = max(0, -steps), min(count, count - steps)
    return lax.ppermute(value, AXES, [(s, s + steps) for s in range(first, last)])


def label_rows(values, width):
    lane = lax.broadcasted_iota(jnp.int32, (EXTRA, width), 1)
    total = jnp.zeros((EXTRA, width), jnp.int32)
    for at, value in enumerate(values):
        total = jnp.where(lane == at, value, total)
    return total.astype(F32).astype(BF)


def pack_kernel(send_rows, aggregate, tent, *refs):
    outs, labels, sem = refs[:4], refs[4], refs[5]
    copies = []
    for n in range(4):
        for g in range(NG):
            copies.append(
                pltpu.make_async_copy(
                    tent.at[send_rows[n, g]], outs[n].at[pl.ds(g * BS, BS)], sem.at[n, g]
                )
            )
    for copy in copies:
        copy.start()
    for n in range(4):
        labels[n] = label_rows([aggregate[send_rows[n, g]] for g in range(NG)], BS)
        copy = pltpu.make_async_copy(labels.at[n], outs[n].at[pl.ds(NG * BS, EXTRA)], sem.at[n, NG])
        copy.start()
        copies.append(copy)
    for copy in copies:
        copy.wait()


def pack(send_rows, aggregate, tent):
    shape = jax.ShapeDtypeStruct((NG * BS + EXTRA, BS), BF)
    return pl.pallas_call(
        pack_kernel,
        out_shape=[shape] * 4,
        in_specs=[spec(SMEM), spec(SMEM), spec(ANY)],
        out_specs=[spec(ANY)] * 4,
        scratch_shapes=[pltpu.VMEM((4, EXTRA, BS), BF), pltpu.SemaphoreType.DMA((4, NG + 1))],
        name="pack",
    )(send_rows, aggregate, tent)


def slots_kernel(
    send_rows, off_columns, aggregate, diag, off, tent, g0, g1, g2, g3,
    own_labels, slots, slots_t, s0, s1, s2, s3,
    table, labels_in, labels_out, label_smem, slot_buf, sem_in, sem_lab, sem_out,
):
    ghosts, sends = (g0, g1, g2, g3), (s0, s1, s2, s3)
    copies = [pltpu.make_async_copy(tent, table.at[pl.ds(0, NB)], sem_in.at[0])]
    for n in range(4):
        for g in range(NG):
            copies.append(
                pltpu.make_async_copy(
                    ghosts[n].at[pl.ds(g * BS, BS)], table.at[NB + n * NG + g], sem_in.at[1 + n * NG + g]
                )
            )
    lab = [
        pltpu.make_async_copy(ghosts[n].at[pl.ds(NG * BS, EXTRA)], labels_out.at[n, :, pl.ds(0, BS)], sem_lab.at[n])
        for n in range(4)
    ]
    for copy in lab + copies:
        copy.start()
    for copy in lab:
        copy.wait()
    for n in range(4):
        labels_in[n] = labels_out[n, :, pl.ds(0, BS)].astype(F32).astype(jnp.int32)[:8]
    to_smem = pltpu.make_async_copy(labels_in, label_smem, sem_lab.at[0])
    to_smem.start()
    for copy in copies:
        copy.wait()
    to_smem.wait()

    eye = lax.broadcasted_iota(jnp.int32, (BS, BS), 0) == lax.broadcasted_iota(jnp.int32, (BS, BS), 1)

    def row(i, carry):
        block = diag[i]
        inv = 1.0 / jnp.sum(jnp.where(eye, block.astype(F32), 0.0), axis=1, keepdims=True)
        scale = 0.6 * inv
        own = table[i]
        first = own.astype(F32) - scale * jnp.dot(block, own, preferred_element_type=F32)
        parts = [first]
        for k in range(3):
            near = table[off_columns[i, k]]
            parts.append(-scale * jnp.dot(off[i, k], near, preferred_element_type=F32))
        for k in range(4):
            slot = parts[k].astype(BF)
            slot_buf[i, :, k * BS : (k + 1) * BS] = slot
            slots_t[i, k * BS : (k + 1) * BS, :] = slot.T
        own_labels[i, 0] = aggregate[i] + 8
        for k in range(3):
            c = off_columns[i, k]
            ghost = jnp.maximum(c - NB, 0)
            n = lax.div(ghost, NG)
            base = 8 - 2 * jnp.where(n == 0, 1, jnp.where(n == 1, -1, jnp.where(n == 2, 2, -2)))
            remote = label_smem[n, 0, lax.rem(ghost, NG)] + base
            local = aggregate[jnp.minimum(c, NB - 1)] + 8
            own_labels[i, k + 1] = jnp.where(c < NB, local, remote)
        return carry

    lax.fori_loop(0, NB, row, 0)

    outs = [pltpu.make_async_copy(slot_buf, slots, sem_out.at[0])]
    for n in range(4):
        for g in range(NG):
            outs.append(
                pltpu.make_async_copy(
                    slot_buf.at[send_rows[n, g]], sends[n].at[pl.ds(g * BS, BS)], sem_out.at[1 + n * NG + g]
                )
            )
    for copy in outs:
        copy.start()
    for n in range(4):
        values = [own_labels[send_rows[n, g], k] for g in range(NG) for k in range(4)]
        labels_out[n] = label_rows(values, SLOTW)
        copy = pltpu.make_async_copy(labels_out.at[n], sends[n].at[pl.ds(NG * BS, EXTRA)], sem_lab.at[n])
        copy.start()
        outs.append(copy)
    for copy in outs:
        copy.wait()


def make_slots(send_rows, off_columns, aggregate, diag, off, tent, ghosts):
    send = jax.ShapeDtypeStruct((NG * BS + EXTRA, SLOTW), BF)
    return pl.pallas_call(
        slots_kernel,
        out_shape=[
            jax.ShapeDtypeStruct((NB, 4), jnp.int32),
            jax.ShapeDtypeStruct((NB, BS, SLOTW), BF),
            jax.ShapeDtypeStruct((NB, SLOTW, BS), BF),
        ]
        + [send] * 4,
        in_specs=[spec(SMEM)] * 3 + [spec(pltpu.VMEM)] * 2 + [spec(ANY)] * 5,
        out_specs=[spec(SMEM), spec(ANY), spec(pltpu.VMEM)] + [spec(ANY)] * 4,
        scratch_shapes=[
            pltpu.VMEM((NT, BS, BS), BF),
            pltpu.VMEM((4, 8, BS), jnp.int32),
            pltpu.VMEM((4, EXTRA, SLOTW), BF),
            pltpu.SMEM((4, 8, BS), jnp.int32),
            pltpu.VMEM((NB, BS, SLOTW), BF),
            pltpu.SemaphoreType.DMA((1 + 4 * NG,)),
            pltpu.SemaphoreType.DMA((4,)),
            pltpu.SemaphoreType.DMA((1 + 4 * NG,)),
        ],
        compiler_params=pltpu.CompilerParams(vmem_limit_bytes=VMEM_LIMIT),
        name="slots",
    )(send_rows, off_columns, aggregate, diag, off, tent, *ghosts)


def coarse_kernel(
    off_columns, own_labels, diag, off, slots, slots_t, g0, g1, g2, g3,
    own_rows, s0, s1, s2, s3,
    table, labels_in, labels_vmem, label_smem, total, applied, coarse, sem_in, sem_lab,
):
    ghosts, sends = (g0, g1, g2, g3), (s0, s1, s2, s3)
    copies = [pltpu.make_async_copy(slots, table.at[pl.ds(0, NB)], sem_in.at[0])]
    for n in range(4):
        for g in range(NG):
            copies.append(
                pltpu.make_async_copy(
                    ghosts[n].at[pl.ds(g * BS, BS)], table.at[NB + n * NG + g], sem_in.at[1 + n * NG + g]
                )
            )
    lab = [
        pltpu.make_async_copy(ghosts[n].at[pl.ds(NG * BS, EXTRA), pl.ds(0, BS)], labels_in.at[n], sem_lab.at[n])
        for n in range(4)
    ]
    for copy in lab + copies:
        copy.start()
    coarse[...] = jnp.zeros_like(coarse)
    for copy in lab:
        copy.wait()
    for n in range(4):
        labels_vmem[n] = labels_in[n].astype(F32).astype(jnp.int32)[:8] - 2 * OFFSETS[n]
    to_smem = pltpu.make_async_copy(labels_vmem, label_smem, sem_lab.at[0])
    to_smem.start()
    for copy in copies:
        copy.wait()
    to_smem.wait()

    def label_of(j, m):
        ghost = jnp.maximum(j - NB, 0)
        remote = label_smem[lax.div(ghost, NG), 0, lax.rem(ghost, NG) * 4 + m]
        local = own_labels[jnp.minimum(j, NB - 1), m]
        return jnp.clip(jnp.where(j < NB, local, remote), 0, FRAME - 1)

    def row(i, carry):
        total[...] = jnp.zeros_like(total)
        for k in range(4):
            j = i if k == 0 else off_columns[i, k - 1]
            block = diag[i] if k == 0 else off[i, k - 1]
            prod = jnp.dot(block, table[j], preferred_element_type=F32)
            for m in range(4):
                at = label_of(j, m)
                total[at] = total[at] + prod[:, m * BS : (m + 1) * BS]
        for at in range(FRAME):
            applied[:, at * BS : (at + 1) * BS] = total[at].astype(BF)
        left = slots_t[i]
        targets = [jnp.clip(own_labels[i, s] - 4, 0, 9) for s in range(4)]
        for t in range(FRAME // 2):
            cols = slice(t * 2 * BS, (t + 1) * 2 * BS)
            res = jnp.dot(left, applied[:, cols], preferred_element_type=F32)
            for s in range(4):
                coarse[targets[s], :, cols] = coarse[targets[s], :, cols] + res[s * BS : (s + 1) * BS]
        return carry

    lax.fori_loop(0, NB, row, 0)
    own_rows[...] = coarse[4:6]
    for n in range(4):
        level = OFFSETS[n] + 2
        sends[n][...] = coarse[2 * level : 2 * level + 2].astype(BF)


def make_coarse(off_columns, own_labels, diag, off, slots, slots_t, ghosts):
    send = jax.ShapeDtypeStruct((2, BS, WIDE), BF)
    return pl.pallas_call(
        coarse_kernel,
        out_shape=[jax.ShapeDtypeStruct((2, BS, WIDE), F32)] + [send] * 4,
        in_specs=[spec(SMEM)] * 2 + [spec(pltpu.VMEM)] * 2 + [spec(ANY), spec(pltpu.VMEM)] + [spec(ANY)] * 4,
        out_specs=[spec(pltpu.VMEM)] * 5,
        scratch_shapes=[
            pltpu.VMEM((NT, BS, SLOTW), BF),
            pltpu.VMEM((4, EXTRA, BS), BF),
            pltpu.VMEM((4, 8, BS), jnp.int32),
            pltpu.SMEM((4, 8, BS), jnp.int32),
            pltpu.VMEM((FRAME, BS, BS), F32),
            pltpu.VMEM((BS, WIDE), BF),
            pltpu.VMEM((10, BS, WIDE), F32),
            pltpu.SemaphoreType.DMA((1 + 4 * NG,)),
            pltpu.SemaphoreType.DMA((4,)),
        ],
        compiler_params=pltpu.CompilerParams(vmem_limit_bytes=VMEM_LIMIT),
        name="coarse",
    )(off_columns, own_labels, diag, off, slots, slots_t, *ghosts)


def local(diag_blocks, off_blocks, off_columns, tentative, aggregate, send_rows):
    sends = pack(send_rows, aggregate, tentative)
    ghosts = [shift(value, by) for value, by in zip(sends, OFFSETS)]
    own_labels, slots, slots_t, *sends = make_slots(
        send_rows, off_columns, aggregate, diag_blocks, off_blocks, tentative, ghosts
    )
    ghosts = [shift(value, by) for value, by in zip(sends, OFFSETS)]
    own_rows, *sends = make_coarse(
        off_columns, own_labels, diag_blocks, off_blocks, slots, slots_t, ghosts
    )

    def band(piece, start):
        lead = start * 2 * BS
        return jnp.pad(piece.astype(F32), ((0, 0), (0, 0), (lead, 26 * BS - lead - WIDE)))

    summed = band(own_rows, 2)
    for value, by in zip(sends, OFFSETS):
        summed = summed + band(shift(value, by), 2 - by)
    return summed


def solution(mesh):
    in_specs = (
        P(AXES, None, None),
        P(AXES, None, None, None),
        P(AXES, None),
        P(AXES, None, None),
        P(AXES),
        P(AXES, None),
    )
    return jax.shard_map(
        local, mesh=mesh, in_specs=in_specs, out_specs=P(AXES, None, None), check_vma=False
    )
```

```python
import jax
import jax.numpy as jnp
from jax import lax
from jax.experimental import pallas as pl
from jax.experimental.pallas import tpu as pltpu
from jax.sharding import PartitionSpec as P

AXES = ("bulk", "coarse")
OFFSETS = (1, -1, 2, -2)
START_ORDER = (2, 3, 0, 1)
BS = 128
NB = 16
NG = 4
NT = NB + 4 * NG
FRAME = 18
WIDE = FRAME * BS
SLOTW = 4 * BS
CHIPWIDE = 20 * BS
BANDWIDE = 26 * BS
TILES = [slice(t * 2 * BS, (t + 1) * 2 * BS) for t in range(FRAME // 2)]
GROUP = 4
CHUNK = 4
EXTRA = 16
BF = jnp.bfloat16
F32 = jnp.float32
SMEM = pltpu.SMEM
ANY = pl.ANY
VMEM_LIMIT = 56 * 1024 * 1024


def spec(space):
    return pl.BlockSpec(memory_space=space)


def shift(value, steps):
    count = lax.axis_size(AXES)
    first, last = max(0, -steps), min(count, count - steps)
    return lax.ppermute(value, AXES, [(s, s + steps) for s in range(first, last)])


def label_rows(values, width):
    lane = lax.broadcasted_iota(jnp.int32, (EXTRA, width), 1)
    total = jnp.zeros((EXTRA, width), jnp.int32)
    for at, value in enumerate(values):
        total = jnp.where(lane == at, value, total)
    return total.astype(F32).astype(BF)


def pack_kernel(send_rows, aggregate, tent, *refs):
    outs, labels, sem = refs[:4], refs[4], refs[5]
    copies = []
    for n in START_ORDER:
        for g in range(NG):
            copies.append(
                pltpu.make_async_copy(
                    tent.at[send_rows[n, g]], outs[n].at[pl.ds(g * BS, BS)], sem.at[n, g]
                )
            )
    for copy in copies:
        copy.start()
    for n in START_ORDER:
        labels[n] = label_rows([aggregate[send_rows[n, g]] for g in range(NG)], BS)
        copy = pltpu.make_async_copy(labels.at[n], outs[n].at[pl.ds(NG * BS, EXTRA)], sem.at[n, NG])
        copy.start()
        copies.append(copy)
    for copy in copies:
        copy.wait()


def pack(send_rows, aggregate, tent):
    shape = jax.ShapeDtypeStruct((NG * BS + EXTRA, BS), BF)
    return pl.pallas_call(
        pack_kernel,
        out_shape=[shape] * 4,
        in_specs=[spec(SMEM), spec(SMEM), spec(pltpu.VMEM)],
        out_specs=[spec(ANY)] * 4,
        scratch_shapes=[pltpu.VMEM((4, EXTRA, BS), BF), pltpu.SemaphoreType.DMA((4, NG + 1))],
        name="pack",
    )(send_rows, aggregate, tent)


def local_slots_kernel(off_columns, aggregate, diag, off, tent, labels, ghost_list, ghost_count, slots, scales):
    eye = lax.broadcasted_iota(jnp.int32, (BS, BS), 0) == lax.broadcasted_iota(jnp.int32, (BS, BS), 1)
    ghost_count[0] = 0

    def row(i, carry):
        block = diag[i]
        inv = 1.0 / jnp.sum(jnp.where(eye, block.astype(F32), 0.0), axis=1, keepdims=True)
        scale = 0.6 * inv
        scales[i] = jnp.broadcast_to(scale, (BS, BS))
        own = tent[i]
        first = own.astype(F32) - scale * jnp.dot(block, own, preferred_element_type=F32)
        slots[i, :, :BS] = first.astype(BF)
        labels[i, 0] = aggregate[i] + 8
        for k in range(1, 4):
            c = off_columns[i, k - 1]
            near = tent[jnp.minimum(c, NB - 1)]
            part = -scale * jnp.dot(off[i, k - 1], near, preferred_element_type=F32)
            slots[i, :, k * BS : (k + 1) * BS] = part.astype(BF)
            labels[i, k] = aggregate[jnp.minimum(c, NB - 1)] + 8
            at = ghost_count[0]
            ghost_list[at] = i * 4 + k
            ghost_count[0] = at + jnp.where(c < NB, 0, 1)
        return carry

    lax.fori_loop(0, NB, row, 0, unroll=4)
    at = ghost_count[0]
    for d in range(GROUP):
        ghost_list[at + d] = NB * 4 + 1


def local_slots(off_columns, aggregate, diag, off, tent):
    return pl.pallas_call(
        local_slots_kernel,
        out_shape=[
            jax.ShapeDtypeStruct((NB, 4), jnp.int32),
            jax.ShapeDtypeStruct((3 * NB + GROUP,), jnp.int32),
            jax.ShapeDtypeStruct((1,), jnp.int32),
            jax.ShapeDtypeStruct((NB, BS, SLOTW), BF),
            jax.ShapeDtypeStruct((NB, BS, BS), F32),
        ],
        in_specs=[spec(SMEM)] * 2 + [spec(pltpu.VMEM)] * 3,
        out_specs=[spec(SMEM)] * 3 + [spec(pltpu.VMEM)] * 2,
        compiler_params=pltpu.CompilerParams(vmem_limit_bytes=VMEM_LIMIT),
        cost_estimate=pl.CostEstimate(flops=10**9, bytes_accessed=6 * 10**6, transcendentals=0),
        name="local_slots",
    )(off_columns, aggregate, diag, off, tent)


def ghost_slots_kernel(
    send_rows, off_columns, local_labels, ghost_list, ghost_count, off, slots_in, scales, g2, g3, g0, g1,
    labels, slots, s2, s3, s0, s1,
    table, labels_in, labels_out, label_smem, slot_buf, off_buf, scale_buf, sem_in, sem_lab, sem_out, sem_big,
):
    ghosts, sends = (g0, g1, g2, g3), (s0, s1, s2, s3)
    big = [
        pltpu.make_async_copy(scales, scale_buf, sem_big.at[0]),
        pltpu.make_async_copy(off, off_buf, sem_big.at[1]),
        pltpu.make_async_copy(slots_in, slot_buf.at[pl.ds(0, NB)], sem_big.at[2]),
    ]
    copies = []
    for n in range(4):
        for g in range(NG):
            copies.append(
                pltpu.make_async_copy(
                    ghosts[n].at[pl.ds(g * BS, BS)], table.at[n * NG + g], sem_in.at[n * NG + g]
                )
            )
    lab = [
        pltpu.make_async_copy(ghosts[n].at[pl.ds(NG * BS, EXTRA)], labels_out.at[n, :, pl.ds(0, BS)], sem_lab.at[n])
        for n in range(4)
    ]
    for copy in lab + copies + big:
        copy.start()
    for i in range(NB):
        for k in range(4):
            labels[i, k] = local_labels[i, k]
    for copy in lab:
        copy.wait()
    for n in range(4):
        base = 8 - 2 * OFFSETS[n]
        labels_in[n] = labels_out[n, :, pl.ds(0, BS)].astype(F32).astype(jnp.int32)[:8] + base
    to_smem = pltpu.make_async_copy(labels_in, label_smem, sem_lab.at[0])
    to_smem.start()
    for copy in copies + big:
        copy.wait()
    to_smem.wait()

    def group(q, carry):
        for u in range(GROUP):
            entry = ghost_list[q * GROUP + u]
            i, k = lax.div(entry, 4), lax.rem(entry, 4)
            row = jnp.minimum(i, NB - 1)
            ghost = jnp.clip(off_columns[row, k - 1] - NB, 0, 4 * NG - 1)
            part = jnp.dot(off_buf[row, k - 1], table[ghost], preferred_element_type=F32)
            part = -scale_buf[row] * part
            slot_buf[i, :, pl.ds(pl.multiple_of(k * BS, BS), BS)] = part.astype(BF)
            labels[i, k] = label_smem[lax.div(ghost, NG), 0, lax.rem(ghost, NG)]
        return carry

    lax.fori_loop(0, lax.div(ghost_count[0] + GROUP - 1, GROUP), group, 0)

    outs = []
    for n in START_ORDER:
        for g in range(NG):
            outs.append(
                pltpu.make_async_copy(
                    slot_buf.at[send_rows[n, g]], sends[n].at[pl.ds(g * BS, BS)], sem_out.at[n * NG + g]
                )
            )
    outs.append(pltpu.make_async_copy(slot_buf.at[pl.ds(0, NB)], slots, sem_big.at[0]))
    for copy in outs:
        copy.start()
    for n in START_ORDER:
        values = [labels[send_rows[n, g], k] for g in range(NG) for k in range(4)]
        labels_out[n] = label_rows(values, SLOTW)
        copy = pltpu.make_async_copy(labels_out.at[n], sends[n].at[pl.ds(NG * BS, EXTRA)], sem_lab.at[n])
        copy.start()
        outs.append(copy)
    for copy in outs:
        copy.wait()


def ghost_slots(send_rows, off_columns, local_labels, ghost_list, ghost_count, off, slots_in, scales, ghosts):
    send = jax.ShapeDtypeStruct((NG * BS + EXTRA, SLOTW), BF)
    labels, slots, *sends = pl.pallas_call(
        ghost_slots_kernel,
        out_shape=[
            jax.ShapeDtypeStruct((NB + 1, 4), jnp.int32),
            jax.ShapeDtypeStruct((NB, BS, SLOTW), BF),
        ]
        + [send] * 4,
        in_specs=[spec(SMEM)] * 5 + [spec(ANY)] * 7,
        out_specs=[spec(SMEM)] + [spec(ANY)] * 5,
        scratch_shapes=[
            pltpu.VMEM((4 * NG, BS, BS), BF),
            pltpu.VMEM((4, 8, BS), jnp.int32),
            pltpu.VMEM((4, EXTRA, SLOTW), BF),
            pltpu.SMEM((4, 8, BS), jnp.int32),
            pltpu.VMEM((NB + 1, BS, SLOTW), BF),
            pltpu.VMEM((NB, 3, BS, BS), BF),
            pltpu.VMEM((NB, BS, BS), F32),
            pltpu.SemaphoreType.DMA((4 * NG,)),
            pltpu.SemaphoreType.DMA((4,)),
            pltpu.SemaphoreType.DMA((4 * NG,)),
            pltpu.SemaphoreType.DMA((3,)),
        ],
        compiler_params=pltpu.CompilerParams(vmem_limit_bytes=VMEM_LIMIT),
        name="ghost_slots",
    )(send_rows, off_columns, local_labels, ghost_list, ghost_count, off, slots_in, scales,
      *[ghosts[n] for n in START_ORDER])
    return labels, slots, [sends[START_ORDER.index(n)] for n in range(4)]


def lists_kernel(labels, slots, lists, counts, blocks):
    for t in range(10):
        counts[t] = 0

    def row(i, carry):
        for k in range(4):
            blocks[i * 4 + k] = slots[i, :, k * BS : (k + 1) * BS].T
            t = jnp.clip(labels[i, k] - 4, 0, 9)
            at = counts[t]
            lists[t, at] = i * 4 + k
            counts[t] = at + 1
        return carry

    lax.fori_loop(0, NB, row, 0, unroll=2)
    blocks[4 * NB] = jnp.zeros((BS, BS), BF)
    for t in range(10):
        at = counts[t]
        for d in range(CHUNK - 1):
            lists[t, at + d] = 4 * NB
        counts[t] = lax.div(at + CHUNK - 1, CHUNK)


def make_lists(labels, slots):
    return pl.pallas_call(
        lists_kernel,
        out_shape=[
            jax.ShapeDtypeStruct((10, 4 * NB + CHUNK), jnp.int32),
            jax.ShapeDtypeStruct((10,), jnp.int32),
            jax.ShapeDtypeStruct((4 * NB + 1, BS, BS), BF),
        ],
        in_specs=[spec(SMEM), spec(pltpu.VMEM)],
        out_specs=[spec(SMEM)] * 2 + [spec(pltpu.VMEM)],
        compiler_params=pltpu.CompilerParams(vmem_limit_bytes=VMEM_LIMIT),
        cost_estimate=pl.CostEstimate(flops=10**8, bytes_accessed=6 * 10**6, transcendentals=0),
        name="lists",
    )(labels, slots)


def coarse_rows(t, at, lists, counts, blocks, applied, coarse):
    def chunk(q, carry):
        entries = [lists[t, q * CHUNK + u] for u in range(CHUNK)]
        left = jnp.concatenate([blocks[e] for e in entries], axis=1)
        rows = [jnp.minimum(lax.div(e, 4), NB - 1) for e in entries]
        for cols in TILES:
            right = jnp.concatenate([applied[r, :, cols] for r in rows], axis=0)
            res = jnp.dot(left, right, preferred_element_type=F32)
            coarse[at, :, cols] = coarse[at, :, cols] + res
        return carry

    coarse[at] = jnp.zeros((BS, WIDE), F32)
    lax.fori_loop(0, counts[t], chunk, 0)


def far_kernel(
    parity, off_columns, labels, lists, counts, diag, off, slots, blocks, g2, g3, g0, g1,
    applied_out, relay_out, relayed_out, direct_out,
    table, labels_in, labels_vmem, label_smem, total, applied, coarse, relay, relayed, direct,
    sem_in, sem_lab, sem_out, sem_piece,
):
    ghosts = (g0, g1, g2, g3)
    copies = [pltpu.make_async_copy(slots, table.at[pl.ds(0, NB)], sem_in.at[0])]
    for n in range(4):
        for g in range(NG):
            copies.append(
                pltpu.make_async_copy(
                    ghosts[n].at[pl.ds(g * BS, BS)], table.at[NB + n * NG + g], sem_in.at[1 + n * NG + g]
                )
            )
    lab = [
        pltpu.make_async_copy(ghosts[n].at[pl.ds(NG * BS, EXTRA), pl.ds(0, BS)], labels_in.at[n], sem_lab.at[n])
        for n in range(4)
    ]
    for copy in lab + copies:
        copy.start()
    odd = parity[0] == 1
    relay_level = jnp.where(odd, 3, 1)
    relayed_level = jnp.where(odd, 0, 4)
    rest = pl.ds(pl.multiple_of((1 - parity[0]) * WIDE, BS), 2 * BS)
    relay[:, :, rest] = jnp.zeros((2, BS, 2 * BS), BF)
    relayed[:, :, rest] = jnp.zeros((2, BS, 2 * BS), F32)
    for copy in lab:
        copy.wait()
    for n in range(4):
        labels_vmem[n] = labels_in[n].astype(F32).astype(jnp.int32)[:8] - 2 * OFFSETS[n]
    to_smem = pltpu.make_async_copy(labels_vmem, label_smem, sem_lab.at[0])
    to_smem.start()
    for copy in copies:
        copy.wait()
    to_smem.wait()

    def label_of(j, m):
        ghost = jnp.maximum(j - NB, 0)
        remote = label_smem[lax.div(ghost, NG), 0, lax.rem(ghost, NG) * 4 + m]
        local = labels[jnp.minimum(j, NB - 1), m]
        return jnp.clip(jnp.where(j < NB, local, remote), 0, FRAME - 1)

    def row(i, carry):
        total[...] = jnp.zeros_like(total)
        for k in range(4):
            j = i if k == 0 else off_columns[i, k - 1]
            block = diag[i] if k == 0 else off[i, k - 1]
            prod = jnp.dot(block, table[j], preferred_element_type=F32)
            for m in range(4):
                at = label_of(j, m)
                total[at] = total[at] + prod[:, m * BS : (m + 1) * BS]
        for at in range(FRAME):
            applied[i, :, at * BS : (at + 1) * BS] = total[at].astype(BF)
        pltpu.make_async_copy(applied.at[i], applied_out.at[i], sem_out.at[i]).start()
        return carry

    lax.fori_loop(0, NB, row, 0)
    into = pl.ds(pl.multiple_of(parity[0] * (2 * BS), BS), WIDE)

    def rows_of(level):
        def one(b, carry):
            coarse_rows(2 * level + b, b, lists, counts, blocks, applied, coarse)
            return carry

        lax.fori_loop(0, 2, one, 0)

    rows_of(4 - relayed_level)
    direct[...] = coarse[...].astype(BF)
    pieces = [pltpu.make_async_copy(direct, direct_out, sem_piece.at[0])]
    pieces[-1].start()
    rows_of(relay_level)
    relay[:, :, into] = coarse[...].astype(BF)
    pieces.append(pltpu.make_async_copy(relay, relay_out, sem_piece.at[1]))
    pieces[-1].start()
    rows_of(relayed_level)
    relayed[:, :, into] = coarse[...]
    pieces.append(pltpu.make_async_copy(relayed, relayed_out, sem_piece.at[2]))
    pieces[-1].start()

    def wait(i, carry):
        pltpu.make_async_copy(applied.at[i], applied_out.at[i], sem_out.at[i]).wait()
        return carry

    lax.fori_loop(0, NB, wait, 0)
    for copy in pieces:
        copy.wait()


def make_far(parity, off_columns, labels, lists, counts, diag, off, slots, blocks, ghosts):
    return pl.pallas_call(
        far_kernel,
        out_shape=[
            jax.ShapeDtypeStruct((NB, BS, WIDE), BF),
            jax.ShapeDtypeStruct((2, BS, CHIPWIDE), BF),
            jax.ShapeDtypeStruct((2, BS, CHIPWIDE), F32),
            jax.ShapeDtypeStruct((2, BS, WIDE), BF),
        ],
        in_specs=[spec(SMEM)] * 5 + [spec(pltpu.VMEM)] * 2 + [spec(ANY), spec(pltpu.VMEM)] + [spec(ANY)] * 4,
        out_specs=[spec(ANY)] * 4,
        scratch_shapes=[
            pltpu.VMEM((NT, BS, SLOTW), BF),
            pltpu.VMEM((4, EXTRA, BS), BF),
            pltpu.VMEM((4, 8, BS), jnp.int32),
            pltpu.SMEM((4, 8, BS), jnp.int32),
            pltpu.VMEM((FRAME, BS, BS), F32),
            pltpu.VMEM((NB, BS, WIDE), BF),
            pltpu.VMEM((2, BS, WIDE), F32),
            pltpu.VMEM((2, BS, CHIPWIDE), BF),
            pltpu.VMEM((2, BS, CHIPWIDE), F32),
            pltpu.VMEM((2, BS, WIDE), BF),
            pltpu.SemaphoreType.DMA((1 + 4 * NG,)),
            pltpu.SemaphoreType.DMA((4,)),
            pltpu.SemaphoreType.DMA((NB,)),
            pltpu.SemaphoreType.DMA((3,)),
        ],
        compiler_params=pltpu.CompilerParams(vmem_limit_bytes=VMEM_LIMIT),
        cost_estimate=pl.CostEstimate(flops=4 * 10**9, bytes_accessed=20 * 10**6, transcendentals=0),
        name="far_rows",
    )(parity, off_columns, labels, lists, counts, diag, off, slots, blocks,
      *[ghosts[n] for n in START_ORDER])


def near_kernel(parity, lists, counts, blocks, applied, own, mate, coarse):
    mate_level = jnp.where(parity[0] == 1, 1, 3)

    def one(b, carry):
        t = jnp.where(b < 2, 2 * mate_level + b, b + 2)
        coarse_rows(t, b, lists, counts, blocks, applied, coarse)
        return carry

    lax.fori_loop(0, 4, one, 0)
    own[...] = coarse[2:4]
    mate[...] = coarse[0:2].astype(BF)


def make_near(parity, lists, counts, blocks, applied):
    return pl.pallas_call(
        near_kernel,
        out_shape=[
            jax.ShapeDtypeStruct((2, BS, WIDE), F32),
            jax.ShapeDtypeStruct((2, BS, WIDE), BF),
        ],
        in_specs=[spec(SMEM)] * 3 + [spec(pltpu.VMEM)] * 2,
        out_specs=[spec(pltpu.VMEM)] * 2,
        scratch_shapes=[pltpu.VMEM((4, BS, WIDE), F32)],
        compiler_params=pltpu.CompilerParams(vmem_limit_bytes=VMEM_LIMIT),
        cost_estimate=pl.CostEstimate(flops=4 * 10**9, bytes_accessed=20 * 10**6, transcendentals=0),
        name="near_rows",
    )(parity, lists, counts, blocks, applied)


def add_kernel(starts, *refs):
    pieces, out = refs[:-1], refs[-1]
    out[...] = jnp.zeros_like(out)
    for at, piece in enumerate(pieces):
        cols = pl.ds(pl.multiple_of(starts[at] * (2 * BS), BS), piece.shape[2])
        out[:, :, cols] = out[:, :, cols] + piece[...].astype(F32)


def add_pieces(starts, pieces):
    rows = 16

    def block(width):
        return pl.BlockSpec((2, rows, width), lambda r: (0, r, 0))

    return pl.pallas_call(
        add_kernel,
        grid=(BS // rows,),
        out_shape=jax.ShapeDtypeStruct((2, BS, BANDWIDE), F32),
        in_specs=[spec(SMEM)] + [block(p.shape[2]) for p in pieces],
        out_specs=block(BANDWIDE),
        compiler_params=pltpu.CompilerParams(vmem_limit_bytes=VMEM_LIMIT),
        cost_estimate=pl.CostEstimate(flops=10**6, bytes_accessed=9 * 10**6, transcendentals=0),
        name="add_pieces",
    )(starts, *pieces)


def permute_by(value, even_step, odd_step):
    count = lax.axis_size(AXES)
    pairs = [(s, s + (odd_step if s % 2 else even_step)) for s in range(count)]
    return lax.ppermute(value, AXES, [(s, t) for s, t in pairs if 0 <= t < count])


def exchange(sends):
    arrived = [None] * 4
    for n in START_ORDER:
        arrived[n] = shift(sends[n], OFFSETS[n])
    return arrived


def local(diag_blocks, off_blocks, off_columns, tentative, aggregate, send_rows):
    odd = lax.rem(lax.axis_index(AXES), 2)
    parity = odd.reshape(1)
    ghosts = exchange(pack(send_rows, aggregate, tentative))
    labels, ghost_list, ghost_count, slots, scales = local_slots(
        off_columns, aggregate, diag_blocks, off_blocks, tentative
    )
    labels, slots, sends = ghost_slots(
        send_rows, off_columns, labels, ghost_list, ghost_count, off_blocks, slots, scales, ghosts
    )
    ghosts = exchange(sends)
    lists, counts, blocks = make_lists(labels, slots)
    applied, relay, relayed, direct = make_far(
        parity, off_columns, labels, lists, counts, diag_blocks, off_blocks, slots, blocks, ghosts
    )
    direct_in = permute_by(direct, -2, 2)
    relay_in = permute_by(relay, 1, -1)
    pair_sum = (relayed + relay_in.astype(F32)).astype(BF)
    pair_in = permute_by(pair_sum, 2, -2)
    applied, pair_sum = lax.optimization_barrier((applied, pair_sum))
    own, mate = make_near(parity, lists, counts, blocks, applied)
    mate_in = permute_by(mate, 1, -1)
    starts = jnp.stack([jnp.int32(2), jnp.where(odd == 1, 1, 3), jnp.where(odd == 1, 0, 4), 3 * odd])
    return add_pieces(starts, [own, mate_in, direct_in, pair_in])


def solution(mesh):
    in_specs = (
        P(AXES, None, None),
        P(AXES, None, None, None),
        P(AXES, None),
        P(AXES, None, None),
        P(AXES),
        P(AXES, None),
    )
    return jax.shard_map(
        local, mesh=mesh, in_specs=in_specs, out_specs=P(AXES, None, None), check_vma=False
    )
```

```python
import jax
import jax.numpy as jnp
from jax import lax
from jax.experimental import pallas as pl
from jax.experimental.pallas import tpu as pltpu
from jax.sharding import PartitionSpec as P

AXES = ("bulk", "coarse")
OFFSETS = (1, -1, 2, -2)
START_ORDER = (2, 3, 0, 1)
BS = 128
NB = 16
NG = 4
NT = NB + 4 * NG
FRAME = 18
WIDE = FRAME * BS
SLOTW = 4 * BS
SENDW = 3 * BS
CHIPWIDE = 20 * BS
BANDWIDE = 26 * BS
TILES = [slice(t * 2 * BS, (t + 1) * 2 * BS) for t in range(FRAME // 2)]
GROUP = 4
CHUNK = 4
EXTRA = 16
BF = jnp.bfloat16
F32 = jnp.float32
SMEM = pltpu.SMEM
ANY = pl.ANY
VMEM_LIMIT = 56 * 1024 * 1024


def spec(space):
    return pl.BlockSpec(memory_space=space)


def shift(value, steps):
    count = lax.axis_size(AXES)
    first, last = max(0, -steps), min(count, count - steps)
    return lax.ppermute(value, AXES, [(s, s + steps) for s in range(first, last)])


def label_rows(values, width):
    lane = lax.broadcasted_iota(jnp.int32, (EXTRA, width), 1)
    total = jnp.zeros((EXTRA, width), jnp.int32)
    for at, value in enumerate(values):
        total = jnp.where(lane == at, value, total)
    return total.astype(F32).astype(BF)


def pack_kernel(send_rows, aggregate, tent, diag, *refs):
    outs, labels, sem = refs[:4], refs[4], refs[5]
    copies = []
    for n in START_ORDER:
        for g in range(NG):
            copies.append(
                pltpu.make_async_copy(
                    tent.at[send_rows[n, g]], outs[n].at[pl.ds(g * BS, BS)], sem.at[n, g]
                )
            )
            copies.append(
                pltpu.make_async_copy(
                    diag.at[send_rows[n, g]], outs[n].at[pl.ds((NG + g) * BS, BS)], sem.at[n, NG + g]
                )
            )
    for copy in copies:
        copy.start()
    for n in START_ORDER:
        labels[n] = label_rows([aggregate[send_rows[n, g]] for g in range(NG)], BS)
        copy = pltpu.make_async_copy(labels.at[n], outs[n].at[pl.ds(2 * NG * BS, EXTRA)], sem.at[n, 2 * NG])
        copy.start()
        copies.append(copy)
    for copy in copies:
        copy.wait()


def pack(send_rows, aggregate, tent, diag):
    shape = jax.ShapeDtypeStruct((2 * NG * BS + EXTRA, BS), BF)
    return pl.pallas_call(
        pack_kernel,
        out_shape=[shape] * 4,
        in_specs=[spec(SMEM), spec(SMEM), spec(pltpu.VMEM), spec(pltpu.VMEM)],
        out_specs=[spec(ANY)] * 4,
        scratch_shapes=[pltpu.VMEM((4, EXTRA, BS), BF), pltpu.SemaphoreType.DMA((4, 2 * NG + 1))],
        name="pack",
    )(send_rows, aggregate, tent, diag)


def first_slot(eye, block, own):
    diagonal = jnp.sum(jnp.where(eye, block.astype(F32), 0.0), axis=1, keepdims=True)
    scale = 0.6 * (1.0 / jnp.where(diagonal == 0.0, 1.0, diagonal))
    first = own.astype(F32) - scale * jnp.dot(block, own, preferred_element_type=F32)
    return first.astype(BF), scale


def local_slots_kernel(off_columns, aggregate, diag, off, tent, labels, ghost_list, ghost_count, slots, scales):
    eye = lax.broadcasted_iota(jnp.int32, (BS, BS), 0) == lax.broadcasted_iota(jnp.int32, (BS, BS), 1)
    ghost_count[0] = 0

    def row(i, carry):
        slots[i, :, :BS], scale = first_slot(eye, diag[i], tent[i])
        scales[i] = jnp.broadcast_to(scale, (BS, BS))
        labels[i, 0] = aggregate[i] + 8
        for k in range(1, 4):
            c = off_columns[k - 1, i]
            near = tent[jnp.minimum(c, NB - 1)]
            part = -scale * jnp.dot(off[i, k - 1], near, preferred_element_type=F32)
            slots[i, :, k * BS : (k + 1) * BS] = part.astype(BF)
            labels[i, k] = aggregate[jnp.minimum(c, NB - 1)] + 8
            at = ghost_count[0]
            ghost_list[at] = i * 4 + k
            ghost_count[0] = at + jnp.where(c < NB, 0, 1)
        return carry

    lax.fori_loop(0, NB, row, 0, unroll=4)
    at = ghost_count[0]
    for d in range(GROUP):
        ghost_list[at + d] = NB * 4 + 1


def local_slots(off_columns, aggregate, diag, off, tent):
    return pl.pallas_call(
        local_slots_kernel,
        out_shape=[
            jax.ShapeDtypeStruct((NB, 4), jnp.int32),
            jax.ShapeDtypeStruct((3 * NB + GROUP,), jnp.int32),
            jax.ShapeDtypeStruct((1,), jnp.int32),
            jax.ShapeDtypeStruct((NB, BS, SLOTW), BF),
            jax.ShapeDtypeStruct((NB, BS, BS), F32),
        ],
        in_specs=[spec(SMEM)] * 2 + [spec(pltpu.VMEM)] * 3,
        out_specs=[spec(SMEM)] * 3 + [spec(pltpu.VMEM)] * 2,
        compiler_params=pltpu.CompilerParams(vmem_limit_bytes=10 * 1024 * 1024),
        cost_estimate=pl.CostEstimate(flops=10**9, bytes_accessed=6 * 10**6, transcendentals=0),
        name="local_slots",
    )(off_columns, aggregate, diag, off, tent)


def ghost_slots_kernel(
    send_rows, off_columns, local_labels, ghost_list, ghost_count, off, slots_in, scales, g2, g3, g0, g1,
    labels, slots, s2, s3, s0, s1,
    table, labels_in, labels_out, label_smem, slot_buf, off_buf, scale_buf, sem_in, sem_lab, sem_out, sem_big,
):
    ghosts, sends = (g0, g1, g2, g3), (s0, s1, s2, s3)
    big = [
        pltpu.make_async_copy(scales, scale_buf, sem_big.at[0]),
        pltpu.make_async_copy(off, off_buf, sem_big.at[1]),
        pltpu.make_async_copy(slots_in, slot_buf.at[pl.ds(0, NB)], sem_big.at[2]),
    ]
    copies = []
    for n in range(4):
        for g in range(NG):
            copies.append(
                pltpu.make_async_copy(
                    ghosts[n].at[pl.ds(g * BS, BS)], table.at[n * NG + g], sem_in.at[n * NG + g]
                )
            )
    lab = [
        pltpu.make_async_copy(ghosts[n].at[pl.ds(2 * NG * BS, EXTRA)], labels_out.at[n, :, pl.ds(0, BS)], sem_lab.at[n])
        for n in range(4)
    ]
    for copy in lab + copies + big:
        copy.start()
    for i in range(NB):
        for k in range(4):
            labels[i, k] = local_labels[i, k]
    for copy in lab:
        copy.wait()
    for n in range(4):
        base = 8 - 2 * OFFSETS[n]
        labels_in[n] = labels_out[n, :, pl.ds(0, BS)].astype(F32).astype(jnp.int32)[:8] + base
    to_smem = pltpu.make_async_copy(labels_in, label_smem, sem_lab.at[0])
    to_smem.start()
    for copy in copies + big:
        copy.wait()
    to_smem.wait()

    def group(q, carry):
        for u in range(GROUP):
            entry = ghost_list[q * GROUP + u]
            i, k = lax.div(entry, 4), lax.rem(entry, 4)
            row = jnp.minimum(i, NB - 1)
            ghost = jnp.clip(off_columns[k - 1, row] - NB, 0, 4 * NG - 1)
            part = jnp.dot(off_buf[row, k - 1], table[ghost], preferred_element_type=F32)
            part = -scale_buf[row] * part
            slot_buf[i, :, pl.ds(pl.multiple_of(k * BS, BS), BS)] = part.astype(BF)
            labels[i, k] = label_smem[lax.div(ghost, NG), 0, lax.rem(ghost, NG)]
        return carry

    lax.fori_loop(0, lax.div(ghost_count[0] + GROUP - 1, GROUP), group, 0)

    outs = []
    for n in START_ORDER:
        for g in range(NG):
            outs.append(
                pltpu.make_async_copy(
                    slot_buf.at[send_rows[n, g], :, pl.ds(BS, SENDW)], sends[n].at[pl.ds(g * BS, BS)], sem_out.at[n * NG + g]
                )
            )
    outs.append(pltpu.make_async_copy(slot_buf.at[pl.ds(0, NB)], slots, sem_big.at[0]))
    for copy in outs:
        copy.start()
    for n in START_ORDER:
        values = [labels[send_rows[n, g], k] for g in range(NG) for k in range(4)]
        labels_out[n] = label_rows(values, SENDW)
        copy = pltpu.make_async_copy(labels_out.at[n], sends[n].at[pl.ds(NG * BS, EXTRA)], sem_lab.at[n])
        copy.start()
        outs.append(copy)
    for copy in outs:
        copy.wait()


def ghost_slots(send_rows, off_columns, local_labels, ghost_list, ghost_count, off, slots_in, scales, ghosts):
    send = jax.ShapeDtypeStruct((NG * BS + EXTRA, SENDW), BF)
    labels, slots, *sends = pl.pallas_call(
        ghost_slots_kernel,
        out_shape=[
            jax.ShapeDtypeStruct((NB + 1, 4), jnp.int32),
            jax.ShapeDtypeStruct((NB, BS, SLOTW), BF),
        ]
        + [send] * 4,
        in_specs=[spec(SMEM)] * 5 + [spec(ANY)] * 7,
        out_specs=[spec(SMEM)] + [spec(ANY)] * 5,
        scratch_shapes=[
            pltpu.VMEM((4 * NG, BS, BS), BF),
            pltpu.VMEM((4, 8, BS), jnp.int32),
            pltpu.VMEM((4, EXTRA, SENDW), BF),
            pltpu.SMEM((4, 8, BS), jnp.int32),
            pltpu.VMEM((NB + 1, BS, SLOTW), BF),
            pltpu.VMEM((NB, 3, BS, BS), BF),
            pltpu.VMEM((NB, BS, BS), F32),
            pltpu.SemaphoreType.DMA((4 * NG,)),
            pltpu.SemaphoreType.DMA((4,)),
            pltpu.SemaphoreType.DMA((4 * NG,)),
            pltpu.SemaphoreType.DMA((3,)),
        ],
        compiler_params=pltpu.CompilerParams(vmem_limit_bytes=12 * 1024 * 1024),
        name="ghost_slots",
    )(send_rows, off_columns, local_labels, ghost_list, ghost_count, off, slots_in, scales,
      *[ghosts[n] for n in START_ORDER])
    return labels, slots, [sends[START_ORDER.index(n)] for n in range(4)]


def lists_kernel(labels, slots, g2, g3, g0, g1, lists, counts, blocks, first_slots, ghost_buf, sem):
    ghosts = (g0, g1, g2, g3)
    copies = [
        pltpu.make_async_copy(ghosts[n].at[pl.ds(0, 2 * NG * BS)], ghost_buf.at[n], sem.at[n])
        for n in range(4)
    ]
    for copy in copies:
        copy.start()
    for t in range(10):
        counts[t] = 0

    def row(i, carry):
        for k in range(4):
            blocks[i * 4 + k] = slots[i, :, k * BS : (k + 1) * BS].T
            t = jnp.clip(labels[i, k] - 4, 0, 9)
            at = counts[t]
            lists[t, at] = i * 4 + k
            counts[t] = at + 1
        return carry

    lax.fori_loop(0, NB, row, 0, unroll=2)
    blocks[4 * NB] = jnp.zeros((BS, BS), BF)
    for t in range(10):
        at = counts[t]
        for d in range(CHUNK - 1):
            lists[t, at + d] = 4 * NB
        counts[t] = lax.div(at + CHUNK - 1, CHUNK)
    for copy in copies:
        copy.wait()
    eye = lax.broadcasted_iota(jnp.int32, (BS, BS), 0) == lax.broadcasted_iota(jnp.int32, (BS, BS), 1)

    def ghost(n, carry):
        for g in range(NG):
            first_slots[n * NG + g] = first_slot(
                eye, ghost_buf[n, (NG + g) * BS : (NG + g + 1) * BS], ghost_buf[n, g * BS : (g + 1) * BS]
            )[0]
        return carry

    lax.fori_loop(0, 4, ghost, 0)


def make_lists(labels, slots, ghosts):
    return pl.pallas_call(
        lists_kernel,
        out_shape=[
            jax.ShapeDtypeStruct((10, 4 * NB + CHUNK), jnp.int32),
            jax.ShapeDtypeStruct((10,), jnp.int32),
            jax.ShapeDtypeStruct((4 * NB + 1, BS, BS), BF),
            jax.ShapeDtypeStruct((4 * NG, BS, BS), BF),
        ],
        in_specs=[spec(SMEM), spec(pltpu.VMEM)] + [spec(ANY)] * 4,
        out_specs=[spec(SMEM)] * 2 + [spec(pltpu.VMEM)] * 2,
        scratch_shapes=[pltpu.VMEM((4, 2 * NG * BS, BS), BF), pltpu.SemaphoreType.DMA((4,))],
        compiler_params=pltpu.CompilerParams(vmem_limit_bytes=12 * 1024 * 1024),
        cost_estimate=pl.CostEstimate(flops=10**8, bytes_accessed=6 * 10**6, transcendentals=0),
        name="lists",
    )(labels, slots, *[ghosts[n] for n in START_ORDER])


def coarse_rows(t, at, lists, counts, blocks, applied, coarse):
    def chunk(q, carry):
        entries = [lists[t, q * CHUNK + u] for u in range(CHUNK)]
        left = jnp.concatenate([blocks[e] for e in entries], axis=1)
        rows = [jnp.minimum(lax.div(e, 4), NB - 1) for e in entries]
        for cols in TILES:
            right = jnp.concatenate([applied[r, :, cols] for r in rows], axis=0)
            res = jnp.dot(left, right, preferred_element_type=F32)
            coarse[at, :, cols] = coarse[at, :, cols] + res
        return carry

    coarse[at] = jnp.zeros((BS, WIDE), F32)
    lax.fori_loop(0, counts[t], chunk, 0)


def far_kernel(
    parity, off_columns, labels, lists, counts, diag, off, slots, blocks, first_slots, g2, g3, g0, g1,
    applied_out, relay_out, relayed_out, direct_out,
    table, labels_in, labels_vmem, label_smem, total_a, total_b, applied, coarse, relay, relayed, direct,
    sem_in, sem_lab, sem_out, sem_piece,
):
    ghosts = (g0, g1, g2, g3)
    copies = [
        pltpu.make_async_copy(slots, table.at[pl.ds(0, NB)], sem_in.at[0]),
        pltpu.make_async_copy(first_slots, table.at[pl.ds(NB, 4 * NG), :, pl.ds(0, BS)], sem_in.at[1]),
    ]
    for n in range(4):
        for g in range(NG):
            copies.append(
                pltpu.make_async_copy(
                    ghosts[n].at[pl.ds(g * BS, BS)],
                    table.at[NB + n * NG + g, :, pl.ds(BS, SENDW)],
                    sem_in.at[2 + n * NG + g],
                )
            )
    lab = [
        pltpu.make_async_copy(ghosts[n].at[pl.ds(NG * BS, EXTRA), pl.ds(0, BS)], labels_in.at[n], sem_lab.at[n])
        for n in range(4)
    ]
    for copy in lab + copies:
        copy.start()
    odd = parity[0] == 1
    relay_level = jnp.where(odd, 3, 1)
    relayed_level = jnp.where(odd, 0, 4)
    rest = pl.ds(pl.multiple_of((1 - parity[0]) * WIDE, BS), 2 * BS)
    relay[:, :, rest] = jnp.zeros((2, BS, 2 * BS), BF)
    relayed[:, :, rest] = jnp.zeros((2, BS, 2 * BS), F32)
    for copy in lab:
        copy.wait()
    for n in range(4):
        labels_vmem[n] = labels_in[n].astype(F32).astype(jnp.int32)[:8] - 2 * OFFSETS[n]
    to_smem = pltpu.make_async_copy(labels_vmem, label_smem, sem_lab.at[0])
    to_smem.start()
    for copy in copies:
        copy.wait()
    to_smem.wait()

    def label_of(j, m):
        ghost = jnp.maximum(j - NB, 0)
        remote = label_smem[lax.div(ghost, NG), 0, lax.rem(ghost, NG) * 4 + m]
        local = labels[jnp.minimum(j, NB - 1), m]
        return jnp.clip(jnp.where(j < NB, local, remote), 0, FRAME - 1)

    def row(i, total):
        total[...] = jnp.zeros_like(total)
        for k in range(4):
            j = i if k == 0 else off_columns[k - 1, i]
            block = diag[i] if k == 0 else off[i, k - 1]
            prod = jnp.dot(block, table[j], preferred_element_type=F32)
            for m in range(4):
                at = label_of(j, m)
                total[at] = total[at] + prod[:, m * BS : (m + 1) * BS]
        for at in range(FRAME):
            applied[i, :, at * BS : (at + 1) * BS] = total[at].astype(BF)
        pltpu.make_async_copy(applied.at[i], applied_out.at[i], sem_out.at[i]).start()

    def row_pair(q, carry):
        row(2 * q, total_a)
        row(2 * q + 1, total_b)
        return carry

    lax.fori_loop(0, NB // 2, row_pair, 0)
    into = pl.ds(pl.multiple_of(parity[0] * (2 * BS), BS), WIDE)

    def rows_of(level):
        def one(b, carry):
            coarse_rows(2 * level + b, b, lists, counts, blocks, applied, coarse)
            return carry

        lax.fori_loop(0, 2, one, 0)

    rows_of(4 - relayed_level)
    direct[...] = coarse[...].astype(BF)
    pieces = [pltpu.make_async_copy(direct, direct_out, sem_piece.at[0])]
    pieces[-1].start()
    rows_of(relay_level)
    relay[:, :, into] = coarse[...].astype(BF)
    pieces.append(pltpu.make_async_copy(relay, relay_out, sem_piece.at[1]))
    pieces[-1].start()
    rows_of(relayed_level)
    relayed[:, :, into] = coarse[...]
    pieces.append(pltpu.make_async_copy(relayed, relayed_out, sem_piece.at[2]))
    pieces[-1].start()

    def wait(i, carry):
        pltpu.make_async_copy(applied.at[i], applied_out.at[i], sem_out.at[i]).wait()
        return carry

    lax.fori_loop(0, NB, wait, 0)
    for copy in pieces:
        copy.wait()


def make_far(parity, off_columns, labels, lists, counts, diag, off, slots, blocks, first_slots, ghosts):
    return pl.pallas_call(
        far_kernel,
        out_shape=[
            jax.ShapeDtypeStruct((NB, BS, WIDE), BF),
            jax.ShapeDtypeStruct((2, BS, CHIPWIDE), BF),
            jax.ShapeDtypeStruct((2, BS, CHIPWIDE), F32),
            jax.ShapeDtypeStruct((2, BS, WIDE), BF),
        ],
        in_specs=[spec(SMEM)] * 5 + [spec(pltpu.VMEM)] * 2 + [spec(ANY), spec(pltpu.VMEM)] + [spec(ANY)] * 5,
        out_specs=[spec(ANY)] * 4,
        scratch_shapes=[
            pltpu.VMEM((NT, BS, SLOTW), BF),
            pltpu.VMEM((4, EXTRA, BS), BF),
            pltpu.VMEM((4, 8, BS), jnp.int32),
            pltpu.SMEM((4, 8, BS), jnp.int32),
            pltpu.VMEM((FRAME, BS, BS), F32),
            pltpu.VMEM((FRAME, BS, BS), F32),
            pltpu.VMEM((NB, BS, WIDE), BF),
            pltpu.VMEM((2, BS, WIDE), F32),
            pltpu.VMEM((2, BS, CHIPWIDE), BF),
            pltpu.VMEM((2, BS, CHIPWIDE), F32),
            pltpu.VMEM((2, BS, WIDE), BF),
            pltpu.SemaphoreType.DMA((2 + 4 * NG,)),
            pltpu.SemaphoreType.DMA((4,)),
            pltpu.SemaphoreType.DMA((NB,)),
            pltpu.SemaphoreType.DMA((3,)),
        ],
        compiler_params=pltpu.CompilerParams(vmem_limit_bytes=34 * 1024 * 1024),
        cost_estimate=pl.CostEstimate(flops=4 * 10**9, bytes_accessed=20 * 10**6, transcendentals=0),
        name="far_rows",
    )(parity, off_columns, labels, lists, counts, diag, off, slots, blocks, first_slots,
      *[ghosts[n] for n in START_ORDER])


def near_kernel(parity, lists, counts, blocks, applied, own, mate, coarse):
    mate_level = jnp.where(parity[0] == 1, 1, 3)

    def one(b, carry):
        t = jnp.where(b < 2, 2 * mate_level + b, b + 2)
        coarse_rows(t, b, lists, counts, blocks, applied, coarse)
        return carry

    lax.fori_loop(0, 4, one, 0)
    own[...] = coarse[2:4]
    mate[...] = coarse[0:2].astype(BF)


def make_near(parity, lists, counts, blocks, applied):
    return pl.pallas_call(
        near_kernel,
        out_shape=[
            jax.ShapeDtypeStruct((2, BS, WIDE), F32),
            jax.ShapeDtypeStruct((2, BS, WIDE), BF),
        ],
        in_specs=[spec(SMEM)] * 3 + [spec(pltpu.VMEM)] * 2,
        out_specs=[spec(pltpu.VMEM)] * 2,
        scratch_shapes=[pltpu.VMEM((4, BS, WIDE), F32)],
        compiler_params=pltpu.CompilerParams(vmem_limit_bytes=26 * 1024 * 1024),
        cost_estimate=pl.CostEstimate(flops=4 * 10**9, bytes_accessed=20 * 10**6, transcendentals=0),
        name="near_rows",
    )(parity, lists, counts, blocks, applied)


def add_near_kernel(parity, own, mate, direct, out):
    edge = 4 * BS
    out[:, :, :edge] = jnp.zeros((2, own.shape[1], edge), F32)
    out[:, :, edge + WIDE :] = jnp.zeros((2, own.shape[1], edge), F32)
    out[:, :, edge : edge + WIDE] = own[...]
    for start, piece in ((3 - 2 * parity[0], mate), (4 - 4 * parity[0], direct)):
        cols = pl.ds(pl.multiple_of(start * (2 * BS), BS), WIDE)
        out[:, :, cols] = out[:, :, cols] + piece[...].astype(F32)


def add_near(parity, own, mate, direct):
    rows = 32

    def block(width):
        return pl.BlockSpec((2, rows, width), lambda r: (0, r, 0))

    return pl.pallas_call(
        add_near_kernel,
        grid=(BS // rows,),
        out_shape=jax.ShapeDtypeStruct((2, BS, BANDWIDE), F32),
        in_specs=[spec(SMEM)] + [block(WIDE)] * 3,
        out_specs=block(BANDWIDE),
        compiler_params=pltpu.CompilerParams(vmem_limit_bytes=16 * 1024 * 1024),
        cost_estimate=pl.CostEstimate(flops=10**6, bytes_accessed=9 * 10**6, transcendentals=0),
        name="add_near",
    )(parity, own, mate, direct)


def add_pair_kernel(parity, band, pair, out, band_buf, pair_buf, sem):
    rows = BS // 4
    cols = pl.ds(pl.multiple_of(parity[0] * (6 * BS), BS), CHIPWIDE)
    parts = [(b, pl.ds(r * rows, rows)) for b in range(2) for r in range(4)]
    loads, stores = [], []
    for at, (b, r) in enumerate(parts):
        loads.append(
            (
                pltpu.make_async_copy(pair.at[b, r], pair_buf.at[b, r], sem.at[0, at]),
                pltpu.make_async_copy(band.at[b, r, cols], band_buf.at[b, r], sem.at[1, at]),
            )
        )
        stores.append(pltpu.make_async_copy(band_buf.at[b, r], out.at[b, r, cols], sem.at[2, at]))
    for pair_of in loads:
        for copy in pair_of:
            copy.start()
    for at, (b, r) in enumerate(parts):
        for copy in loads[at]:
            copy.wait()
        band_buf[b, r] = band_buf[b, r] + pair_buf[b, r].astype(F32)
        stores[at].start()
    for copy in stores:
        copy.wait()


def add_pair(parity, band, pair):
    return pl.pallas_call(
        add_pair_kernel,
        out_shape=jax.ShapeDtypeStruct((2, BS, BANDWIDE), F32),
        in_specs=[spec(SMEM), spec(ANY), spec(ANY)],
        out_specs=spec(ANY),
        input_output_aliases={1: 0},
        scratch_shapes=[
            pltpu.VMEM((2, BS, CHIPWIDE), F32),
            pltpu.VMEM((2, BS, CHIPWIDE), BF),
            pltpu.SemaphoreType.DMA((3, 8)),
        ],
        compiler_params=pltpu.CompilerParams(vmem_limit_bytes=8 * 1024 * 1024),
        name="add_pair",
    )(parity, band, pair)


def permute_by(value, even_step, odd_step):
    count = lax.axis_size(AXES)
    pairs = [(s, s + (odd_step if s % 2 else even_step)) for s in range(count)]
    return lax.ppermute(value, AXES, [(s, t) for s, t in pairs if 0 <= t < count])


def exchange(sends):
    arrived = [None] * 4
    for n in START_ORDER:
        arrived[n] = shift(sends[n], OFFSETS[n])
    return arrived


def local(diag_blocks, off_blocks, off_columns, tentative, aggregate, send_rows):
    off_columns = off_columns.T
    odd = lax.rem(lax.axis_index(AXES), 2)
    parity = odd.reshape(1)
    ghosts = exchange(pack(send_rows, aggregate, tentative, diag_blocks))
    labels, ghost_list, ghost_count, slots, scales = local_slots(
        off_columns, aggregate, diag_blocks, off_blocks, tentative
    )
    labels, slots, sends = ghost_slots(
        send_rows, off_columns, labels, ghost_list, ghost_count, off_blocks, slots, scales, ghosts
    )
    lists, counts, blocks, first_slots = make_lists(labels, slots, ghosts)
    ghosts = exchange(sends)
    applied, relay, relayed, direct = make_far(
        parity, off_columns, labels, lists, counts, diag_blocks, off_blocks, slots, blocks, first_slots, ghosts
    )
    direct_in = permute_by(direct, -2, 2)
    relay_in = permute_by(relay, 1, -1)
    pair_sum = (relayed + relay_in.astype(F32)).astype(BF)
    pair_in = permute_by(pair_sum, 2, -2)
    applied, pair_sum = lax.optimization_barrier((applied, pair_sum))
    own, mate = make_near(parity, lists, counts, blocks, applied)
    mate_in = permute_by(mate, 1, -1)
    band = add_near(parity, own, mate_in, direct_in)
    return add_pair(parity, band, pair_in)


def solution(mesh):
    in_specs = (
        P(AXES, None, None),
        P(AXES, None, None, None),
        P(AXES, None),
        P(AXES, None, None),
        P(AXES),
        P(AXES, None),
    )
    return jax.shard_map(
        local, mesh=mesh, in_specs=in_specs, out_specs=P(AXES, None, None), check_vma=False
    )
```

```python
import jax
import jax.numpy as jnp
from jax import lax
from jax.experimental import pallas as pl
from jax.experimental.pallas import tpu as pltpu
from jax.sharding import PartitionSpec as P

AXES = ("bulk", "coarse")
STEPS = ((-2, 2), (2, -2), (-1, 1), (1, -1))
BS = 128
NB = 16
NG = 4
NT = NB + 4 * NG
FRAME = 18
WIDE = FRAME * BS
SLOTW = 4 * BS
SENDW = 3 * BS
CHIPWIDE = 20 * BS
BANDWIDE = 26 * BS
TILES = [slice(t * 2 * BS, (t + 1) * 2 * BS) for t in range(FRAME // 2)]
GROUP = 4
CHUNK = 4
EXTRA = 16
BF = jnp.bfloat16
F32 = jnp.float32
SMEM = pltpu.SMEM
ANY = pl.ANY
VMEM_LIMIT = 56 * 1024 * 1024


def spec(space):
    return pl.BlockSpec(memory_space=space)


def sent_to(odd):
    return (3 - odd, 2 + odd, 1 - odd, odd)


def came_from(odd):
    return (
        (3 - odd, 4 * odd - 2),
        (2 + odd, 2 - 4 * odd),
        (odd, 1 - 2 * odd),
        (1 - odd, 2 * odd - 1),
    )


def label_rows(values, width):
    lane = lax.broadcasted_iota(jnp.int32, (EXTRA, width), 1)
    total = jnp.zeros((EXTRA, width), jnp.int32)
    for at, value in enumerate(values):
        total = jnp.where(lane == at, value, total)
    return total.astype(F32).astype(BF)


def pack_kernel(parity, send_rows, aggregate, tent, diag, *refs):
    outs, labels, sem = refs[:4], refs[4], refs[5]
    targets = sent_to(parity[0])
    copies = []
    for at, n in enumerate(targets):
        for g in range(NG):
            row = send_rows[n, g]
            copies.append(
                pltpu.make_async_copy(tent.at[row], outs[at].at[pl.ds(g * BS, BS)], sem.at[at, g])
            )
            copies.append(
                pltpu.make_async_copy(
                    diag.at[row], outs[at].at[pl.ds((NG + g) * BS, BS)], sem.at[at, NG + g]
                )
            )
    for copy in copies:
        copy.start()
    for at, n in enumerate(targets):
        labels[at] = label_rows([aggregate[send_rows[n, g]] for g in range(NG)], BS)
        copy = pltpu.make_async_copy(
            labels.at[at], outs[at].at[pl.ds(2 * NG * BS, EXTRA)], sem.at[at, 2 * NG]
        )
        copy.start()
        copies.append(copy)
    for copy in copies:
        copy.wait()


def pack(parity, send_rows, aggregate, tent, diag):
    shape = jax.ShapeDtypeStruct((2 * NG * BS + EXTRA, BS), BF)
    return pl.pallas_call(
        pack_kernel,
        out_shape=[shape] * 4,
        in_specs=[spec(SMEM)] * 3 + [spec(pltpu.VMEM)] * 2,
        out_specs=[spec(ANY)] * 4,
        scratch_shapes=[pltpu.VMEM((4, EXTRA, BS), BF), pltpu.SemaphoreType.DMA((4, 2 * NG + 1))],
        name="pack",
    )(parity, send_rows, aggregate, tent, diag)


def first_slot(eye, block, own):
    diagonal = jnp.sum(jnp.where(eye, block.astype(F32), 0.0), axis=1, keepdims=True)
    scale = 0.6 * (1.0 / jnp.where(diagonal == 0.0, 1.0, diagonal))
    first = own.astype(F32) - scale * jnp.dot(block, own, preferred_element_type=F32)
    return first.astype(BF), scale


def local_slots_kernel(off_columns, aggregate, diag, off, tent, labels, ghost_list, ghost_count, slots, scales):
    eye = lax.broadcasted_iota(jnp.int32, (BS, BS), 0) == lax.broadcasted_iota(jnp.int32, (BS, BS), 1)
    ghost_count[0] = 0

    def row(i, carry):
        slots[i, :, :BS], scale = first_slot(eye, diag[i], tent[i])
        scales[i] = jnp.broadcast_to(scale, (BS, BS))
        labels[i, 0] = aggregate[i] + 8
        for k in range(1, 4):
            c = off_columns[k - 1, i]
            near = tent[jnp.minimum(c, NB - 1)]
            part = -scale * jnp.dot(off[i, k - 1], near, preferred_element_type=F32)
            slots[i, :, k * BS : (k + 1) * BS] = part.astype(BF)
            labels[i, k] = aggregate[jnp.minimum(c, NB - 1)] + 8
            at = ghost_count[0]
            ghost_list[at] = i * 4 + k
            ghost_count[0] = at + jnp.where(c < NB, 0, 1)
        return carry

    lax.fori_loop(0, NB, row, 0, unroll=4)
    at = ghost_count[0]
    for d in range(GROUP):
        ghost_list[at + d] = NB * 4 + 1


def local_slots(off_columns, aggregate, diag, off, tent):
    return pl.pallas_call(
        local_slots_kernel,
        out_shape=[
            jax.ShapeDtypeStruct((NB, 4), jnp.int32),
            jax.ShapeDtypeStruct((3 * NB + GROUP,), jnp.int32),
            jax.ShapeDtypeStruct((1,), jnp.int32),
            jax.ShapeDtypeStruct((NB, BS, SLOTW), BF),
            jax.ShapeDtypeStruct((NB, BS, BS), F32),
        ],
        in_specs=[spec(SMEM)] * 2 + [spec(pltpu.VMEM)] * 3,
        out_specs=[spec(SMEM)] * 3 + [spec(pltpu.VMEM)] * 2,
        compiler_params=pltpu.CompilerParams(vmem_limit_bytes=10 * 1024 * 1024),
        cost_estimate=pl.CostEstimate(flops=10**9, bytes_accessed=6 * 10**6, transcendentals=0),
        name="local_slots",
    )(off_columns, aggregate, diag, off, tent)


def ghost_slots_kernel(
    parity, send_rows, off_columns, local_labels, ghost_list, ghost_count, off, slots_in, scales,
    g0, g1, g2, g3,
    labels, slots, s0, s1, s2, s3,
    table, labels_in, label_smem, sem,
):
    ghosts, sends = (g0, g1, g2, g3), (s0, s1, s2, s3)
    copy = pltpu.make_async_copy(slots_in, slots.at[pl.ds(0, NB)], sem.at[0])
    copy.start()
    arrivals = came_from(parity[0])
    for at, (n, offset) in enumerate(arrivals):
        row = ghosts[at][2 * NG * BS :, :].astype(F32).astype(jnp.int32)[:8]
        labels_in[n] = row + (8 - 2 * offset)
    to_smem = pltpu.make_async_copy(labels_in, label_smem, sem.at[1])
    to_smem.start()
    for at, (n, _) in enumerate(arrivals):
        for g in range(NG):
            table[n * NG + g] = ghosts[at][g * BS : (g + 1) * BS, :]
    for i in range(NB):
        for k in range(4):
            labels[i, k] = local_labels[i, k]
    to_smem.wait()
    copy.wait()

    def group(q, carry):
        for u in range(GROUP):
            entry = ghost_list[q * GROUP + u]
            i, k = lax.div(entry, 4), lax.rem(entry, 4)
            row = jnp.minimum(i, NB - 1)
            ghost = jnp.clip(off_columns[k - 1, row] - NB, 0, 4 * NG - 1)
            part = jnp.dot(off[row, k - 1], table[ghost], preferred_element_type=F32)
            part = -scales[row] * part
            slots[i, :, pl.ds(pl.multiple_of(k * BS, BS), BS)] = part.astype(BF)
            labels[i, k] = label_smem[lax.div(ghost, NG), 0, lax.rem(ghost, NG)]
        return carry

    lax.fori_loop(0, lax.div(ghost_count[0] + GROUP - 1, GROUP), group, 0)

    for at, n in enumerate(sent_to(parity[0])):
        for g in range(NG):
            sends[at][g * BS : (g + 1) * BS, :] = slots[send_rows[n, g], :, BS:]
        values = [labels[send_rows[n, g], k] for g in range(NG) for k in range(4)]
        sends[at][NG * BS :, :] = label_rows(values, SENDW)


def ghost_slots(parity, send_rows, off_columns, local_labels, ghost_list, ghost_count, off, slots_in, scales, ghosts):
    send = jax.ShapeDtypeStruct((NG * BS + EXTRA, SENDW), BF)
    return pl.pallas_call(
        ghost_slots_kernel,
        out_shape=[
            jax.ShapeDtypeStruct((NB + 1, 4), jnp.int32),
            jax.ShapeDtypeStruct((NB + 1, BS, SLOTW), BF),
        ]
        + [send] * 4,
        in_specs=[spec(SMEM)] * 6 + [spec(pltpu.VMEM)] * 7,
        out_specs=[spec(SMEM)] + [spec(pltpu.VMEM)] * 5,
        scratch_shapes=[
            pltpu.VMEM((4 * NG, BS, BS), BF),
            pltpu.VMEM((4, 8, BS), jnp.int32),
            pltpu.SMEM((4, 8, BS), jnp.int32),
            pltpu.SemaphoreType.DMA((2,)),
        ],
        compiler_params=pltpu.CompilerParams(vmem_limit_bytes=16 * 1024 * 1024),
        name="ghost_slots",
    )(parity, send_rows, off_columns, local_labels, ghost_list, ghost_count, off, slots_in, scales, *ghosts)


def lists_kernel(parity, labels, slots, g0, g1, g2, g3, lists, counts, blocks, first_slots, ghost_buf, sem):
    ghosts = (g0, g1, g2, g3)
    copies = [
        pltpu.make_async_copy(ghosts[n].at[pl.ds(0, 2 * NG * BS)], ghost_buf.at[n], sem.at[n])
        for n in range(4)
    ]
    for copy in copies:
        copy.start()
    for t in range(10):
        counts[t] = 0

    def row(i, carry):
        for k in range(4):
            blocks[i * 4 + k] = slots[i, :, k * BS : (k + 1) * BS].T
            t = jnp.clip(labels[i, k] - 4, 0, 9)
            at = counts[t]
            lists[t, at] = i * 4 + k
            counts[t] = at + 1
        return carry

    lax.fori_loop(0, NB, row, 0, unroll=2)
    blocks[4 * NB] = jnp.zeros((BS, BS), BF)
    for t in range(10):
        at = counts[t]
        for d in range(CHUNK - 1):
            lists[t, at + d] = 4 * NB
        counts[t] = lax.div(at + CHUNK - 1, CHUNK)
    for copy in copies:
        copy.wait()
    eye = lax.broadcasted_iota(jnp.int32, (BS, BS), 0) == lax.broadcasted_iota(jnp.int32, (BS, BS), 1)

    for at, (n, _) in enumerate(came_from(parity[0])):
        for g in range(NG):
            first_slots[n * NG + g] = first_slot(
                eye, ghost_buf[at, (NG + g) * BS : (NG + g + 1) * BS], ghost_buf[at, g * BS : (g + 1) * BS]
            )[0]


def make_lists(parity, labels, slots, ghosts):
    return pl.pallas_call(
        lists_kernel,
        out_shape=[
            jax.ShapeDtypeStruct((10, 4 * NB + CHUNK), jnp.int32),
            jax.ShapeDtypeStruct((10,), jnp.int32),
            jax.ShapeDtypeStruct((4 * NB + 1, BS, BS), BF),
            jax.ShapeDtypeStruct((4 * NG, BS, BS), BF),
        ],
        in_specs=[spec(SMEM)] * 2 + [spec(pltpu.VMEM)] + [spec(ANY)] * 4,
        out_specs=[spec(SMEM)] * 2 + [spec(pltpu.VMEM)] * 2,
        scratch_shapes=[pltpu.VMEM((4, 2 * NG * BS, BS), BF), pltpu.SemaphoreType.DMA((4,))],
        compiler_params=pltpu.CompilerParams(vmem_limit_bytes=12 * 1024 * 1024),
        cost_estimate=pl.CostEstimate(flops=10**8, bytes_accessed=6 * 10**6, transcendentals=0),
        name="lists",
    )(parity, labels, slots, *ghosts)


def coarse_rows(t, at, lists, counts, blocks, applied, coarse):
    def chunk(q, carry):
        entries = [lists[t, q * CHUNK + u] for u in range(CHUNK)]
        left = jnp.concatenate([blocks[e] for e in entries], axis=1)
        rows = [jnp.minimum(lax.div(e, 4), NB - 1) for e in entries]
        for cols in TILES:
            right = jnp.concatenate([applied[r, :, cols] for r in rows], axis=0)
            res = jnp.dot(left, right, preferred_element_type=F32)
            coarse[at, :, cols] = coarse[at, :, cols] + res
        return carry

    coarse[at] = jnp.zeros((BS, WIDE), F32)
    lax.fori_loop(0, counts[t], chunk, 0)


def far_kernel(
    parity, off_columns, labels, lists, counts, diag, off, slots, blocks, first_slots, g0, g1, g2, g3,
    applied_out, relay_out, relayed_out, direct_out,
    table, labels_in, labels_vmem, label_smem, total_a, total_b, applied, coarse, relay, relayed, direct,
    sem_in, sem_lab, sem_out, sem_piece,
):
    ghosts = (g0, g1, g2, g3)
    copies = [
        pltpu.make_async_copy(slots.at[pl.ds(0, NB)], table.at[pl.ds(0, NB)], sem_in.at[0]),
        pltpu.make_async_copy(first_slots, table.at[pl.ds(NB, 4 * NG), :, pl.ds(0, BS)], sem_in.at[1]),
    ]
    arrivals = came_from(parity[0])
    for at, (n, _) in enumerate(arrivals):
        for g in range(NG):
            copies.append(
                pltpu.make_async_copy(
                    ghosts[at].at[pl.ds(g * BS, BS)],
                    table.at[NB + n * NG + g, :, pl.ds(BS, SENDW)],
                    sem_in.at[2 + at * NG + g],
                )
            )
    lab = [
        pltpu.make_async_copy(ghosts[n].at[pl.ds(NG * BS, EXTRA), pl.ds(0, BS)], labels_in.at[n], sem_lab.at[n])
        for n in range(4)
    ]
    for copy in lab + copies:
        copy.start()
    odd = parity[0] == 1
    relay_level = jnp.where(odd, 3, 1)
    relayed_level = jnp.where(odd, 0, 4)
    rest = pl.ds(pl.multiple_of((1 - parity[0]) * WIDE, BS), 2 * BS)
    relay[:, :, rest] = jnp.zeros((2, BS, 2 * BS), BF)
    relayed[:, :, rest] = jnp.zeros((2, BS, 2 * BS), F32)
    for copy in lab:
        copy.wait()
    for at, (n, offset) in enumerate(arrivals):
        labels_vmem[n] = labels_in[at].astype(F32).astype(jnp.int32)[:8] - 2 * offset
    to_smem = pltpu.make_async_copy(labels_vmem, label_smem, sem_lab.at[0])
    to_smem.start()
    for copy in copies:
        copy.wait()
    to_smem.wait()

    def label_of(j, m):
        ghost = jnp.maximum(j - NB, 0)
        remote = label_smem[lax.div(ghost, NG), 0, lax.rem(ghost, NG) * 4 + m]
        local = labels[jnp.minimum(j, NB - 1), m]
        return jnp.clip(jnp.where(j < NB, local, remote), 0, FRAME - 1)

    def row(i, total):
        total[...] = jnp.zeros_like(total)
        for k in range(4):
            j = i if k == 0 else off_columns[k - 1, i]
            block = diag[i] if k == 0 else off[i, k - 1]
            prod = jnp.dot(block, table[j], preferred_element_type=F32)
            for m in range(4):
                at = label_of(j, m)
                total[at] = total[at] + prod[:, m * BS : (m + 1) * BS]
        for at in range(FRAME):
            applied[i, :, at * BS : (at + 1) * BS] = total[at].astype(BF)
        pltpu.make_async_copy(applied.at[i], applied_out.at[i], sem_out.at[i]).start()

    def row_pair(q, carry):
        row(2 * q, total_a)
        row(2 * q + 1, total_b)
        return carry

    lax.fori_loop(0, NB // 2, row_pair, 0)
    into = pl.ds(pl.multiple_of(parity[0] * (2 * BS), BS), WIDE)

    def rows_of(level):
        def one(b, carry):
            coarse_rows(2 * level + b, b, lists, counts, blocks, applied, coarse)
            return carry

        lax.fori_loop(0, 2, one, 0)

    rows_of(4 - relayed_level)
    direct[...] = coarse[...].astype(BF)
    pieces = [pltpu.make_async_copy(direct, direct_out, sem_piece.at[0])]
    pieces[-1].start()
    rows_of(relay_level)
    relay[:, :, into] = coarse[...].astype(BF)
    pieces.append(pltpu.make_async_copy(relay, relay_out, sem_piece.at[1]))
    pieces[-1].start()
    rows_of(relayed_level)
    relayed[:, :, into] = coarse[...]
    pieces.append(pltpu.make_async_copy(relayed, relayed_out, sem_piece.at[2]))
    pieces[-1].start()

    def wait(i, carry):
        pltpu.make_async_copy(applied.at[i], applied_out.at[i], sem_out.at[i]).wait()
        return carry

    lax.fori_loop(0, NB, wait, 0)
    for copy in pieces:
        copy.wait()


def make_far(parity, off_columns, labels, lists, counts, diag, off, slots, blocks, first_slots, ghosts):
    return pl.pallas_call(
        far_kernel,
        out_shape=[
            jax.ShapeDtypeStruct((NB, BS, WIDE), BF),
            jax.ShapeDtypeStruct((2, BS, CHIPWIDE), BF),
            jax.ShapeDtypeStruct((2, BS, CHIPWIDE), F32),
            jax.ShapeDtypeStruct((2, BS, WIDE), BF),
        ],
        in_specs=[spec(SMEM)] * 5 + [spec(pltpu.VMEM)] * 2 + [spec(ANY), spec(pltpu.VMEM)] + [spec(ANY)] * 5,
        out_specs=[spec(ANY)] * 4,
        scratch_shapes=[
            pltpu.VMEM((NT, BS, SLOTW), BF),
            pltpu.VMEM((4, EXTRA, BS), BF),
            pltpu.VMEM((4, 8, BS), jnp.int32),
            pltpu.SMEM((4, 8, BS), jnp.int32),
            pltpu.VMEM((FRAME, BS, BS), F32),
            pltpu.VMEM((FRAME, BS, BS), F32),
            pltpu.VMEM((NB, BS, WIDE), BF),
            pltpu.VMEM((2, BS, WIDE), F32),
            pltpu.VMEM((2, BS, CHIPWIDE), BF),
            pltpu.VMEM((2, BS, CHIPWIDE), F32),
            pltpu.VMEM((2, BS, WIDE), BF),
            pltpu.SemaphoreType.DMA((2 + 4 * NG,)),
            pltpu.SemaphoreType.DMA((4,)),
            pltpu.SemaphoreType.DMA((NB,)),
            pltpu.SemaphoreType.DMA((3,)),
        ],
        compiler_params=pltpu.CompilerParams(vmem_limit_bytes=34 * 1024 * 1024),
        cost_estimate=pl.CostEstimate(flops=4 * 10**9, bytes_accessed=20 * 10**6, transcendentals=0),
        name="far_rows",
    )(parity, off_columns, labels, lists, counts, diag, off, slots, blocks, first_slots, *ghosts)


def near_kernel(parity, lists, counts, blocks, applied, own, mate, coarse):
    mate_level = jnp.where(parity[0] == 1, 1, 3)

    def one(b, carry):
        t = jnp.where(b < 2, 2 * mate_level + b, b + 2)
        coarse_rows(t, b, lists, counts, blocks, applied, coarse)
        return carry

    lax.fori_loop(0, 4, one, 0)
    own[...] = coarse[2:4]
    mate[...] = coarse[0:2].astype(BF)


def make_near(parity, lists, counts, blocks, applied):
    return pl.pallas_call(
        near_kernel,
        out_shape=[
            jax.ShapeDtypeStruct((2, BS, WIDE), F32),
            jax.ShapeDtypeStruct((2, BS, WIDE), BF),
        ],
        in_specs=[spec(SMEM)] * 3 + [spec(pltpu.VMEM)] * 2,
        out_specs=[spec(pltpu.VMEM)] * 2,
        scratch_shapes=[pltpu.VMEM((4, BS, WIDE), F32)],
        compiler_params=pltpu.CompilerParams(vmem_limit_bytes=26 * 1024 * 1024),
        cost_estimate=pl.CostEstimate(flops=4 * 10**9, bytes_accessed=20 * 10**6, transcendentals=0),
        name="near_rows",
    )(parity, lists, counts, blocks, applied)


def add_near_kernel(parity, own, mate, direct, out):
    edge = 4 * BS
    out[:, :, :edge] = jnp.zeros((2, own.shape[1], edge), F32)
    out[:, :, edge + WIDE :] = jnp.zeros((2, own.shape[1], edge), F32)
    out[:, :, edge : edge + WIDE] = own[...]
    for start, piece in ((3 - 2 * parity[0], mate), (4 - 4 * parity[0], direct)):
        cols = pl.ds(pl.multiple_of(start * (2 * BS), BS), WIDE)
        out[:, :, cols] = out[:, :, cols] + piece[...].astype(F32)


def add_near(parity, own, mate, direct):
    rows = 32

    def block(width):
        return pl.BlockSpec((2, rows, width), lambda r: (0, r, 0))

    return pl.pallas_call(
        add_near_kernel,
        grid=(BS // rows,),
        out_shape=jax.ShapeDtypeStruct((2, BS, BANDWIDE), F32),
        in_specs=[spec(SMEM)] + [block(WIDE)] * 3,
        out_specs=block(BANDWIDE),
        compiler_params=pltpu.CompilerParams(vmem_limit_bytes=16 * 1024 * 1024),
        cost_estimate=pl.CostEstimate(flops=10**6, bytes_accessed=9 * 10**6, transcendentals=0),
        name="add_near",
    )(parity, own, mate, direct)


def add_pair_kernel(parity, band, pair, out, buf, sem):
    rows = BS // 4
    cols = pl.ds(pl.multiple_of(parity[0] * (6 * BS), BS), CHIPWIDE)
    stores = []
    for b in range(2):
        for r in range(4):
            part = pl.ds(r * rows, rows)
            buf[b, part] = band[b, part]
            buf[b, part, cols] = band[b, part, cols] + pair[b, part].astype(F32)
            stores.append(pltpu.make_async_copy(buf.at[b, part], out.at[b, part], sem.at[b, r]))
            stores[-1].start()
    for copy in stores:
        copy.wait()


def add_pair(parity, band, pair):
    return pl.pallas_call(
        add_pair_kernel,
        out_shape=jax.ShapeDtypeStruct((2, BS, BANDWIDE), F32),
        in_specs=[spec(SMEM)] + [spec(pltpu.VMEM)] * 2,
        out_specs=spec(ANY),
        scratch_shapes=[pltpu.VMEM((2, BS, BANDWIDE), F32), pltpu.SemaphoreType.DMA((2, 4))],
        compiler_params=pltpu.CompilerParams(vmem_limit_bytes=12 * 1024 * 1024),
        name="add_pair",
    )(parity, band, pair)


def permute_by(value, even_step, odd_step):
    count = lax.axis_size(AXES)
    pairs = [(s, s + (odd_step if s % 2 else even_step)) for s in range(count)]
    return lax.ppermute(value, AXES, [(s, t) for s, t in pairs if 0 <= t < count])


def exchange(sends):
    return [permute_by(value, *steps) for value, steps in zip(sends, STEPS)]


def local(diag_blocks, off_blocks, off_columns, tentative, aggregate, send_rows):
    off_columns = off_columns.T
    odd = lax.rem(lax.axis_index(AXES), 2)
    parity = odd.reshape(1)
    ghosts = exchange(pack(parity, send_rows, aggregate, tentative, diag_blocks))
    labels, ghost_list, ghost_count, slots, scales = local_slots(
        off_columns, aggregate, diag_blocks, off_blocks, tentative
    )
    labels, slots, *sends = ghost_slots(
        parity, send_rows, off_columns, labels, ghost_list, ghost_count, off_blocks, slots, scales, ghosts
    )
    lists, counts, blocks, first_slots = make_lists(parity, labels, slots, ghosts)
    ghosts = exchange(sends)
    applied, relay, relayed, direct = make_far(
        parity, off_columns, labels, lists, counts, diag_blocks, off_blocks, slots, blocks, first_slots, ghosts
    )
    direct_in = permute_by(direct, -2, 2)
    relay_in = permute_by(relay, 1, -1)
    pair_sum = (relayed + relay_in.astype(F32)).astype(BF)
    pair_in = permute_by(pair_sum, 2, -2)
    applied, pair_sum = lax.optimization_barrier((applied, pair_sum))
    own, mate = make_near(parity, lists, counts, blocks, applied)
    mate_in = permute_by(mate, 1, -1)
    band = add_near(parity, own, mate_in, direct_in)
    return add_pair(parity, band, pair_in)


def solution(mesh):
    in_specs = (
        P(AXES, None, None),
        P(AXES, None, None, None),
        P(AXES, None),
        P(AXES, None, None),
        P(AXES),
        P(AXES, None),
    )
    return jax.shard_map(
        local, mesh=mesh, in_specs=in_specs, out_specs=P(AXES, None, None), check_vma=False
    )
```

```python
import jax
import jax.numpy as jnp
from jax import lax
from jax.experimental import pallas as pl
from jax.experimental.pallas import tpu as pltpu
from jax.sharding import PartitionSpec as P

AXES = ("bulk", "coarse")
STEPS = ((-2, 2), (2, -2), (-1, 1), (1, -1))
BS = 128
NB = 16
NG = 4
NT = NB + 4 * NG
FRAME = 18
WIDE = FRAME * BS
SLOTW = 4 * BS
SENDW = 3 * BS
CHIPWIDE = 20 * BS
BANDWIDE = 26 * BS
TILES = [slice(t * 2 * BS, (t + 1) * 2 * BS) for t in range(FRAME // 2)]
FAR_MB = 26
GROUP = 4
CHUNK = 4
EXTRA = 16
BF = jnp.bfloat16
F32 = jnp.float32
SMEM = pltpu.SMEM
ANY = pl.ANY
VMEM_LIMIT = 56 * 1024 * 1024


def spec(space):
    return pl.BlockSpec(memory_space=space)


def sent_to(odd):
    return (3 - odd, 2 + odd, 1 - odd, odd)


def came_from(odd):
    return (
        (3 - odd, 4 * odd - 2),
        (2 + odd, 2 - 4 * odd),
        (odd, 1 - 2 * odd),
        (1 - odd, 2 * odd - 1),
    )


def label_rows(values, width):
    lane = lax.broadcasted_iota(jnp.int32, (EXTRA, width), 1)
    total = jnp.zeros((EXTRA, width), jnp.int32)
    for at, value in enumerate(values):
        total = jnp.where(lane == at, value, total)
    return total.astype(F32).astype(BF)


def pack_kernel(parity, send_rows, aggregate, tent, diag, *refs):
    outs, labels, sem = refs[:4], refs[4], refs[5]
    targets = sent_to(parity[0])
    copies = []
    for at, n in enumerate(targets):
        for g in range(NG):
            row = send_rows[n, g]
            copies.append(
                pltpu.make_async_copy(tent.at[row], outs[at].at[pl.ds(g * BS, BS)], sem.at[at, g])
            )
            copies.append(
                pltpu.make_async_copy(
                    diag.at[row], outs[at].at[pl.ds((NG + g) * BS, BS)], sem.at[at, NG + g]
                )
            )
    for copy in copies:
        copy.start()
    for at, n in enumerate(targets):
        labels[at] = label_rows([aggregate[send_rows[n, g]] for g in range(NG)], BS)
        copy = pltpu.make_async_copy(
            labels.at[at], outs[at].at[pl.ds(2 * NG * BS, EXTRA)], sem.at[at, 2 * NG]
        )
        copy.start()
        copies.append(copy)
    for copy in copies:
        copy.wait()


def pack(parity, send_rows, aggregate, tent, diag):
    shape = jax.ShapeDtypeStruct((2 * NG * BS + EXTRA, BS), BF)
    return pl.pallas_call(
        pack_kernel,
        out_shape=[shape] * 4,
        in_specs=[spec(SMEM)] * 3 + [spec(pltpu.VMEM)] * 2,
        out_specs=[spec(ANY)] * 4,
        scratch_shapes=[pltpu.VMEM((4, EXTRA, BS), BF), pltpu.SemaphoreType.DMA((4, 2 * NG + 1))],
        name="pack",
    )(parity, send_rows, aggregate, tent, diag)


def first_slot(eye, block, own):
    diagonal = jnp.sum(jnp.where(eye, block.astype(F32), 0.0), axis=1, keepdims=True)
    scale = 0.6 * (1.0 / jnp.where(diagonal == 0.0, 1.0, diagonal))
    first = own.astype(F32) - scale * jnp.dot(block, own, preferred_element_type=F32)
    return first.astype(BF), scale


def local_slots_kernel(off_columns, aggregate, diag, off, tent, labels, ghost_list, ghost_count, slots, scales):
    eye = lax.broadcasted_iota(jnp.int32, (BS, BS), 0) == lax.broadcasted_iota(jnp.int32, (BS, BS), 1)
    ghost_count[0] = 0

    def row(i, carry):
        slots[i, :, :BS], scale = first_slot(eye, diag[i], tent[i])
        scales[i] = jnp.broadcast_to(scale, (BS, BS))
        labels[i, 0] = aggregate[i] + 8
        for k in range(1, 4):
            c = off_columns[k - 1, i]
            near = tent[jnp.minimum(c, NB - 1)]
            part = -scale * jnp.dot(off[i, k - 1], near, preferred_element_type=F32)
            slots[i, :, k * BS : (k + 1) * BS] = part.astype(BF)
            labels[i, k] = aggregate[jnp.minimum(c, NB - 1)] + 8
            at = ghost_count[0]
            ghost_list[at] = i * 4 + k
            ghost_count[0] = at + jnp.where(c < NB, 0, 1)
        return carry

    lax.fori_loop(0, NB, row, 0, unroll=4)
    at = ghost_count[0]
    for d in range(GROUP):
        ghost_list[at + d] = NB * 4 + 1


def local_slots(off_columns, aggregate, diag, off, tent):
    return pl.pallas_call(
        local_slots_kernel,
        out_shape=[
            jax.ShapeDtypeStruct((NB, 4), jnp.int32),
            jax.ShapeDtypeStruct((3 * NB + GROUP,), jnp.int32),
            jax.ShapeDtypeStruct((1,), jnp.int32),
            jax.ShapeDtypeStruct((NB, BS, SLOTW), BF),
            jax.ShapeDtypeStruct((NB, BS, BS), F32),
        ],
        in_specs=[spec(SMEM)] * 2 + [spec(pltpu.VMEM)] * 3,
        out_specs=[spec(SMEM)] * 3 + [spec(pltpu.VMEM)] * 2,
        compiler_params=pltpu.CompilerParams(vmem_limit_bytes=10 * 1024 * 1024),
        cost_estimate=pl.CostEstimate(flops=10**9, bytes_accessed=6 * 10**6, transcendentals=0),
        name="local_slots",
    )(off_columns, aggregate, diag, off, tent)


def ghost_slots_kernel(
    parity, send_rows, off_columns, local_labels, ghost_list, ghost_count, off, slots_in, scales,
    g0, g1, g2, g3,
    labels, slots, s0, s1, s2, s3,
    table, labels_in, label_smem, sem,
):
    ghosts, sends = (g0, g1, g2, g3), (s0, s1, s2, s3)
    copy = pltpu.make_async_copy(slots_in, slots.at[pl.ds(0, NB)], sem.at[0])
    copy.start()
    arrivals = came_from(parity[0])
    for at, (n, offset) in enumerate(arrivals):
        row = ghosts[at][2 * NG * BS :, :].astype(F32).astype(jnp.int32)[:8]
        labels_in[n] = row + (8 - 2 * offset)
    to_smem = pltpu.make_async_copy(labels_in, label_smem, sem.at[1])
    to_smem.start()
    for at, (n, _) in enumerate(arrivals):
        for g in range(NG):
            table[n * NG + g] = ghosts[at][g * BS : (g + 1) * BS, :]
    for i in range(NB):
        for k in range(4):
            labels[i, k] = local_labels[i, k]
    to_smem.wait()
    copy.wait()

    def group(q, carry):
        for u in range(GROUP):
            entry = ghost_list[q * GROUP + u]
            i, k = lax.div(entry, 4), lax.rem(entry, 4)
            row = jnp.minimum(i, NB - 1)
            ghost = jnp.clip(off_columns[k - 1, row] - NB, 0, 4 * NG - 1)
            part = jnp.dot(off[row, k - 1], table[ghost], preferred_element_type=F32)
            part = -scales[row] * part
            slots[i, :, pl.ds(pl.multiple_of(k * BS, BS), BS)] = part.astype(BF)
            labels[i, k] = label_smem[lax.div(ghost, NG), 0, lax.rem(ghost, NG)]
        return carry

    lax.fori_loop(0, lax.div(ghost_count[0] + GROUP - 1, GROUP), group, 0)

    for at, n in enumerate(sent_to(parity[0])):
        for g in range(NG):
            sends[at][g * BS : (g + 1) * BS, :] = slots[send_rows[n, g], :, BS:]
        values = [labels[send_rows[n, g], k] for g in range(NG) for k in range(4)]
        sends[at][NG * BS :, :] = label_rows(values, SENDW)


def ghost_slots(parity, send_rows, off_columns, local_labels, ghost_list, ghost_count, off, slots_in, scales, ghosts):
    send = jax.ShapeDtypeStruct((NG * BS + EXTRA, SENDW), BF)
    return pl.pallas_call(
        ghost_slots_kernel,
        out_shape=[
            jax.ShapeDtypeStruct((NB + 1, 4), jnp.int32),
            jax.ShapeDtypeStruct((NB + 1, BS, SLOTW), BF),
        ]
        + [send] * 4,
        in_specs=[spec(SMEM)] * 6 + [spec(pltpu.VMEM)] * 7,
        out_specs=[spec(SMEM)] + [spec(pltpu.VMEM)] * 5,
        scratch_shapes=[
            pltpu.VMEM((4 * NG, BS, BS), BF),
            pltpu.VMEM((4, 8, BS), jnp.int32),
            pltpu.SMEM((4, 8, BS), jnp.int32),
            pltpu.SemaphoreType.DMA((2,)),
        ],
        compiler_params=pltpu.CompilerParams(vmem_limit_bytes=16 * 1024 * 1024),
        name="ghost_slots",
    )(parity, send_rows, off_columns, local_labels, ghost_list, ghost_count, off, slots_in, scales, *ghosts)


def lists_kernel(parity, labels, slots, g0, g1, g2, g3, lists, counts, blocks, first_slots, ghost_buf, sem):
    ghosts = (g0, g1, g2, g3)
    copies = [
        pltpu.make_async_copy(ghosts[n].at[pl.ds(0, 2 * NG * BS)], ghost_buf.at[n], sem.at[n])
        for n in range(4)
    ]
    for copy in copies:
        copy.start()
    for t in range(10):
        counts[t] = 0

    def row(i, carry):
        for k in range(4):
            blocks[i * 4 + k] = slots[i, :, k * BS : (k + 1) * BS].T
            t = jnp.clip(labels[i, k] - 4, 0, 9)
            at = counts[t]
            lists[t, at] = i * 4 + k
            counts[t] = at + 1
        return carry

    lax.fori_loop(0, NB, row, 0, unroll=2)
    blocks[4 * NB] = jnp.zeros((BS, BS), BF)
    for t in range(10):
        at = counts[t]
        for d in range(CHUNK - 1):
            lists[t, at + d] = 4 * NB
        counts[t] = lax.div(at + CHUNK - 1, CHUNK)
    for copy in copies:
        copy.wait()
    eye = lax.broadcasted_iota(jnp.int32, (BS, BS), 0) == lax.broadcasted_iota(jnp.int32, (BS, BS), 1)

    for at, (n, _) in enumerate(came_from(parity[0])):
        for g in range(NG):
            first_slots[n * NG + g] = first_slot(
                eye, ghost_buf[at, (NG + g) * BS : (NG + g + 1) * BS], ghost_buf[at, g * BS : (g + 1) * BS]
            )[0]


def make_lists(parity, labels, slots, ghosts):
    return pl.pallas_call(
        lists_kernel,
        out_shape=[
            jax.ShapeDtypeStruct((10, 4 * NB + CHUNK), jnp.int32),
            jax.ShapeDtypeStruct((10,), jnp.int32),
            jax.ShapeDtypeStruct((4 * NB + 1, BS, BS), BF),
            jax.ShapeDtypeStruct((4 * NG, BS, BS), BF),
        ],
        in_specs=[spec(SMEM)] * 2 + [spec(pltpu.VMEM)] + [spec(ANY)] * 4,
        out_specs=[spec(SMEM)] * 2 + [spec(pltpu.VMEM)] * 2,
        scratch_shapes=[pltpu.VMEM((4, 2 * NG * BS, BS), BF), pltpu.SemaphoreType.DMA((4,))],
        compiler_params=pltpu.CompilerParams(vmem_limit_bytes=12 * 1024 * 1024),
        cost_estimate=pl.CostEstimate(flops=10**8, bytes_accessed=6 * 10**6, transcendentals=0),
        name="lists",
    )(parity, labels, slots, *ghosts)


def coarse_rows(t, at, lists, counts, blocks, applied, coarse):
    def chunk(q, carry):
        entries = [lists[t, q * CHUNK + u] for u in range(CHUNK)]
        left = jnp.concatenate([blocks[e] for e in entries], axis=1)
        rows = [jnp.minimum(lax.div(e, 4), NB - 1) for e in entries]
        for cols in TILES:
            right = jnp.concatenate([applied[r, :, cols] for r in rows], axis=0)
            res = jnp.dot(left, right, preferred_element_type=F32)
            coarse[at, :, cols] = coarse[at, :, cols] + res
        return carry

    coarse[at] = jnp.zeros((BS, WIDE), F32)
    lax.fori_loop(0, counts[t], chunk, 0)


def rows_of(level, lists, counts, blocks, applied, coarse):
    def one(b, carry):
        coarse_rows(2 * level + b, b, lists, counts, blocks, applied, coarse)
        return carry

    lax.fori_loop(0, 2, one, 0)


def chip_frame(odd):
    into = pl.ds(pl.multiple_of(odd * (2 * BS), BS), WIDE)
    return into, pl.ds(pl.multiple_of((1 - odd) * WIDE, BS), 2 * BS)


def far_kernel(
    parity, off_columns, labels, lists, counts, diag, off, slots, blocks, first_slots, g0, g1, g2, g3,
    applied, direct, relay,
    table, labels_in, labels_vmem, label_smem, total_a, total_b, coarse, sem_in, sem_lab,
):
    ghosts = (g0, g1, g2, g3)
    copies = [
        pltpu.make_async_copy(slots.at[pl.ds(0, NB)], table.at[pl.ds(0, NB)], sem_in.at[0]),
        pltpu.make_async_copy(first_slots, table.at[pl.ds(NB, 4 * NG), :, pl.ds(0, BS)], sem_in.at[1]),
    ]
    arrivals = came_from(parity[0])
    for at, (n, _) in enumerate(arrivals):
        for g in range(NG):
            copies.append(
                pltpu.make_async_copy(
                    ghosts[at].at[pl.ds(g * BS, BS)],
                    table.at[NB + n * NG + g, :, pl.ds(BS, SENDW)],
                    sem_in.at[2 + at * NG + g],
                )
            )
    lab = [
        pltpu.make_async_copy(ghosts[n].at[pl.ds(NG * BS, EXTRA), pl.ds(0, BS)], labels_in.at[n], sem_lab.at[n])
        for n in range(4)
    ]
    for copy in lab + copies:
        copy.start()
    for copy in lab:
        copy.wait()
    for at, (n, offset) in enumerate(arrivals):
        labels_vmem[n] = labels_in[at].astype(F32).astype(jnp.int32)[:8] - 2 * offset
    to_smem = pltpu.make_async_copy(labels_vmem, label_smem, sem_lab.at[0])
    to_smem.start()
    for copy in copies:
        copy.wait()
    to_smem.wait()

    def label_of(j, m):
        ghost = jnp.maximum(j - NB, 0)
        remote = label_smem[lax.div(ghost, NG), 0, lax.rem(ghost, NG) * 4 + m]
        local = labels[jnp.minimum(j, NB - 1), m]
        return jnp.clip(jnp.where(j < NB, local, remote), 0, FRAME - 1)

    def row(i, total):
        total[...] = jnp.zeros_like(total)
        for k in range(4):
            j = i if k == 0 else off_columns[k - 1, i]
            block = diag[i] if k == 0 else off[i, k - 1]
            prod = jnp.dot(block, table[j], preferred_element_type=F32)
            for m in range(4):
                at = label_of(j, m)
                total[at] = total[at] + prod[:, m * BS : (m + 1) * BS]
        for at in range(FRAME):
            applied[i, :, at * BS : (at + 1) * BS] = total[at].astype(BF)

    def row_pair(q, carry):
        row(2 * q, total_a)
        row(2 * q + 1, total_b)
        return carry

    lax.fori_loop(0, NB // 2, row_pair, 0)
    rows_of(4 * parity[0], lists, counts, blocks, applied, coarse)
    direct[...] = coarse[...].astype(BF)
    rows_of(1 + 2 * parity[0], lists, counts, blocks, applied, coarse)
    into, rest = chip_frame(parity[0])
    relay[:, :, rest] = jnp.zeros((2, BS, 2 * BS), BF)
    relay[:, :, into] = coarse[...].astype(BF)


def make_far(parity, off_columns, labels, lists, counts, diag, off, slots, blocks, first_slots, ghosts):
    return pl.pallas_call(
        far_kernel,
        out_shape=[
            jax.ShapeDtypeStruct((NB, BS, WIDE), BF),
            jax.ShapeDtypeStruct((2, BS, WIDE), BF),
            jax.ShapeDtypeStruct((2, BS, CHIPWIDE), BF),
        ],
        in_specs=[spec(SMEM)] * 5 + [spec(pltpu.VMEM)] * 2 + [spec(ANY), spec(pltpu.VMEM)] + [spec(ANY)] * 5,
        out_specs=[spec(pltpu.VMEM)] * 3,
        scratch_shapes=[
            pltpu.VMEM((NT, BS, SLOTW), BF),
            pltpu.VMEM((4, EXTRA, BS), BF),
            pltpu.VMEM((4, 8, BS), jnp.int32),
            pltpu.SMEM((4, 8, BS), jnp.int32),
            pltpu.VMEM((FRAME, BS, BS), F32),
            pltpu.VMEM((FRAME, BS, BS), F32),
            pltpu.VMEM((2, BS, WIDE), F32),
            pltpu.SemaphoreType.DMA((2 + 4 * NG,)),
            pltpu.SemaphoreType.DMA((4,)),
        ],
        compiler_params=pltpu.CompilerParams(vmem_limit_bytes=FAR_MB * 1024 * 1024),
        cost_estimate=pl.CostEstimate(flops=4 * 10**9, bytes_accessed=20 * 10**6, transcendentals=0),
        name="far_rows",
    )(parity, off_columns, labels, lists, counts, diag, off, slots, blocks, first_slots, *ghosts)


def pair_kernel(parity, lists, counts, blocks, applied, relay, pair, coarse):
    rows_of(4 - 4 * parity[0], lists, counts, blocks, applied, coarse)
    into, rest = chip_frame(parity[0])
    pair[:, :, rest] = relay[:, :, rest]
    pair[:, :, into] = (coarse[...] + relay[:, :, into].astype(F32)).astype(BF)


def make_pair(parity, lists, counts, blocks, applied, relay):
    return pl.pallas_call(
        pair_kernel,
        out_shape=jax.ShapeDtypeStruct((2, BS, CHIPWIDE), BF),
        in_specs=[spec(SMEM)] * 3 + [spec(pltpu.VMEM)] * 3,
        out_specs=spec(pltpu.VMEM),
        scratch_shapes=[pltpu.VMEM((2, BS, WIDE), F32)],
        compiler_params=pltpu.CompilerParams(vmem_limit_bytes=22 * 1024 * 1024),
        cost_estimate=pl.CostEstimate(flops=2 * 10**9, bytes_accessed=10 * 10**6, transcendentals=0),
        name="pair_rows",
    )(parity, lists, counts, blocks, applied, relay)


def near_kernel(parity, lists, counts, blocks, applied, own, mate, coarse):
    mate_level = jnp.where(parity[0] == 1, 1, 3)

    def one(b, carry):
        t = jnp.where(b < 2, 2 * mate_level + b, b + 2)
        coarse_rows(t, b, lists, counts, blocks, applied, coarse)
        return carry

    lax.fori_loop(0, 4, one, 0)
    own[...] = coarse[2:4]
    mate[...] = coarse[0:2].astype(BF)


def make_near(parity, lists, counts, blocks, applied):
    return pl.pallas_call(
        near_kernel,
        out_shape=[
            jax.ShapeDtypeStruct((2, BS, WIDE), F32),
            jax.ShapeDtypeStruct((2, BS, WIDE), BF),
        ],
        in_specs=[spec(SMEM)] * 3 + [spec(pltpu.VMEM)] * 2,
        out_specs=[spec(pltpu.VMEM)] * 2,
        scratch_shapes=[pltpu.VMEM((4, BS, WIDE), F32)],
        compiler_params=pltpu.CompilerParams(vmem_limit_bytes=26 * 1024 * 1024),
        cost_estimate=pl.CostEstimate(flops=4 * 10**9, bytes_accessed=20 * 10**6, transcendentals=0),
        name="near_rows",
    )(parity, lists, counts, blocks, applied)


def add_near_kernel(parity, own, mate, direct, out):
    edge = 4 * BS
    out[:, :, :edge] = jnp.zeros((2, own.shape[1], edge), F32)
    out[:, :, edge + WIDE :] = jnp.zeros((2, own.shape[1], edge), F32)
    out[:, :, edge : edge + WIDE] = own[...]
    for start, piece in ((3 - 2 * parity[0], mate), (4 - 4 * parity[0], direct)):
        cols = pl.ds(pl.multiple_of(start * (2 * BS), BS), WIDE)
        out[:, :, cols] = out[:, :, cols] + piece[...].astype(F32)


def add_near(parity, own, mate, direct):
    rows = 32

    def block(width):
        return pl.BlockSpec((2, rows, width), lambda r: (0, r, 0))

    return pl.pallas_call(
        add_near_kernel,
        grid=(BS // rows,),
        out_shape=jax.ShapeDtypeStruct((2, BS, BANDWIDE), F32),
        in_specs=[spec(SMEM)] + [block(WIDE)] * 3,
        out_specs=block(BANDWIDE),
        compiler_params=pltpu.CompilerParams(vmem_limit_bytes=16 * 1024 * 1024),
        cost_estimate=pl.CostEstimate(flops=10**6, bytes_accessed=9 * 10**6, transcendentals=0),
        name="add_near",
    )(parity, own, mate, direct)


def add_pair_kernel(parity, band, pair, out, buf, sem):
    rows = BS // 4
    cols = pl.ds(pl.multiple_of(parity[0] * (6 * BS), BS), CHIPWIDE)
    stores = []
    for b in range(2):
        for r in range(4):
            part = pl.ds(r * rows, rows)
            buf[b, part] = band[b, part]
            buf[b, part, cols] = band[b, part, cols] + pair[b, part].astype(F32)
            stores.append(pltpu.make_async_copy(buf.at[b, part], out.at[b, part], sem.at[b, r]))
            stores[-1].start()
    for copy in stores:
        copy.wait()


def add_pair(parity, band, pair):
    return pl.pallas_call(
        add_pair_kernel,
        out_shape=jax.ShapeDtypeStruct((2, BS, BANDWIDE), F32),
        in_specs=[spec(SMEM)] + [spec(pltpu.VMEM)] * 2,
        out_specs=spec(ANY),
        scratch_shapes=[pltpu.VMEM((2, BS, BANDWIDE), F32), pltpu.SemaphoreType.DMA((2, 4))],
        compiler_params=pltpu.CompilerParams(vmem_limit_bytes=12 * 1024 * 1024),
        name="add_pair",
    )(parity, band, pair)


def permute_by(value, even_step, odd_step):
    count = lax.axis_size(AXES)
    pairs = [(s, s + (odd_step if s % 2 else even_step)) for s in range(count)]
    return lax.ppermute(value, AXES, [(s, t) for s, t in pairs if 0 <= t < count])


def exchange(sends):
    return [permute_by(value, *steps) for value, steps in zip(sends, STEPS)]


def local(diag_blocks, off_blocks, off_columns, tentative, aggregate, send_rows):
    off_columns = off_columns.T
    odd = lax.rem(lax.axis_index(AXES), 2)
    parity = odd.reshape(1)
    ghosts = exchange(pack(parity, send_rows, aggregate, tentative, diag_blocks))
    labels, ghost_list, ghost_count, slots, scales = local_slots(
        off_columns, aggregate, diag_blocks, off_blocks, tentative
    )
    labels, slots, *sends = ghost_slots(
        parity, send_rows, off_columns, labels, ghost_list, ghost_count, off_blocks, slots, scales, ghosts
    )
    lists, counts, blocks, first_slots = make_lists(parity, labels, slots, ghosts)
    ghosts = exchange(sends)
    applied, direct, relay = make_far(
        parity, off_columns, labels, lists, counts, diag_blocks, off_blocks, slots, blocks, first_slots, ghosts
    )
    direct_in = permute_by(direct, -2, 2)
    relay_in = permute_by(relay, 1, -1)
    pair_sum = make_pair(parity, lists, counts, blocks, applied, relay_in)
    pair_in = permute_by(pair_sum, 2, -2)
    applied, pair_sum = lax.optimization_barrier((applied, pair_sum))
    own, mate = make_near(parity, lists, counts, blocks, applied)
    mate_in = permute_by(mate, 1, -1)
    band = add_near(parity, own, mate_in, direct_in)
    return add_pair(parity, band, pair_in)


def solution(mesh):
    in_specs = (
        P(AXES, None, None),
        P(AXES, None, None, None),
        P(AXES, None),
        P(AXES, None, None),
        P(AXES),
        P(AXES, None),
    )
    return jax.shard_map(
        local, mesh=mesh, in_specs=in_specs, out_specs=P(AXES, None, None), check_vma=False
    )
```

```python
import jax
import jax.numpy as jnp
from jax import lax
from jax.experimental import pallas as pl
from jax.experimental.pallas import tpu as pltpu
from jax.sharding import PartitionSpec as P

AXES = ("bulk", "coarse")
STEPS = ((-2, 2), (2, -2), (-1, 1), (1, -1))
BS = 128
NB = 16
NG = 4
NT = NB + 4 * NG
FRAME = 18
WIDE = FRAME * BS
SLOTW = 4 * BS
SENDW = 3 * BS
CHIPWIDE = 20 * BS
BANDWIDE = 26 * BS
TILES = [slice(t * 2 * BS, (t + 1) * 2 * BS) for t in range(FRAME // 2)]
FAR_MB = 26
GROUP = 8
CHUNK = 4
EXTRA = 16
BF = jnp.bfloat16
F32 = jnp.float32
SMEM = pltpu.SMEM
ANY = pl.ANY
VMEM_LIMIT = 56 * 1024 * 1024


def spec(space):
    return pl.BlockSpec(memory_space=space)


def sent_to(odd):
    return (3 - odd, 2 + odd, 1 - odd, odd)


def came_from(odd):
    return (
        (3 - odd, 4 * odd - 2),
        (2 + odd, 2 - 4 * odd),
        (odd, 1 - 2 * odd),
        (1 - odd, 2 * odd - 1),
    )


def label_rows(values, width):
    lane = lax.broadcasted_iota(jnp.int32, (EXTRA, width), 1)
    total = jnp.zeros((EXTRA, width), jnp.int32)
    for at, value in enumerate(values):
        total = jnp.where(lane == at, value, total)
    return total.astype(F32).astype(BF)


def pack_kernel(parity, send_rows, aggregate, tent, diag, *refs):
    outs, labels, sem = refs[:4], refs[4], refs[5]
    targets = sent_to(parity[0])
    copies = []
    for at, n in enumerate(targets):
        for g in range(NG):
            row = send_rows[n, g]
            copies.append(
                pltpu.make_async_copy(tent.at[row], outs[at].at[pl.ds(g * BS, BS)], sem.at[at, g])
            )
            copies.append(
                pltpu.make_async_copy(
                    diag.at[row], outs[at].at[pl.ds((NG + g) * BS, BS)], sem.at[at, NG + g]
                )
            )
    for copy in copies:
        copy.start()
    for at, n in enumerate(targets):
        labels[at] = label_rows([aggregate[send_rows[n, g]] for g in range(NG)], BS)
        copy = pltpu.make_async_copy(
            labels.at[at], outs[at].at[pl.ds(2 * NG * BS, EXTRA)], sem.at[at, 2 * NG]
        )
        copy.start()
        copies.append(copy)
    for copy in copies:
        copy.wait()


def pack(parity, send_rows, aggregate, tent, diag):
    shape = jax.ShapeDtypeStruct((2 * NG * BS + EXTRA, BS), BF)
    return pl.pallas_call(
        pack_kernel,
        out_shape=[shape] * 4,
        in_specs=[spec(SMEM)] * 3 + [spec(pltpu.VMEM)] * 2,
        out_specs=[spec(ANY)] * 4,
        scratch_shapes=[pltpu.VMEM((4, EXTRA, BS), BF), pltpu.SemaphoreType.DMA((4, 2 * NG + 1))],
        name="pack",
    )(parity, send_rows, aggregate, tent, diag)


def first_slot(eye, block, own):
    diagonal = jnp.sum(jnp.where(eye, block.astype(F32), 0.0), axis=1, keepdims=True)
    scale = 0.6 * (1.0 / jnp.where(diagonal == 0.0, 1.0, diagonal))
    first = own.astype(F32) - scale * jnp.dot(block, own, preferred_element_type=F32)
    return first.astype(BF), scale


def local_slots_kernel(off_columns, aggregate, diag, off, tent, labels, ghost_list, ghost_count, slots, scales):
    eye = lax.broadcasted_iota(jnp.int32, (BS, BS), 0) == lax.broadcasted_iota(jnp.int32, (BS, BS), 1)
    ghost_count[0] = 0

    def row(i, carry):
        slots[i, :, :BS], scale = first_slot(eye, diag[i], tent[i])
        scales[i] = jnp.broadcast_to(scale, (BS, BS))
        labels[i, 0] = aggregate[i] + 8
        for k in range(1, 4):
            c = off_columns[k - 1, i]
            near = tent[jnp.minimum(c, NB - 1)]
            part = -scale * jnp.dot(off[i, k - 1], near, preferred_element_type=F32)
            slots[i, :, k * BS : (k + 1) * BS] = part.astype(BF)
            labels[i, k] = aggregate[jnp.minimum(c, NB - 1)] + 8
            at = ghost_count[0]
            ghost_list[at] = i * 4 + k
            ghost_count[0] = at + jnp.where(c < NB, 0, 1)
        return carry

    lax.fori_loop(0, NB, row, 0, unroll=4)
    at = ghost_count[0]
    for d in range(GROUP):
        ghost_list[at + d] = NB * 4 + 1


def local_slots(off_columns, aggregate, diag, off, tent):
    return pl.pallas_call(
        local_slots_kernel,
        out_shape=[
            jax.ShapeDtypeStruct((NB, 4), jnp.int32),
            jax.ShapeDtypeStruct((3 * NB + GROUP,), jnp.int32),
            jax.ShapeDtypeStruct((1,), jnp.int32),
            jax.ShapeDtypeStruct((NB, BS, SLOTW), BF),
            jax.ShapeDtypeStruct((NB, BS, BS), F32),
        ],
        in_specs=[spec(SMEM)] * 2 + [spec(pltpu.VMEM)] * 3,
        out_specs=[spec(SMEM)] * 3 + [spec(pltpu.VMEM)] * 2,
        compiler_params=pltpu.CompilerParams(vmem_limit_bytes=10 * 1024 * 1024),
        cost_estimate=pl.CostEstimate(flops=10**9, bytes_accessed=6 * 10**6, transcendentals=0),
        name="local_slots",
    )(off_columns, aggregate, diag, off, tent)


def ghost_slots_kernel(
    parity, send_rows, off_columns, local_labels, ghost_list, ghost_count, off, slots_in, scales,
    g0, g1, g2, g3,
    labels, slots, s0, s1, s2, s3,
    table, labels_in, label_smem, sem,
):
    ghosts, sends = (g0, g1, g2, g3), (s0, s1, s2, s3)
    arrivals = came_from(parity[0])
    for at, (n, offset) in enumerate(arrivals):
        row = ghosts[at][2 * NG * BS :, :].astype(F32).astype(jnp.int32)[:8]
        labels_in[n] = row + (8 - 2 * offset)
    to_smem = pltpu.make_async_copy(labels_in, label_smem, sem.at[0])
    to_smem.start()
    for at, (n, _) in enumerate(arrivals):
        for g in range(NG):
            table[n * NG + g] = ghosts[at][g * BS : (g + 1) * BS, :]

    def keep(i, carry):
        slots[i] = slots_in[i]
        for k in range(4):
            labels[i, k] = local_labels[i, k]
        return carry

    lax.fori_loop(0, NB, keep, 0)
    to_smem.wait()

    def group(q, carry):
        for u in range(GROUP):
            entry = ghost_list[q * GROUP + u]
            i, k = lax.div(entry, 4), lax.rem(entry, 4)
            row = jnp.minimum(i, NB - 1)
            ghost = jnp.clip(off_columns[k - 1, row] - NB, 0, 4 * NG - 1)
            part = jnp.dot(off[row, k - 1], table[ghost], preferred_element_type=F32)
            part = -scales[row] * part
            slots[i, :, pl.ds(pl.multiple_of(k * BS, BS), BS)] = part.astype(BF)
            labels[i, k] = label_smem[lax.div(ghost, NG), 0, lax.rem(ghost, NG)]
        return carry

    lax.fori_loop(0, lax.div(ghost_count[0] + GROUP - 1, GROUP), group, 0)

    for at, n in enumerate(sent_to(parity[0])):
        for g in range(NG):
            sends[at][g * BS : (g + 1) * BS, :] = slots[send_rows[n, g], :, BS:]
        values = [labels[send_rows[n, g], k] for g in range(NG) for k in range(4)]
        sends[at][NG * BS :, :] = label_rows(values, SENDW)


def ghost_slots(parity, send_rows, off_columns, local_labels, ghost_list, ghost_count, off, slots_in, scales, ghosts):
    send = jax.ShapeDtypeStruct((NG * BS + EXTRA, SENDW), BF)
    return pl.pallas_call(
        ghost_slots_kernel,
        out_shape=[
            jax.ShapeDtypeStruct((NB + 1, 4), jnp.int32),
            jax.ShapeDtypeStruct((NB + 1, BS, SLOTW), BF),
        ]
        + [send] * 4,
        in_specs=[spec(SMEM)] * 6 + [spec(pltpu.VMEM)] * 7,
        out_specs=[spec(SMEM)] + [spec(pltpu.VMEM)] * 5,
        scratch_shapes=[
            pltpu.VMEM((4 * NG, BS, BS), BF),
            pltpu.VMEM((4, 8, BS), jnp.int32),
            pltpu.SMEM((4, 8, BS), jnp.int32),
            pltpu.SemaphoreType.DMA((1,)),
        ],
        compiler_params=pltpu.CompilerParams(vmem_limit_bytes=16 * 1024 * 1024),
        name="ghost_slots",
    )(parity, send_rows, off_columns, local_labels, ghost_list, ghost_count, off, slots_in, scales, *ghosts)


def lists_kernel(parity, labels, slots, g0, g1, g2, g3, lists, counts, blocks, first_slots, ghost_buf, sem):
    ghosts = (g0, g1, g2, g3)
    copies = [
        pltpu.make_async_copy(ghosts[n].at[pl.ds(0, 2 * NG * BS)], ghost_buf.at[n], sem.at[n])
        for n in range(4)
    ]
    for copy in copies:
        copy.start()
    for t in range(10):
        counts[t] = 0

    def row(i, carry):
        for k in range(4):
            blocks[i * 4 + k] = slots[i, :, k * BS : (k + 1) * BS].T
            t = jnp.clip(labels[i, k] - 4, 0, 9)
            at = counts[t]
            lists[t, at] = i * 4 + k
            counts[t] = at + 1
        return carry

    lax.fori_loop(0, NB, row, 0, unroll=2)
    blocks[4 * NB] = jnp.zeros((BS, BS), BF)
    for t in range(10):
        at = counts[t]
        for d in range(CHUNK - 1):
            lists[t, at + d] = 4 * NB
        counts[t] = lax.div(at + CHUNK - 1, CHUNK)
    for copy in copies:
        copy.wait()
    eye = lax.broadcasted_iota(jnp.int32, (BS, BS), 0) == lax.broadcasted_iota(jnp.int32, (BS, BS), 1)

    for at, (n, _) in enumerate(came_from(parity[0])):
        for g in range(NG):
            first_slots[n * NG + g] = first_slot(
                eye, ghost_buf[at, (NG + g) * BS : (NG + g + 1) * BS], ghost_buf[at, g * BS : (g + 1) * BS]
            )[0]


def make_lists(parity, labels, slots, ghosts):
    return pl.pallas_call(
        lists_kernel,
        out_shape=[
            jax.ShapeDtypeStruct((10, 4 * NB + CHUNK), jnp.int32),
            jax.ShapeDtypeStruct((10,), jnp.int32),
            jax.ShapeDtypeStruct((4 * NB + 1, BS, BS), BF),
            jax.ShapeDtypeStruct((4 * NG, BS, BS), BF),
        ],
        in_specs=[spec(SMEM)] * 2 + [spec(pltpu.VMEM)] + [spec(ANY)] * 4,
        out_specs=[spec(SMEM)] * 2 + [spec(pltpu.VMEM)] * 2,
        scratch_shapes=[pltpu.VMEM((4, 2 * NG * BS, BS), BF), pltpu.SemaphoreType.DMA((4,))],
        compiler_params=pltpu.CompilerParams(vmem_limit_bytes=12 * 1024 * 1024),
        cost_estimate=pl.CostEstimate(flops=10**8, bytes_accessed=6 * 10**6, transcendentals=0),
        name="lists",
    )(parity, labels, slots, *ghosts)


def coarse_rows(t, at, lists, counts, blocks, applied, coarse):
    def chunk(q, carry):
        entries = [lists[t, q * CHUNK + u] for u in range(CHUNK)]
        left = jnp.concatenate([blocks[e] for e in entries], axis=1)
        rows = [jnp.minimum(lax.div(e, 4), NB - 1) for e in entries]
        for cols in TILES:
            right = jnp.concatenate([applied[r, :, cols] for r in rows], axis=0)
            res = jnp.dot(left, right, preferred_element_type=F32)
            coarse[at, :, cols] = coarse[at, :, cols] + res
        return carry

    coarse[at] = jnp.zeros((BS, WIDE), F32)
    lax.fori_loop(0, counts[t], chunk, 0)


def rows_of(level, lists, counts, blocks, applied, coarse):
    def one(b, carry):
        coarse_rows(2 * level + b, b, lists, counts, blocks, applied, coarse)
        return carry

    lax.fori_loop(0, 2, one, 0)


def chip_frame(odd):
    into = pl.ds(pl.multiple_of(odd * (2 * BS), BS), WIDE)
    return into, pl.ds(pl.multiple_of((1 - odd) * WIDE, BS), 2 * BS)


def far_kernel(
    parity, off_columns, labels, lists, counts, diag, off, slots, blocks, first_slots, g0, g1, g2, g3,
    applied, direct, relay,
    table, labels_vmem, label_smem, total_a, total_b, coarse, sem,
):
    ghosts = (g0, g1, g2, g3)
    arrivals = came_from(parity[0])
    for at, (n, offset) in enumerate(arrivals):
        row = ghosts[at][NG * BS :, :BS].astype(F32).astype(jnp.int32)[:8]
        labels_vmem[n] = row - 2 * offset
    to_smem = pltpu.make_async_copy(labels_vmem, label_smem, sem.at[0])
    to_smem.start()

    def keep(i, carry):
        table[i] = slots[i]
        table[NB + i, :, :BS] = first_slots[i]
        return carry

    lax.fori_loop(0, NB, keep, 0)
    for at, (n, _) in enumerate(arrivals):
        for g in range(NG):
            table[NB + n * NG + g, :, BS:] = ghosts[at][g * BS : (g + 1) * BS, :]
    to_smem.wait()

    def label_of(j, m):
        ghost = jnp.maximum(j - NB, 0)
        remote = label_smem[lax.div(ghost, NG), 0, lax.rem(ghost, NG) * 4 + m]
        local = labels[jnp.minimum(j, NB - 1), m]
        return jnp.clip(jnp.where(j < NB, local, remote), 0, FRAME - 1)

    def row(i, total):
        total[...] = jnp.zeros_like(total)
        for k in range(4):
            j = i if k == 0 else off_columns[k - 1, i]
            block = diag[i] if k == 0 else off[i, k - 1]
            prod = jnp.dot(block, table[j], preferred_element_type=F32)
            for m in range(4):
                at = label_of(j, m)
                total[at] = total[at] + prod[:, m * BS : (m + 1) * BS]
        for at in range(FRAME):
            applied[i, :, at * BS : (at + 1) * BS] = total[at].astype(BF)

    def row_pair(q, carry):
        row(2 * q, total_a)
        row(2 * q + 1, total_b)
        return carry

    lax.fori_loop(0, NB // 2, row_pair, 0)
    rows_of(4 * parity[0], lists, counts, blocks, applied, coarse)
    direct[...] = coarse[...].astype(BF)
    rows_of(1 + 2 * parity[0], lists, counts, blocks, applied, coarse)
    into, rest = chip_frame(parity[0])
    relay[:, :, rest] = jnp.zeros((2, BS, 2 * BS), BF)
    relay[:, :, into] = coarse[...].astype(BF)


def make_far(parity, off_columns, labels, lists, counts, diag, off, slots, blocks, first_slots, ghosts):
    return pl.pallas_call(
        far_kernel,
        out_shape=[
            jax.ShapeDtypeStruct((NB, BS, WIDE), BF),
            jax.ShapeDtypeStruct((2, BS, WIDE), BF),
            jax.ShapeDtypeStruct((2, BS, CHIPWIDE), BF),
        ],
        in_specs=[spec(SMEM)] * 5 + [spec(pltpu.VMEM)] * 9,
        out_specs=[spec(pltpu.VMEM)] * 3,
        scratch_shapes=[
            pltpu.VMEM((NT, BS, SLOTW), BF),
            pltpu.VMEM((4, 8, BS), jnp.int32),
            pltpu.SMEM((4, 8, BS), jnp.int32),
            pltpu.VMEM((FRAME, BS, BS), F32),
            pltpu.VMEM((FRAME, BS, BS), F32),
            pltpu.VMEM((2, BS, WIDE), F32),
            pltpu.SemaphoreType.DMA((1,)),
        ],
        compiler_params=pltpu.CompilerParams(vmem_limit_bytes=FAR_MB * 1024 * 1024),
        cost_estimate=pl.CostEstimate(flops=4 * 10**9, bytes_accessed=20 * 10**6, transcendentals=0),
        name="far_rows",
    )(parity, off_columns, labels, lists, counts, diag, off, slots, blocks, first_slots, *ghosts)


def pair_kernel(parity, lists, counts, blocks, applied, relay, pair, coarse):
    rows_of(4 - 4 * parity[0], lists, counts, blocks, applied, coarse)
    into, rest = chip_frame(parity[0])
    pair[:, :, rest] = relay[:, :, rest]
    pair[:, :, into] = (coarse[...] + relay[:, :, into].astype(F32)).astype(BF)


def make_pair(parity, lists, counts, blocks, applied, relay):
    return pl.pallas_call(
        pair_kernel,
        out_shape=jax.ShapeDtypeStruct((2, BS, CHIPWIDE), BF),
        in_specs=[spec(SMEM)] * 3 + [spec(pltpu.VMEM)] * 3,
        out_specs=spec(pltpu.VMEM),
        scratch_shapes=[pltpu.VMEM((2, BS, WIDE), F32)],
        compiler_params=pltpu.CompilerParams(vmem_limit_bytes=22 * 1024 * 1024),
        cost_estimate=pl.CostEstimate(flops=2 * 10**9, bytes_accessed=10 * 10**6, transcendentals=0),
        name="pair_rows",
    )(parity, lists, counts, blocks, applied, relay)


def near_kernel(parity, lists, counts, blocks, applied, own, mate, coarse):
    mate_level = jnp.where(parity[0] == 1, 1, 3)

    def one(b, carry):
        t = jnp.where(b < 2, 2 * mate_level + b, b + 2)
        coarse_rows(t, b, lists, counts, blocks, applied, coarse)
        return carry

    lax.fori_loop(0, 4, one, 0)
    own[...] = coarse[2:4]
    mate[...] = coarse[0:2].astype(BF)


def make_near(parity, lists, counts, blocks, applied):
    return pl.pallas_call(
        near_kernel,
        out_shape=[
            jax.ShapeDtypeStruct((2, BS, WIDE), F32),
            jax.ShapeDtypeStruct((2, BS, WIDE), BF),
        ],
        in_specs=[spec(SMEM)] * 3 + [spec(pltpu.VMEM)] * 2,
        out_specs=[spec(pltpu.VMEM)] * 2,
        scratch_shapes=[pltpu.VMEM((4, BS, WIDE), F32)],
        compiler_params=pltpu.CompilerParams(vmem_limit_bytes=26 * 1024 * 1024),
        cost_estimate=pl.CostEstimate(flops=4 * 10**9, bytes_accessed=20 * 10**6, transcendentals=0),
        name="near_rows",
    )(parity, lists, counts, blocks, applied)


def add_near_kernel(parity, own, mate, direct, out):
    edge = 4 * BS
    out[:, :, :edge] = jnp.zeros((2, own.shape[1], edge), F32)
    out[:, :, edge + WIDE :] = jnp.zeros((2, own.shape[1], edge), F32)
    out[:, :, edge : edge + WIDE] = own[...]
    for start, piece in ((3 - 2 * parity[0], mate), (4 - 4 * parity[0], direct)):
        cols = pl.ds(pl.multiple_of(start * (2 * BS), BS), WIDE)
        out[:, :, cols] = out[:, :, cols] + piece[...].astype(F32)


def add_near(parity, own, mate, direct):
    rows = 32

    def block(width):
        return pl.BlockSpec((2, rows, width), lambda r: (0, r, 0))

    return pl.pallas_call(
        add_near_kernel,
        grid=(BS // rows,),
        out_shape=jax.ShapeDtypeStruct((2, BS, BANDWIDE), F32),
        in_specs=[spec(SMEM)] + [block(WIDE)] * 3,
        out_specs=block(BANDWIDE),
        compiler_params=pltpu.CompilerParams(vmem_limit_bytes=16 * 1024 * 1024),
        cost_estimate=pl.CostEstimate(flops=10**6, bytes_accessed=9 * 10**6, transcendentals=0),
        name="add_near",
    )(parity, own, mate, direct)


def add_pair_kernel(parity, band, pair, out, buf, sem):
    rows = BS // 4
    cols = pl.ds(pl.multiple_of(parity[0] * (6 * BS), BS), CHIPWIDE)
    stores = []
    for b in range(2):
        for r in range(4):
            part = pl.ds(r * rows, rows)
            buf[b, part] = band[b, part]
            buf[b, part, cols] = band[b, part, cols] + pair[b, part].astype(F32)
            stores.append(pltpu.make_async_copy(buf.at[b, part], out.at[b, part], sem.at[b, r]))
            stores[-1].start()
    for copy in stores:
        copy.wait()


def add_pair(parity, band, pair):
    return pl.pallas_call(
        add_pair_kernel,
        out_shape=jax.ShapeDtypeStruct((2, BS, BANDWIDE), F32),
        in_specs=[spec(SMEM)] + [spec(pltpu.VMEM)] * 2,
        out_specs=spec(ANY),
        scratch_shapes=[pltpu.VMEM((2, BS, BANDWIDE), F32), pltpu.SemaphoreType.DMA((2, 4))],
        compiler_params=pltpu.CompilerParams(vmem_limit_bytes=12 * 1024 * 1024),
        name="add_pair",
    )(parity, band, pair)


def permute_by(value, even_step, odd_step):
    count = lax.axis_size(AXES)
    pairs = [(s, s + (odd_step if s % 2 else even_step)) for s in range(count)]
    return lax.ppermute(value, AXES, [(s, t) for s, t in pairs if 0 <= t < count])


def exchange(sends):
    return [permute_by(value, *steps) for value, steps in zip(sends, STEPS)]


def local(diag_blocks, off_blocks, off_columns, tentative, aggregate, send_rows):
    off_columns = off_columns.T
    odd = lax.rem(lax.axis_index(AXES), 2)
    parity = odd.reshape(1)
    ghosts = exchange(pack(parity, send_rows, aggregate, tentative, diag_blocks))
    labels, ghost_list, ghost_count, slots, scales = local_slots(
        off_columns, aggregate, diag_blocks, off_blocks, tentative
    )
    labels, slots, *sends = ghost_slots(
        parity, send_rows, off_columns, labels, ghost_list, ghost_count, off_blocks, slots, scales, ghosts
    )
    lists, counts, blocks, first_slots = make_lists(parity, labels, slots, ghosts)
    ghosts = exchange(sends)
    applied, direct, relay = make_far(
        parity, off_columns, labels, lists, counts, diag_blocks, off_blocks, slots, blocks, first_slots, ghosts
    )
    direct_in = permute_by(direct, -2, 2)
    relay_in = permute_by(relay, 1, -1)
    pair_sum = make_pair(parity, lists, counts, blocks, applied, relay_in)
    pair_in = permute_by(pair_sum, 2, -2)
    applied, pair_sum = lax.optimization_barrier((applied, pair_sum))
    own, mate = make_near(parity, lists, counts, blocks, applied)
    mate_in = permute_by(mate, 1, -1)
    band = add_near(parity, own, mate_in, direct_in)
    return add_pair(parity, band, pair_in)


def solution(mesh):
    in_specs = (
        P(AXES, None, None),
        P(AXES, None, None, None),
        P(AXES, None),
        P(AXES, None, None),
        P(AXES),
        P(AXES, None),
    )
    return jax.shard_map(
        local, mesh=mesh, in_specs=in_specs, out_specs=P(AXES, None, None), check_vma=False
    )
```

```python
import jax
import jax.numpy as jnp
from jax import lax
from jax.experimental import pallas as pl
from jax.experimental.pallas import tpu as pltpu
from jax.sharding import PartitionSpec as P

AXES = ("bulk", "coarse")
STEPS = ((-2, 2), (2, -2), (-1, 1), (1, -1))
TENT_ORDER = (0, 1, 2, 3)
SLOT_ORDER = (0, 2, 1, 3)
BS = 128
NB = 16
NG = 4
NT = NB + 4 * NG
FRAME = 18
WIDE = FRAME * BS
SLOTW = 4 * BS
SENDW = 3 * BS
CHIPWIDE = 20 * BS
BANDWIDE = 26 * BS
TILES = [slice(t * 2 * BS, (t + 1) * 2 * BS) for t in range(FRAME // 2)]
FAR_MB = 26
GROUP = 8
CHUNK = 4
EXTRA = 16
BF = jnp.bfloat16
F32 = jnp.float32
SMEM = pltpu.SMEM
ANY = pl.ANY
VMEM_LIMIT = 56 * 1024 * 1024


def spec(space):
    return pl.BlockSpec(memory_space=space)


def sent_to(odd, order):
    all_four = (3 - odd, 2 + odd, 1 - odd, odd)
    return [all_four[at] for at in order]


def came_from(odd, order):
    all_four = (
        (3 - odd, 4 * odd - 2),
        (2 + odd, 2 - 4 * odd),
        (odd, 1 - 2 * odd),
        (1 - odd, 2 * odd - 1),
    )
    return [all_four[at] for at in order]


def label_rows(values, width):
    lane = lax.broadcasted_iota(jnp.int32, (EXTRA, width), 1)
    total = jnp.zeros((EXTRA, width), jnp.int32)
    for at, value in enumerate(values):
        total = jnp.where(lane == at, value, total)
    return total.astype(F32).astype(BF)


def pack_kernel(parity, send_rows, aggregate, tent, diag, *refs):
    outs, labels, sem = refs[:4], refs[4], refs[5]
    targets = sent_to(parity[0], TENT_ORDER)
    copies = []
    for at, n in enumerate(targets):
        for g in range(NG):
            row = send_rows[n, g]
            copies.append(
                pltpu.make_async_copy(tent.at[row], outs[at].at[pl.ds(g * BS, BS)], sem.at[at, g])
            )
            copies.append(
                pltpu.make_async_copy(
                    diag.at[row], outs[at].at[pl.ds((NG + g) * BS, BS)], sem.at[at, NG + g]
                )
            )
    for copy in copies:
        copy.start()
    for at, n in enumerate(targets):
        labels[at] = label_rows([aggregate[send_rows[n, g]] for g in range(NG)], BS)
        copy = pltpu.make_async_copy(
            labels.at[at], outs[at].at[pl.ds(2 * NG * BS, EXTRA)], sem.at[at, 2 * NG]
        )
        copy.start()
        copies.append(copy)
    for copy in copies:
        copy.wait()


def pack(parity, send_rows, aggregate, tent, diag):
    shape = jax.ShapeDtypeStruct((2 * NG * BS + EXTRA, BS), BF)
    return pl.pallas_call(
        pack_kernel,
        out_shape=[shape] * 4,
        in_specs=[spec(SMEM)] * 3 + [spec(pltpu.VMEM)] * 2,
        out_specs=[spec(ANY)] * 4,
        scratch_shapes=[pltpu.VMEM((4, EXTRA, BS), BF), pltpu.SemaphoreType.DMA((4, 2 * NG + 1))],
        name="pack",
    )(parity, send_rows, aggregate, tent, diag)


def first_slot(eye, block, own):
    diagonal = jnp.sum(jnp.where(eye, block.astype(F32), 0.0), axis=1, keepdims=True)
    scale = 0.6 * (1.0 / jnp.where(diagonal == 0.0, 1.0, diagonal))
    first = own.astype(F32) - scale * jnp.dot(block, own, preferred_element_type=F32)
    return first.astype(BF), scale


def local_slots_kernel(off_columns, aggregate, diag, off, tent, labels, ghost_list, ghost_count, slots, scales):
    eye = lax.broadcasted_iota(jnp.int32, (BS, BS), 0) == lax.broadcasted_iota(jnp.int32, (BS, BS), 1)
    ghost_count[0] = 0

    def row(i, carry):
        slots[i, :, :BS], scale = first_slot(eye, diag[i], tent[i])
        scales[i] = jnp.broadcast_to(scale, (BS, BS))
        labels[i, 0] = aggregate[i] + 8
        for k in range(1, 4):
            c = off_columns[k - 1, i]
            near = tent[jnp.minimum(c, NB - 1)]
            part = -scale * jnp.dot(off[i, k - 1], near, preferred_element_type=F32)
            slots[i, :, k * BS : (k + 1) * BS] = part.astype(BF)
            labels[i, k] = aggregate[jnp.minimum(c, NB - 1)] + 8
            at = ghost_count[0]
            ghost_list[at] = i * 4 + k
            ghost_count[0] = at + jnp.where(c < NB, 0, 1)
        return carry

    lax.fori_loop(0, NB, row, 0, unroll=4)
    at = ghost_count[0]
    for d in range(GROUP):
        ghost_list[at + d] = NB * 4 + 1


def local_slots(off_columns, aggregate, diag, off, tent):
    return pl.pallas_call(
        local_slots_kernel,
        out_shape=[
            jax.ShapeDtypeStruct((NB, 4), jnp.int32),
            jax.ShapeDtypeStruct((3 * NB + GROUP,), jnp.int32),
            jax.ShapeDtypeStruct((1,), jnp.int32),
            jax.ShapeDtypeStruct((NB, BS, SLOTW), BF),
            jax.ShapeDtypeStruct((NB, BS, BS), F32),
        ],
        in_specs=[spec(SMEM)] * 2 + [spec(pltpu.VMEM)] * 3,
        out_specs=[spec(SMEM)] * 3 + [spec(pltpu.VMEM)] * 2,
        compiler_params=pltpu.CompilerParams(vmem_limit_bytes=10 * 1024 * 1024),
        cost_estimate=pl.CostEstimate(flops=10**9, bytes_accessed=6 * 10**6, transcendentals=0),
        name="local_slots",
    )(off_columns, aggregate, diag, off, tent)


def ghost_slots_kernel(
    parity, send_rows, off_columns, local_labels, ghost_list, ghost_count, off, slots_in, scales,
    g0, g1, g2, g3,
    labels, slots, s0, s1, s2, s3,
    table, labels_in, label_smem, sem,
):
    ghosts, sends = (g0, g1, g2, g3), (s0, s1, s2, s3)
    arrivals = came_from(parity[0], TENT_ORDER)
    for at, (n, offset) in enumerate(arrivals):
        row = ghosts[at][2 * NG * BS :, :].astype(F32).astype(jnp.int32)[:8]
        labels_in[n] = row + (8 - 2 * offset)
    to_smem = pltpu.make_async_copy(labels_in, label_smem, sem.at[0])
    to_smem.start()
    for at, (n, _) in enumerate(arrivals):
        for g in range(NG):
            table[n * NG + g] = ghosts[at][g * BS : (g + 1) * BS, :]

    def keep(i, carry):
        slots[i] = slots_in[i]
        for k in range(4):
            labels[i, k] = local_labels[i, k]
        return carry

    lax.fori_loop(0, NB, keep, 0)
    to_smem.wait()

    def group(q, carry):
        for u in range(GROUP):
            entry = ghost_list[q * GROUP + u]
            i, k = lax.div(entry, 4), lax.rem(entry, 4)
            row = jnp.minimum(i, NB - 1)
            ghost = jnp.clip(off_columns[k - 1, row] - NB, 0, 4 * NG - 1)
            part = jnp.dot(off[row, k - 1], table[ghost], preferred_element_type=F32)
            part = -scales[row] * part
            slots[i, :, pl.ds(pl.multiple_of(k * BS, BS), BS)] = part.astype(BF)
            labels[i, k] = label_smem[lax.div(ghost, NG), 0, lax.rem(ghost, NG)]
        return carry

    lax.fori_loop(0, lax.div(ghost_count[0] + GROUP - 1, GROUP), group, 0)

    for at, n in enumerate(sent_to(parity[0], SLOT_ORDER)):
        for g in range(NG):
            sends[at][g * BS : (g + 1) * BS, :] = slots[send_rows[n, g], :, BS:]
        values = [labels[send_rows[n, g], k] for g in range(NG) for k in range(4)]
        sends[at][NG * BS :, :] = label_rows(values, SENDW)


def ghost_slots(parity, send_rows, off_columns, local_labels, ghost_list, ghost_count, off, slots_in, scales, ghosts):
    send = jax.ShapeDtypeStruct((NG * BS + EXTRA, SENDW), BF)
    return pl.pallas_call(
        ghost_slots_kernel,
        out_shape=[
            jax.ShapeDtypeStruct((NB + 1, 4), jnp.int32),
            jax.ShapeDtypeStruct((NB + 1, BS, SLOTW), BF),
        ]
        + [send] * 4,
        in_specs=[spec(SMEM)] * 6 + [spec(pltpu.VMEM)] * 7,
        out_specs=[spec(SMEM)] + [spec(pltpu.VMEM)] * 5,
        scratch_shapes=[
            pltpu.VMEM((4 * NG, BS, BS), BF),
            pltpu.VMEM((4, 8, BS), jnp.int32),
            pltpu.SMEM((4, 8, BS), jnp.int32),
            pltpu.SemaphoreType.DMA((1,)),
        ],
        compiler_params=pltpu.CompilerParams(vmem_limit_bytes=16 * 1024 * 1024),
        name="ghost_slots",
    )(parity, send_rows, off_columns, local_labels, ghost_list, ghost_count, off, slots_in, scales, *ghosts)


def lists_kernel(parity, labels, slots, g0, g1, g2, g3, lists, counts, blocks, first_slots, ghost_buf, sem):
    ghosts = (g0, g1, g2, g3)
    copies = [
        pltpu.make_async_copy(ghosts[n].at[pl.ds(0, 2 * NG * BS)], ghost_buf.at[n], sem.at[n])
        for n in range(4)
    ]
    for copy in copies:
        copy.start()
    for t in range(10):
        counts[t] = 0

    def row(i, carry):
        for k in range(4):
            blocks[i * 4 + k] = slots[i, :, k * BS : (k + 1) * BS].T
            t = jnp.clip(labels[i, k] - 4, 0, 9)
            at = counts[t]
            lists[t, at] = i * 4 + k
            counts[t] = at + 1
        return carry

    lax.fori_loop(0, NB, row, 0, unroll=2)
    blocks[4 * NB] = jnp.zeros((BS, BS), BF)
    for t in range(10):
        at = counts[t]
        for d in range(CHUNK - 1):
            lists[t, at + d] = 4 * NB
        counts[t] = lax.div(at + CHUNK - 1, CHUNK)
    for copy in copies:
        copy.wait()
    eye = lax.broadcasted_iota(jnp.int32, (BS, BS), 0) == lax.broadcasted_iota(jnp.int32, (BS, BS), 1)

    for at, (n, _) in enumerate(came_from(parity[0], TENT_ORDER)):
        for g in range(NG):
            first_slots[n * NG + g] = first_slot(
                eye, ghost_buf[at, (NG + g) * BS : (NG + g + 1) * BS], ghost_buf[at, g * BS : (g + 1) * BS]
            )[0]


def make_lists(parity, labels, slots, ghosts):
    return pl.pallas_call(
        lists_kernel,
        out_shape=[
            jax.ShapeDtypeStruct((10, 4 * NB + CHUNK), jnp.int32),
            jax.ShapeDtypeStruct((10,), jnp.int32),
            jax.ShapeDtypeStruct((4 * NB + 1, BS, BS), BF),
            jax.ShapeDtypeStruct((4 * NG, BS, BS), BF),
        ],
        in_specs=[spec(SMEM)] * 2 + [spec(pltpu.VMEM)] + [spec(ANY)] * 4,
        out_specs=[spec(SMEM)] * 2 + [spec(pltpu.VMEM)] * 2,
        scratch_shapes=[pltpu.VMEM((4, 2 * NG * BS, BS), BF), pltpu.SemaphoreType.DMA((4,))],
        compiler_params=pltpu.CompilerParams(vmem_limit_bytes=12 * 1024 * 1024),
        cost_estimate=pl.CostEstimate(flops=10**8, bytes_accessed=6 * 10**6, transcendentals=0),
        name="lists",
    )(parity, labels, slots, *ghosts)


def coarse_rows(t, at, lists, counts, blocks, applied, coarse):
    def chunk(q, carry):
        entries = [lists[t, q * CHUNK + u] for u in range(CHUNK)]
        left = jnp.concatenate([blocks[e] for e in entries], axis=1)
        rows = [jnp.minimum(lax.div(e, 4), NB - 1) for e in entries]
        for cols in TILES:
            right = jnp.concatenate([applied[r, :, cols] for r in rows], axis=0)
            res = jnp.dot(left, right, preferred_element_type=F32)
            coarse[at, :, cols] = coarse[at, :, cols] + res
        return carry

    coarse[at] = jnp.zeros((BS, WIDE), F32)
    lax.fori_loop(0, counts[t], chunk, 0)


def rows_of(level, lists, counts, blocks, applied, coarse):
    def one(b, carry):
        coarse_rows(2 * level + b, b, lists, counts, blocks, applied, coarse)
        return carry

    lax.fori_loop(0, 2, one, 0)


def chip_frame(odd):
    into = pl.ds(pl.multiple_of(odd * (2 * BS), BS), WIDE)
    return into, pl.ds(pl.multiple_of((1 - odd) * WIDE, BS), 2 * BS)


def far_kernel(
    parity, off_columns, labels, lists, counts, diag, off, slots, blocks, first_slots, g0, g1, g2, g3,
    applied, direct, relay,
    table, labels_vmem, label_smem, total_a, total_b, coarse, sem,
):
    ghosts = (g0, g1, g2, g3)
    arrivals = came_from(parity[0], SLOT_ORDER)
    for at, (n, offset) in enumerate(arrivals):
        row = ghosts[at][NG * BS :, :BS].astype(F32).astype(jnp.int32)[:8]
        labels_vmem[n] = row - 2 * offset
    to_smem = pltpu.make_async_copy(labels_vmem, label_smem, sem.at[0])
    to_smem.start()

    def keep(i, carry):
        table[i] = slots[i]
        table[NB + i, :, :BS] = first_slots[i]
        return carry

    lax.fori_loop(0, NB, keep, 0)
    for at, (n, _) in enumerate(arrivals):
        for g in range(NG):
            table[NB + n * NG + g, :, BS:] = ghosts[at][g * BS : (g + 1) * BS, :]
    to_smem.wait()

    def label_of(j, m):
        ghost = jnp.maximum(j - NB, 0)
        remote = label_smem[lax.div(ghost, NG), 0, lax.rem(ghost, NG) * 4 + m]
        local = labels[jnp.minimum(j, NB - 1), m]
        return jnp.clip(jnp.where(j < NB, local, remote), 0, FRAME - 1)

    def row(i, total):
        total[...] = jnp.zeros_like(total)
        for k in range(4):
            j = i if k == 0 else off_columns[k - 1, i]
            block = diag[i] if k == 0 else off[i, k - 1]
            prod = jnp.dot(block, table[j], preferred_element_type=F32)
            for m in range(4):
                at = label_of(j, m)
                total[at] = total[at] + prod[:, m * BS : (m + 1) * BS]
        for at in range(FRAME):
            applied[i, :, at * BS : (at + 1) * BS] = total[at].astype(BF)

    def row_pair(q, carry):
        row(2 * q, total_a)
        row(2 * q + 1, total_b)
        return carry

    lax.fori_loop(0, NB // 2, row_pair, 0)
    rows_of(4 * parity[0], lists, counts, blocks, applied, coarse)
    direct[...] = coarse[...].astype(BF)
    rows_of(1 + 2 * parity[0], lists, counts, blocks, applied, coarse)
    into, rest = chip_frame(parity[0])
    relay[:, :, rest] = jnp.zeros((2, BS, 2 * BS), BF)
    relay[:, :, into] = coarse[...].astype(BF)


def make_far(parity, off_columns, labels, lists, counts, diag, off, slots, blocks, first_slots, ghosts):
    return pl.pallas_call(
        far_kernel,
        out_shape=[
            jax.ShapeDtypeStruct((NB, BS, WIDE), BF),
            jax.ShapeDtypeStruct((2, BS, WIDE), BF),
            jax.ShapeDtypeStruct((2, BS, CHIPWIDE), BF),
        ],
        in_specs=[spec(SMEM)] * 5 + [spec(pltpu.VMEM)] * 9,
        out_specs=[spec(pltpu.VMEM)] * 3,
        scratch_shapes=[
            pltpu.VMEM((NT, BS, SLOTW), BF),
            pltpu.VMEM((4, 8, BS), jnp.int32),
            pltpu.SMEM((4, 8, BS), jnp.int32),
            pltpu.VMEM((FRAME, BS, BS), F32),
            pltpu.VMEM((FRAME, BS, BS), F32),
            pltpu.VMEM((2, BS, WIDE), F32),
            pltpu.SemaphoreType.DMA((1,)),
        ],
        compiler_params=pltpu.CompilerParams(vmem_limit_bytes=FAR_MB * 1024 * 1024),
        cost_estimate=pl.CostEstimate(flops=4 * 10**9, bytes_accessed=20 * 10**6, transcendentals=0),
        name="far_rows",
    )(parity, off_columns, labels, lists, counts, diag, off, slots, blocks, first_slots, *ghosts)


def pair_kernel(parity, lists, counts, blocks, applied, relay, pair, coarse):
    rows_of(4 - 4 * parity[0], lists, counts, blocks, applied, coarse)
    into, rest = chip_frame(parity[0])
    pair[:, :, rest] = relay[:, :, rest]
    pair[:, :, into] = (coarse[...] + relay[:, :, into].astype(F32)).astype(BF)


def make_pair(parity, lists, counts, blocks, applied, relay):
    return pl.pallas_call(
        pair_kernel,
        out_shape=jax.ShapeDtypeStruct((2, BS, CHIPWIDE), BF),
        in_specs=[spec(SMEM)] * 3 + [spec(pltpu.VMEM)] * 3,
        out_specs=spec(pltpu.VMEM),
        scratch_shapes=[pltpu.VMEM((2, BS, WIDE), F32)],
        compiler_params=pltpu.CompilerParams(vmem_limit_bytes=22 * 1024 * 1024),
        cost_estimate=pl.CostEstimate(flops=2 * 10**9, bytes_accessed=10 * 10**6, transcendentals=0),
        name="pair_rows",
    )(parity, lists, counts, blocks, applied, relay)


def near_kernel(parity, lists, counts, blocks, applied, own, mate, coarse):
    mate_level = jnp.where(parity[0] == 1, 1, 3)

    def one(b, carry):
        t = jnp.where(b < 2, 2 * mate_level + b, b + 2)
        coarse_rows(t, b, lists, counts, blocks, applied, coarse)
        return carry

    lax.fori_loop(0, 4, one, 0)
    own[...] = coarse[2:4]
    mate[...] = coarse[0:2].astype(BF)


def make_near(parity, lists, counts, blocks, applied):
    return pl.pallas_call(
        near_kernel,
        out_shape=[
            jax.ShapeDtypeStruct((2, BS, WIDE), F32),
            jax.ShapeDtypeStruct((2, BS, WIDE), BF),
        ],
        in_specs=[spec(SMEM)] * 3 + [spec(pltpu.VMEM)] * 2,
        out_specs=[spec(pltpu.VMEM)] * 2,
        scratch_shapes=[pltpu.VMEM((4, BS, WIDE), F32)],
        compiler_params=pltpu.CompilerParams(vmem_limit_bytes=26 * 1024 * 1024),
        cost_estimate=pl.CostEstimate(flops=4 * 10**9, bytes_accessed=20 * 10**6, transcendentals=0),
        name="near_rows",
    )(parity, lists, counts, blocks, applied)


def add_near_kernel(parity, own, mate, direct, out):
    edge = 4 * BS
    out[:, :, :edge] = jnp.zeros((2, own.shape[1], edge), F32)
    out[:, :, edge + WIDE :] = jnp.zeros((2, own.shape[1], edge), F32)
    out[:, :, edge : edge + WIDE] = own[...]
    for start, piece in ((3 - 2 * parity[0], mate), (4 - 4 * parity[0], direct)):
        cols = pl.ds(pl.multiple_of(start * (2 * BS), BS), WIDE)
        out[:, :, cols] = out[:, :, cols] + piece[...].astype(F32)


def add_near(parity, own, mate, direct):
    rows = 32

    def block(width):
        return pl.BlockSpec((2, rows, width), lambda r: (0, r, 0))

    return pl.pallas_call(
        add_near_kernel,
        grid=(BS // rows,),
        out_shape=jax.ShapeDtypeStruct((2, BS, BANDWIDE), F32),
        in_specs=[spec(SMEM)] + [block(WIDE)] * 3,
        out_specs=block(BANDWIDE),
        compiler_params=pltpu.CompilerParams(vmem_limit_bytes=16 * 1024 * 1024),
        cost_estimate=pl.CostEstimate(flops=10**6, bytes_accessed=9 * 10**6, transcendentals=0),
        name="add_near",
    )(parity, own, mate, direct)


def add_pair_kernel(parity, band, pair, out, buf, sem):
    rows = BS // 4
    cols = pl.ds(pl.multiple_of(parity[0] * (6 * BS), BS), CHIPWIDE)
    stores = []
    for b in range(2):
        for r in range(4):
            part = pl.ds(r * rows, rows)
            buf[b, part] = band[b, part]
            buf[b, part, cols] = band[b, part, cols] + pair[b, part].astype(F32)
            stores.append(pltpu.make_async_copy(buf.at[b, part], out.at[b, part], sem.at[b, r]))
            stores[-1].start()
    for copy in stores:
        copy.wait()


def add_pair(parity, band, pair):
    return pl.pallas_call(
        add_pair_kernel,
        out_shape=jax.ShapeDtypeStruct((2, BS, BANDWIDE), F32),
        in_specs=[spec(SMEM)] + [spec(pltpu.VMEM)] * 2,
        out_specs=spec(ANY),
        scratch_shapes=[pltpu.VMEM((2, BS, BANDWIDE), F32), pltpu.SemaphoreType.DMA((2, 4))],
        compiler_params=pltpu.CompilerParams(vmem_limit_bytes=12 * 1024 * 1024),
        name="add_pair",
    )(parity, band, pair)


def permute_by(value, even_step, odd_step):
    count = lax.axis_size(AXES)
    pairs = [(s, s + (odd_step if s % 2 else even_step)) for s in range(count)]
    return lax.ppermute(value, AXES, [(s, t) for s, t in pairs if 0 <= t < count])


def exchange(sends, order):
    return [permute_by(value, *STEPS[at]) for value, at in zip(sends, order)]


def local(diag_blocks, off_blocks, off_columns, tentative, aggregate, send_rows):
    off_columns = off_columns.T
    odd = lax.rem(lax.axis_index(AXES), 2)
    parity = odd.reshape(1)
    ghosts = exchange(pack(parity, send_rows, aggregate, tentative, diag_blocks), TENT_ORDER)
    labels, ghost_list, ghost_count, slots, scales = local_slots(
        off_columns, aggregate, diag_blocks, off_blocks, tentative
    )
    labels, slots, *sends = ghost_slots(
        parity, send_rows, off_columns, labels, ghost_list, ghost_count, off_blocks, slots, scales, ghosts
    )
    lists, counts, blocks, first_slots = make_lists(parity, labels, slots, ghosts)
    ghosts = exchange(sends, SLOT_ORDER)
    applied, direct, relay = make_far(
        parity, off_columns, labels, lists, counts, diag_blocks, off_blocks, slots, blocks, first_slots, ghosts
    )
    direct_in = permute_by(direct, -2, 2)
    relay_in = permute_by(relay, 1, -1)
    pair_sum = make_pair(parity, lists, counts, blocks, applied, relay_in)
    pair_in = permute_by(pair_sum, 2, -2)
    applied, pair_sum = lax.optimization_barrier((applied, pair_sum))
    own, mate = make_near(parity, lists, counts, blocks, applied)
    mate_in = permute_by(mate, 1, -1)
    band = add_near(parity, own, mate_in, direct_in)
    return add_pair(parity, band, pair_in)


def solution(mesh):
    in_specs = (
        P(AXES, None, None),
        P(AXES, None, None, None),
        P(AXES, None),
        P(AXES, None, None),
        P(AXES),
        P(AXES, None),
    )
    return jax.shard_map(
        local, mesh=mesh, in_specs=in_specs, out_specs=P(AXES, None, None), check_vma=False
    )
```

```python
import jax
import jax.numpy as jnp
from jax import lax
from jax.experimental import pallas as pl
from jax.experimental.pallas import tpu as pltpu
from jax.sharding import PartitionSpec as P

AXES = ("bulk", "coarse")
STEPS = ((-2, 2), (2, -2), (-1, 1), (1, -1))
TENT_ORDER = (0, 1, 2, 3)
SLOT_ORDER = (0, 2, 1, 3)
BS = 128
NB = 16
NG = 4
NT = NB + 4 * NG
FRAME = 18
WIDE = FRAME * BS
SLOTW = 4 * BS
SENDW = 3 * BS
CHIPWIDE = 20 * BS
BANDWIDE = 26 * BS
TILES = [slice(t * 2 * BS, (t + 1) * 2 * BS) for t in range(FRAME // 2)]
FAR_MB = 26
GROUP = 12
CHUNK = 4
EXTRA = 16
BF = jnp.bfloat16
F32 = jnp.float32
SMEM = pltpu.SMEM
ANY = pl.ANY
VMEM_LIMIT = 56 * 1024 * 1024


def spec(space):
    return pl.BlockSpec(memory_space=space)


def sent_to(odd, order):
    all_four = (3 - odd, 2 + odd, 1 - odd, odd)
    return [all_four[at] for at in order]


def came_from(odd, order):
    all_four = (
        (3 - odd, 4 * odd - 2),
        (2 + odd, 2 - 4 * odd),
        (odd, 1 - 2 * odd),
        (1 - odd, 2 * odd - 1),
    )
    return [all_four[at] for at in order]


def label_rows(values, width):
    lane = lax.broadcasted_iota(jnp.int32, (EXTRA, width), 1)
    total = jnp.zeros((EXTRA, width), jnp.int32)
    for at, value in enumerate(values):
        total = jnp.where(lane == at, value, total)
    return total.astype(F32).astype(BF)


def pack_kernel(parity, send_rows, aggregate, tent, diag, *refs):
    outs, labels, sem = refs[:4], refs[4], refs[5]
    targets = sent_to(parity[0], TENT_ORDER)
    copies = []
    for at, n in enumerate(targets):
        for g in range(NG):
            row = send_rows[n, g]
            copies.append(
                pltpu.make_async_copy(tent.at[row], outs[at].at[pl.ds(g * BS, BS)], sem.at[at, g])
            )
            copies.append(
                pltpu.make_async_copy(
                    diag.at[row], outs[at].at[pl.ds((NG + g) * BS, BS)], sem.at[at, NG + g]
                )
            )
    for copy in copies:
        copy.start()
    for at, n in enumerate(targets):
        labels[at] = label_rows([aggregate[send_rows[n, g]] for g in range(NG)], BS)
        copy = pltpu.make_async_copy(
            labels.at[at], outs[at].at[pl.ds(2 * NG * BS, EXTRA)], sem.at[at, 2 * NG]
        )
        copy.start()
        copies.append(copy)
    for copy in copies:
        copy.wait()


def pack(parity, send_rows, aggregate, tent, diag):
    shape = jax.ShapeDtypeStruct((2 * NG * BS + EXTRA, BS), BF)
    return pl.pallas_call(
        pack_kernel,
        out_shape=[shape] * 4,
        in_specs=[spec(SMEM)] * 3 + [spec(pltpu.VMEM)] * 2,
        out_specs=[spec(ANY)] * 4,
        scratch_shapes=[pltpu.VMEM((4, EXTRA, BS), BF), pltpu.SemaphoreType.DMA((4, 2 * NG + 1))],
        name="pack",
    )(parity, send_rows, aggregate, tent, diag)


def first_slot(eye, block, own):
    diagonal = jnp.sum(jnp.where(eye, block.astype(F32), 0.0), axis=1, keepdims=True)
    scale = 0.6 * (1.0 / jnp.where(diagonal == 0.0, 1.0, diagonal))
    first = own.astype(F32) - scale * jnp.dot(block, own, preferred_element_type=F32)
    return first.astype(BF), scale


def local_slots_kernel(off_columns, aggregate, diag, off, tent, labels, ghost_list, ghost_count, slots, scales):
    eye = lax.broadcasted_iota(jnp.int32, (BS, BS), 0) == lax.broadcasted_iota(jnp.int32, (BS, BS), 1)
    ghost_count[0] = 0

    def row(i, carry):
        slots[i, :, :BS], scale = first_slot(eye, diag[i], tent[i])
        scales[i] = jnp.broadcast_to(scale, (BS, BS))
        labels[i, 0] = aggregate[i] + 8
        for k in range(1, 4):
            c = off_columns[k - 1, i]
            near = tent[jnp.minimum(c, NB - 1)]
            part = -scale * jnp.dot(off[i, k - 1], near, preferred_element_type=F32)
            slots[i, :, k * BS : (k + 1) * BS] = part.astype(BF)
            labels[i, k] = aggregate[jnp.minimum(c, NB - 1)] + 8
            at = ghost_count[0]
            ghost_list[at] = i * 4 + k
            ghost_count[0] = at + jnp.where(c < NB, 0, 1)
        return carry

    lax.fori_loop(0, NB, row, 0, unroll=4)
    at = ghost_count[0]
    for d in range(GROUP):
        ghost_list[at + d] = NB * 4 + 1


def local_slots(off_columns, aggregate, diag, off, tent):
    return pl.pallas_call(
        local_slots_kernel,
        out_shape=[
            jax.ShapeDtypeStruct((NB, 4), jnp.int32),
            jax.ShapeDtypeStruct((3 * NB + GROUP,), jnp.int32),
            jax.ShapeDtypeStruct((1,), jnp.int32),
            jax.ShapeDtypeStruct((NB, BS, SLOTW), BF),
            jax.ShapeDtypeStruct((NB, BS, BS), F32),
        ],
        in_specs=[spec(SMEM)] * 2 + [spec(pltpu.VMEM)] * 3,
        out_specs=[spec(SMEM)] * 3 + [spec(pltpu.VMEM)] * 2,
        compiler_params=pltpu.CompilerParams(vmem_limit_bytes=10 * 1024 * 1024),
        cost_estimate=pl.CostEstimate(flops=10**9, bytes_accessed=6 * 10**6, transcendentals=0),
        name="local_slots",
    )(off_columns, aggregate, diag, off, tent)


def ghost_slots_kernel(
    parity, send_rows, off_columns, local_labels, ghost_list, ghost_count, off, slots_in, scales,
    g0, g1, g2, g3,
    labels, slots, s0, s1, s2, s3,
    table, labels_in, label_smem, sem,
):
    ghosts, sends = (g0, g1, g2, g3), (s0, s1, s2, s3)
    arrivals = came_from(parity[0], TENT_ORDER)
    for at, (n, offset) in enumerate(arrivals):
        row = ghosts[at][2 * NG * BS :, :].astype(F32).astype(jnp.int32)[:8]
        labels_in[n] = row + (8 - 2 * offset)
    to_smem = pltpu.make_async_copy(labels_in, label_smem, sem.at[0])
    to_smem.start()
    for at, (n, _) in enumerate(arrivals):
        for g in range(NG):
            table[n * NG + g] = ghosts[at][g * BS : (g + 1) * BS, :]

    def keep(i, carry):
        slots[i] = slots_in[i]
        for k in range(4):
            labels[i, k] = local_labels[i, k]
        return carry

    lax.fori_loop(0, NB, keep, 0)
    to_smem.wait()

    def group(q, carry):
        for u in range(GROUP):
            entry = ghost_list[q * GROUP + u]
            i, k = lax.div(entry, 4), lax.rem(entry, 4)
            row = jnp.minimum(i, NB - 1)
            ghost = jnp.clip(off_columns[k - 1, row] - NB, 0, 4 * NG - 1)
            part = jnp.dot(off[row, k - 1], table[ghost], preferred_element_type=F32)
            part = -scales[row] * part
            slots[i, :, pl.ds(pl.multiple_of(k * BS, BS), BS)] = part.astype(BF)
            labels[i, k] = label_smem[lax.div(ghost, NG), 0, lax.rem(ghost, NG)]
        return carry

    lax.fori_loop(0, lax.div(ghost_count[0] + GROUP - 1, GROUP), group, 0)

    for at, n in enumerate(sent_to(parity[0], SLOT_ORDER)):
        for g in range(NG):
            sends[at][g * BS : (g + 1) * BS, :] = slots[send_rows[n, g], :, BS:]
        values = [labels[send_rows[n, g], k] for g in range(NG) for k in range(4)]
        sends[at][NG * BS :, :] = label_rows(values, SENDW)


def ghost_slots(parity, send_rows, off_columns, local_labels, ghost_list, ghost_count, off, slots_in, scales, ghosts):
    send = jax.ShapeDtypeStruct((NG * BS + EXTRA, SENDW), BF)
    return pl.pallas_call(
        ghost_slots_kernel,
        out_shape=[
            jax.ShapeDtypeStruct((NB + 1, 4), jnp.int32),
            jax.ShapeDtypeStruct((NB + 1, BS, SLOTW), BF),
        ]
        + [send] * 4,
        in_specs=[spec(SMEM)] * 6 + [spec(pltpu.VMEM)] * 7,
        out_specs=[spec(SMEM)] + [spec(pltpu.VMEM)] * 5,
        scratch_shapes=[
            pltpu.VMEM((4 * NG, BS, BS), BF),
            pltpu.VMEM((4, 8, BS), jnp.int32),
            pltpu.SMEM((4, 8, BS), jnp.int32),
            pltpu.SemaphoreType.DMA((1,)),
        ],
        compiler_params=pltpu.CompilerParams(vmem_limit_bytes=16 * 1024 * 1024),
        name="ghost_slots",
    )(parity, send_rows, off_columns, local_labels, ghost_list, ghost_count, off, slots_in, scales, *ghosts)


def lists_kernel(parity, labels, slots, g0, g1, g2, g3, lists, counts, blocks, first_slots, ghost_buf, sem):
    ghosts = (g0, g1, g2, g3)
    copies = [
        pltpu.make_async_copy(ghosts[n].at[pl.ds(0, 2 * NG * BS)], ghost_buf.at[n], sem.at[n])
        for n in range(4)
    ]
    for copy in copies:
        copy.start()
    for t in range(10):
        counts[t] = 0

    def row(i, carry):
        for k in range(4):
            blocks[i * 4 + k] = slots[i, :, k * BS : (k + 1) * BS].T
            t = jnp.clip(labels[i, k] - 4, 0, 9)
            at = counts[t]
            lists[t, at] = i * 4 + k
            counts[t] = at + 1
        return carry

    lax.fori_loop(0, NB, row, 0, unroll=2)
    blocks[4 * NB] = jnp.zeros((BS, BS), BF)
    for t in range(10):
        at = counts[t]
        for d in range(CHUNK - 1):
            lists[t, at + d] = 4 * NB
        counts[t] = lax.div(at + CHUNK - 1, CHUNK)
    for copy in copies:
        copy.wait()
    eye = lax.broadcasted_iota(jnp.int32, (BS, BS), 0) == lax.broadcasted_iota(jnp.int32, (BS, BS), 1)

    for at, (n, _) in enumerate(came_from(parity[0], TENT_ORDER)):
        for g in range(NG):
            first_slots[n * NG + g] = first_slot(
                eye, ghost_buf[at, (NG + g) * BS : (NG + g + 1) * BS], ghost_buf[at, g * BS : (g + 1) * BS]
            )[0]


def make_lists(parity, labels, slots, ghosts):
    return pl.pallas_call(
        lists_kernel,
        out_shape=[
            jax.ShapeDtypeStruct((10, 4 * NB + CHUNK), jnp.int32),
            jax.ShapeDtypeStruct((10,), jnp.int32),
            jax.ShapeDtypeStruct((4 * NB + 1, BS, BS), BF),
            jax.ShapeDtypeStruct((4 * NG, BS, BS), BF),
        ],
        in_specs=[spec(SMEM)] * 2 + [spec(pltpu.VMEM)] + [spec(ANY)] * 4,
        out_specs=[spec(SMEM)] * 2 + [spec(pltpu.VMEM)] * 2,
        scratch_shapes=[pltpu.VMEM((4, 2 * NG * BS, BS), BF), pltpu.SemaphoreType.DMA((4,))],
        compiler_params=pltpu.CompilerParams(vmem_limit_bytes=12 * 1024 * 1024),
        cost_estimate=pl.CostEstimate(flops=10**8, bytes_accessed=6 * 10**6, transcendentals=0),
        name="lists",
    )(parity, labels, slots, *ghosts)


def coarse_rows(t, at, lists, counts, blocks, applied, coarse):
    def chunk(q, carry):
        entries = [lists[t, q * CHUNK + u] for u in range(CHUNK)]
        left = jnp.concatenate([blocks[e] for e in entries], axis=1)
        rows = [jnp.minimum(lax.div(e, 4), NB - 1) for e in entries]
        for cols in TILES:
            right = jnp.concatenate([applied[r, :, cols] for r in rows], axis=0)
            res = jnp.dot(left, right, preferred_element_type=F32)
            coarse[at, :, cols] = coarse[at, :, cols] + res
        return carry

    coarse[at] = jnp.zeros((BS, WIDE), F32)
    lax.fori_loop(0, counts[t], chunk, 0)


def rows_of(level, lists, counts, blocks, applied, coarse):
    def one(b, carry):
        coarse_rows(2 * level + b, b, lists, counts, blocks, applied, coarse)
        return carry

    lax.fori_loop(0, 2, one, 0)


def chip_frame(odd):
    into = pl.ds(pl.multiple_of(odd * (2 * BS), BS), WIDE)
    return into, pl.ds(pl.multiple_of((1 - odd) * WIDE, BS), 2 * BS)


def far_kernel(
    parity, off_columns, labels, lists, counts, diag, off, slots, blocks, first_slots, g0, g1, g2, g3,
    applied, direct, relay,
    table, labels_vmem, label_smem, total_a, total_b, coarse, sem,
):
    ghosts = (g0, g1, g2, g3)
    arrivals = came_from(parity[0], SLOT_ORDER)
    for at, (n, offset) in enumerate(arrivals):
        row = ghosts[at][NG * BS :, :BS].astype(F32).astype(jnp.int32)[:8]
        labels_vmem[n] = row - 2 * offset
    to_smem = pltpu.make_async_copy(labels_vmem, label_smem, sem.at[0])
    to_smem.start()

    def keep(i, carry):
        table[i] = slots[i]
        table[NB + i, :, :BS] = first_slots[i]
        return carry

    lax.fori_loop(0, NB, keep, 0)
    for at, (n, _) in enumerate(arrivals):
        for g in range(NG):
            table[NB + n * NG + g, :, BS:] = ghosts[at][g * BS : (g + 1) * BS, :]
    to_smem.wait()

    def label_of(j, m):
        ghost = jnp.maximum(j - NB, 0)
        remote = label_smem[lax.div(ghost, NG), 0, lax.rem(ghost, NG) * 4 + m]
        local = labels[jnp.minimum(j, NB - 1), m]
        return jnp.clip(jnp.where(j < NB, local, remote), 0, FRAME - 1)

    def row_pair(q, carry):
        pair = ((2 * q, total_a), (2 * q + 1, total_b))
        for _, total in pair:
            total[...] = jnp.zeros_like(total)
        for k in range(4):
            prods = []
            for i, _ in pair:
                j = i if k == 0 else off_columns[k - 1, i]
                block = diag[i] if k == 0 else off[i, k - 1]
                prods.append(jnp.dot(block, table[j], preferred_element_type=F32))
            for (i, total), prod in zip(pair, prods):
                j = i if k == 0 else off_columns[k - 1, i]
                for m in range(4):
                    at = label_of(j, m)
                    total[at] = total[at] + prod[:, m * BS : (m + 1) * BS]
        for i, total in pair:
            for at in range(FRAME):
                applied[i, :, at * BS : (at + 1) * BS] = total[at].astype(BF)
        return carry

    lax.fori_loop(0, NB // 2, row_pair, 0)
    rows_of(4 * parity[0], lists, counts, blocks, applied, coarse)
    direct[...] = coarse[...].astype(BF)
    rows_of(1 + 2 * parity[0], lists, counts, blocks, applied, coarse)
    into, rest = chip_frame(parity[0])
    relay[:, :, rest] = jnp.zeros((2, BS, 2 * BS), BF)
    relay[:, :, into] = coarse[...].astype(BF)


def make_far(parity, off_columns, labels, lists, counts, diag, off, slots, blocks, first_slots, ghosts):
    return pl.pallas_call(
        far_kernel,
        out_shape=[
            jax.ShapeDtypeStruct((NB, BS, WIDE), BF),
            jax.ShapeDtypeStruct((2, BS, WIDE), BF),
            jax.ShapeDtypeStruct((2, BS, CHIPWIDE), BF),
        ],
        in_specs=[spec(SMEM)] * 5 + [spec(pltpu.VMEM)] * 9,
        out_specs=[spec(pltpu.VMEM)] * 3,
        scratch_shapes=[
            pltpu.VMEM((NT, BS, SLOTW), BF),
            pltpu.VMEM((4, 8, BS), jnp.int32),
            pltpu.SMEM((4, 8, BS), jnp.int32),
            pltpu.VMEM((FRAME, BS, BS), F32),
            pltpu.VMEM((FRAME, BS, BS), F32),
            pltpu.VMEM((2, BS, WIDE), F32),
            pltpu.SemaphoreType.DMA((1,)),
        ],
        compiler_params=pltpu.CompilerParams(vmem_limit_bytes=FAR_MB * 1024 * 1024),
        cost_estimate=pl.CostEstimate(flops=4 * 10**9, bytes_accessed=20 * 10**6, transcendentals=0),
        name="far_rows",
    )(parity, off_columns, labels, lists, counts, diag, off, slots, blocks, first_slots, *ghosts)


def pair_kernel(parity, lists, counts, blocks, applied, relay, pair, coarse):
    rows_of(4 - 4 * parity[0], lists, counts, blocks, applied, coarse)
    into, rest = chip_frame(parity[0])
    pair[:, :, rest] = relay[:, :, rest]
    pair[:, :, into] = (coarse[...] + relay[:, :, into].astype(F32)).astype(BF)


def make_pair(parity, lists, counts, blocks, applied, relay):
    return pl.pallas_call(
        pair_kernel,
        out_shape=jax.ShapeDtypeStruct((2, BS, CHIPWIDE), BF),
        in_specs=[spec(SMEM)] * 3 + [spec(pltpu.VMEM)] * 3,
        out_specs=spec(pltpu.VMEM),
        scratch_shapes=[pltpu.VMEM((2, BS, WIDE), F32)],
        compiler_params=pltpu.CompilerParams(vmem_limit_bytes=22 * 1024 * 1024),
        cost_estimate=pl.CostEstimate(flops=2 * 10**9, bytes_accessed=10 * 10**6, transcendentals=0),
        name="pair_rows",
    )(parity, lists, counts, blocks, applied, relay)


def near_kernel(parity, lists, counts, blocks, applied, own, mate, coarse):
    mate_level = jnp.where(parity[0] == 1, 1, 3)

    def one(b, carry):
        t = jnp.where(b < 2, 2 * mate_level + b, b + 2)
        coarse_rows(t, b, lists, counts, blocks, applied, coarse)
        return carry

    lax.fori_loop(0, 4, one, 0)
    own[...] = coarse[2:4]
    mate[...] = coarse[0:2].astype(BF)


def make_near(parity, lists, counts, blocks, applied):
    return pl.pallas_call(
        near_kernel,
        out_shape=[
            jax.ShapeDtypeStruct((2, BS, WIDE), F32),
            jax.ShapeDtypeStruct((2, BS, WIDE), BF),
        ],
        in_specs=[spec(SMEM)] * 3 + [spec(pltpu.VMEM)] * 2,
        out_specs=[spec(pltpu.VMEM)] * 2,
        scratch_shapes=[pltpu.VMEM((4, BS, WIDE), F32)],
        compiler_params=pltpu.CompilerParams(vmem_limit_bytes=26 * 1024 * 1024),
        cost_estimate=pl.CostEstimate(flops=4 * 10**9, bytes_accessed=20 * 10**6, transcendentals=0),
        name="near_rows",
    )(parity, lists, counts, blocks, applied)


def add_near_kernel(parity, own, mate, direct, out):
    edge = 4 * BS
    out[:, :, :edge] = jnp.zeros((2, own.shape[1], edge), F32)
    out[:, :, edge + WIDE :] = jnp.zeros((2, own.shape[1], edge), F32)
    out[:, :, edge : edge + WIDE] = own[...]
    for start, piece in ((3 - 2 * parity[0], mate), (4 - 4 * parity[0], direct)):
        cols = pl.ds(pl.multiple_of(start * (2 * BS), BS), WIDE)
        out[:, :, cols] = out[:, :, cols] + piece[...].astype(F32)


def add_near(parity, own, mate, direct):
    rows = 32

    def block(width):
        return pl.BlockSpec((2, rows, width), lambda r: (0, r, 0))

    return pl.pallas_call(
        add_near_kernel,
        grid=(BS // rows,),
        out_shape=jax.ShapeDtypeStruct((2, BS, BANDWIDE), F32),
        in_specs=[spec(SMEM)] + [block(WIDE)] * 3,
        out_specs=block(BANDWIDE),
        compiler_params=pltpu.CompilerParams(vmem_limit_bytes=16 * 1024 * 1024),
        cost_estimate=pl.CostEstimate(flops=10**6, bytes_accessed=9 * 10**6, transcendentals=0),
        name="add_near",
    )(parity, own, mate, direct)


def add_pair_kernel(parity, band, pair, out, buf, sem):
    rows = BS // 4
    cols = pl.ds(pl.multiple_of(parity[0] * (6 * BS), BS), CHIPWIDE)
    stores = []
    for b in range(2):
        for r in range(4):
            part = pl.ds(r * rows, rows)
            buf[b, part] = band[b, part]
            buf[b, part, cols] = band[b, part, cols] + pair[b, part].astype(F32)
            stores.append(pltpu.make_async_copy(buf.at[b, part], out.at[b, part], sem.at[b, r]))
            stores[-1].start()
    for copy in stores:
        copy.wait()


def add_pair(parity, band, pair):
    return pl.pallas_call(
        add_pair_kernel,
        out_shape=jax.ShapeDtypeStruct((2, BS, BANDWIDE), F32),
        in_specs=[spec(SMEM)] + [spec(pltpu.VMEM)] * 2,
        out_specs=spec(ANY),
        scratch_shapes=[pltpu.VMEM((2, BS, BANDWIDE), F32), pltpu.SemaphoreType.DMA((2, 4))],
        compiler_params=pltpu.CompilerParams(vmem_limit_bytes=12 * 1024 * 1024),
        name="add_pair",
    )(parity, band, pair)


def permute_by(value, even_step, odd_step):
    count = lax.axis_size(AXES)
    pairs = [(s, s + (odd_step if s % 2 else even_step)) for s in range(count)]
    return lax.ppermute(value, AXES, [(s, t) for s, t in pairs if 0 <= t < count])


def exchange(sends, order):
    return [permute_by(value, *STEPS[at]) for value, at in zip(sends, order)]


def local(diag_blocks, off_blocks, off_columns, tentative, aggregate, send_rows):
    off_columns = off_columns.T
    odd = lax.rem(lax.axis_index(AXES), 2)
    parity = odd.reshape(1)
    ghosts = exchange(pack(parity, send_rows, aggregate, tentative, diag_blocks), TENT_ORDER)
    labels, ghost_list, ghost_count, slots, scales = local_slots(
        off_columns, aggregate, diag_blocks, off_blocks, tentative
    )
    labels, slots, *sends = ghost_slots(
        parity, send_rows, off_columns, labels, ghost_list, ghost_count, off_blocks, slots, scales, ghosts
    )
    lists, counts, blocks, first_slots = make_lists(parity, labels, slots, ghosts)
    ghosts = exchange(sends, SLOT_ORDER)
    applied, direct, relay = make_far(
        parity, off_columns, labels, lists, counts, diag_blocks, off_blocks, slots, blocks, first_slots, ghosts
    )
    direct_in = permute_by(direct, -2, 2)
    relay_in = permute_by(relay, 1, -1)
    pair_sum = make_pair(parity, lists, counts, blocks, applied, relay_in)
    pair_in = permute_by(pair_sum, 2, -2)
    applied, pair_sum = lax.optimization_barrier((applied, pair_sum))
    own, mate = make_near(parity, lists, counts, blocks, applied)
    mate_in = permute_by(mate, 1, -1)
    band = add_near(parity, own, mate_in, direct_in)
    return add_pair(parity, band, pair_in)


def solution(mesh):
    in_specs = (
        P(AXES, None, None),
        P(AXES, None, None, None),
        P(AXES, None),
        P(AXES, None, None),
        P(AXES),
        P(AXES, None),
    )
    return jax.shard_map(
        local, mesh=mesh, in_specs=in_specs, out_specs=P(AXES, None, None), check_vma=False
    )
```

```python
import jax
import jax.numpy as jnp
from jax import lax
from jax.experimental import pallas as pl
from jax.experimental.pallas import tpu as pltpu
from jax.sharding import PartitionSpec as P

AXES = ("bulk", "coarse")
STEPS = ((-2, 2), (2, -2), (-1, 1), (1, -1))
TENT_ORDER = (0, 1, 2, 3)
SLOT_ORDER = (0, 2, 1, 3)
BS = 128
NB = 16
NG = 4
NT = NB + 4 * NG
FRAME = 18
WIDE = FRAME * BS
SLOTW = 4 * BS
SENDW = 3 * BS
CHIPWIDE = 20 * BS
BANDWIDE = 26 * BS
TILES = [slice(t * 2 * BS, (t + 1) * 2 * BS) for t in range(FRAME // 2)]
FAR_MB = 26
GROUP = 12
CHUNK = 6
EXTRA = 16
BF = jnp.bfloat16
F32 = jnp.float32
SMEM = pltpu.SMEM
ANY = pl.ANY
VMEM_LIMIT = 56 * 1024 * 1024


def spec(space):
    return pl.BlockSpec(memory_space=space)


def sent_to(odd, order):
    all_four = (3 - odd, 2 + odd, 1 - odd, odd)
    return [all_four[at] for at in order]


def came_from(odd, order):
    all_four = (
        (3 - odd, 4 * odd - 2),
        (2 + odd, 2 - 4 * odd),
        (odd, 1 - 2 * odd),
        (1 - odd, 2 * odd - 1),
    )
    return [all_four[at] for at in order]


def label_rows(values, width):
    lane = lax.broadcasted_iota(jnp.int32, (EXTRA, width), 1)
    total = jnp.zeros((EXTRA, width), jnp.int32)
    for at, value in enumerate(values):
        total = jnp.where(lane == at, value, total)
    return total.astype(F32).astype(BF)


def pack_kernel(parity, send_rows, aggregate, tent, diag, *refs):
    outs, labels, sem = refs[:4], refs[4], refs[5]
    targets = sent_to(parity[0], TENT_ORDER)
    copies = []
    for at, n in enumerate(targets):
        for g in range(NG):
            row = send_rows[n, g]
            copies.append(
                pltpu.make_async_copy(tent.at[row], outs[at].at[pl.ds(g * BS, BS)], sem.at[at, g])
            )
            copies.append(
                pltpu.make_async_copy(
                    diag.at[row], outs[at].at[pl.ds((NG + g) * BS, BS)], sem.at[at, NG + g]
                )
            )
    for copy in copies:
        copy.start()
    for at, n in enumerate(targets):
        labels[at] = label_rows([aggregate[send_rows[n, g]] for g in range(NG)], BS)
        copy = pltpu.make_async_copy(
            labels.at[at], outs[at].at[pl.ds(2 * NG * BS, EXTRA)], sem.at[at, 2 * NG]
        )
        copy.start()
        copies.append(copy)
    for copy in copies:
        copy.wait()


def pack(parity, send_rows, aggregate, tent, diag):
    shape = jax.ShapeDtypeStruct((2 * NG * BS + EXTRA, BS), BF)
    return pl.pallas_call(
        pack_kernel,
        out_shape=[shape] * 4,
        in_specs=[spec(SMEM)] * 3 + [spec(pltpu.VMEM)] * 2,
        out_specs=[spec(ANY)] * 4,
        scratch_shapes=[pltpu.VMEM((4, EXTRA, BS), BF), pltpu.SemaphoreType.DMA((4, 2 * NG + 1))],
        name="pack",
    )(parity, send_rows, aggregate, tent, diag)


def first_slot(eye, block, own):
    diagonal = jnp.sum(jnp.where(eye, block.astype(F32), 0.0), axis=1, keepdims=True)
    scale = 0.6 * (1.0 / jnp.where(diagonal == 0.0, 1.0, diagonal))
    first = own.astype(F32) - scale * jnp.dot(block, own, preferred_element_type=F32)
    return first.astype(BF), scale


def local_slots_kernel(off_columns, aggregate, diag, off, tent, labels, ghost_list, ghost_count, slots, scales):
    eye = lax.broadcasted_iota(jnp.int32, (BS, BS), 0) == lax.broadcasted_iota(jnp.int32, (BS, BS), 1)
    ghost_count[0] = 0

    def row(i, carry):
        slots[i, :, :BS], scale = first_slot(eye, diag[i], tent[i])
        scales[i] = jnp.broadcast_to(scale, (BS, BS))
        labels[i, 0] = aggregate[i] + 8
        for k in range(1, 4):
            c = off_columns[k - 1, i]
            near = tent[jnp.minimum(c, NB - 1)]
            part = -scale * jnp.dot(off[i, k - 1], near, preferred_element_type=F32)
            slots[i, :, k * BS : (k + 1) * BS] = part.astype(BF)
            labels[i, k] = aggregate[jnp.minimum(c, NB - 1)] + 8
            at = ghost_count[0]
            ghost_list[at] = i * 4 + k
            ghost_count[0] = at + jnp.where(c < NB, 0, 1)
        return carry

    lax.fori_loop(0, NB, row, 0, unroll=4)
    at = ghost_count[0]
    for d in range(GROUP):
        ghost_list[at + d] = NB * 4 + 1


def local_slots(off_columns, aggregate, diag, off, tent):
    return pl.pallas_call(
        local_slots_kernel,
        out_shape=[
            jax.ShapeDtypeStruct((NB, 4), jnp.int32),
            jax.ShapeDtypeStruct((3 * NB + GROUP,), jnp.int32),
            jax.ShapeDtypeStruct((1,), jnp.int32),
            jax.ShapeDtypeStruct((NB, BS, SLOTW), BF),
            jax.ShapeDtypeStruct((NB, BS, BS), F32),
        ],
        in_specs=[spec(SMEM)] * 2 + [spec(pltpu.VMEM)] * 3,
        out_specs=[spec(SMEM)] * 3 + [spec(pltpu.VMEM)] * 2,
        compiler_params=pltpu.CompilerParams(vmem_limit_bytes=10 * 1024 * 1024),
        cost_estimate=pl.CostEstimate(flops=10**9, bytes_accessed=6 * 10**6, transcendentals=0),
        name="local_slots",
    )(off_columns, aggregate, diag, off, tent)


def ghost_slots_kernel(
    parity, send_rows, off_columns, local_labels, ghost_list, ghost_count, off, slots_in, scales,
    g0, g1, g2, g3,
    labels, slots, s0, s1, s2, s3,
    table, labels_in, label_smem, sem,
):
    ghosts, sends = (g0, g1, g2, g3), (s0, s1, s2, s3)
    arrivals = came_from(parity[0], TENT_ORDER)
    for at, (n, offset) in enumerate(arrivals):
        row = ghosts[at][2 * NG * BS :, :].astype(F32).astype(jnp.int32)[:8]
        labels_in[n] = row + (8 - 2 * offset)
    to_smem = pltpu.make_async_copy(labels_in, label_smem, sem.at[0])
    to_smem.start()
    for at, (n, _) in enumerate(arrivals):
        for g in range(NG):
            table[n * NG + g] = ghosts[at][g * BS : (g + 1) * BS, :]

    def keep(i, carry):
        slots[i] = slots_in[i]
        for k in range(4):
            labels[i, k] = local_labels[i, k]
        return carry

    lax.fori_loop(0, NB, keep, 0)
    to_smem.wait()

    def group(q, carry):
        for u in range(GROUP):
            entry = ghost_list[q * GROUP + u]
            i, k = lax.div(entry, 4), lax.rem(entry, 4)
            row = jnp.minimum(i, NB - 1)
            ghost = jnp.clip(off_columns[k - 1, row] - NB, 0, 4 * NG - 1)
            part = jnp.dot(off[row, k - 1], table[ghost], preferred_element_type=F32)
            part = -scales[row] * part
            slots[i, :, pl.ds(pl.multiple_of(k * BS, BS), BS)] = part.astype(BF)
            labels[i, k] = label_smem[lax.div(ghost, NG), 0, lax.rem(ghost, NG)]
        return carry

    lax.fori_loop(0, lax.div(ghost_count[0] + GROUP - 1, GROUP), group, 0)

    for at, n in enumerate(sent_to(parity[0], SLOT_ORDER)):
        for g in range(NG):
            sends[at][g * BS : (g + 1) * BS, :] = slots[send_rows[n, g], :, BS:]
        values = [labels[send_rows[n, g], k] for g in range(NG) for k in range(4)]
        sends[at][NG * BS :, :] = label_rows(values, SENDW)


def ghost_slots(parity, send_rows, off_columns, local_labels, ghost_list, ghost_count, off, slots_in, scales, ghosts):
    send = jax.ShapeDtypeStruct((NG * BS + EXTRA, SENDW), BF)
    return pl.pallas_call(
        ghost_slots_kernel,
        out_shape=[
            jax.ShapeDtypeStruct((NB + 1, 4), jnp.int32),
            jax.ShapeDtypeStruct((NB + 1, BS, SLOTW), BF),
        ]
        + [send] * 4,
        in_specs=[spec(SMEM)] * 6 + [spec(pltpu.VMEM)] * 7,
        out_specs=[spec(SMEM)] + [spec(pltpu.VMEM)] * 5,
        scratch_shapes=[
            pltpu.VMEM((4 * NG, BS, BS), BF),
            pltpu.VMEM((4, 8, BS), jnp.int32),
            pltpu.SMEM((4, 8, BS), jnp.int32),
            pltpu.SemaphoreType.DMA((1,)),
        ],
        compiler_params=pltpu.CompilerParams(vmem_limit_bytes=16 * 1024 * 1024),
        name="ghost_slots",
    )(parity, send_rows, off_columns, local_labels, ghost_list, ghost_count, off, slots_in, scales, *ghosts)


def lists_kernel(parity, labels, slots, g0, g1, g2, g3, lists, counts, blocks, first_slots, ghost_buf, sem):
    ghosts = (g0, g1, g2, g3)
    copies = [
        pltpu.make_async_copy(ghosts[n].at[pl.ds(0, 2 * NG * BS)], ghost_buf.at[n], sem.at[n])
        for n in range(4)
    ]
    for copy in copies:
        copy.start()
    for t in range(10):
        counts[t] = 0

    def row(i, carry):
        for k in range(4):
            blocks[i * 4 + k] = slots[i, :, k * BS : (k + 1) * BS].T
            t = jnp.clip(labels[i, k] - 4, 0, 9)
            at = counts[t]
            lists[t, at] = i * 4 + k
            counts[t] = at + 1
        return carry

    lax.fori_loop(0, NB, row, 0, unroll=2)
    blocks[4 * NB] = jnp.zeros((BS, BS), BF)
    for t in range(10):
        at = counts[t]
        for d in range(CHUNK - 1):
            lists[t, at + d] = 4 * NB
        counts[t] = lax.div(at + CHUNK - 1, CHUNK)
    for copy in copies:
        copy.wait()
    eye = lax.broadcasted_iota(jnp.int32, (BS, BS), 0) == lax.broadcasted_iota(jnp.int32, (BS, BS), 1)

    for at, (n, _) in enumerate(came_from(parity[0], TENT_ORDER)):
        for g in range(NG):
            first_slots[n * NG + g] = first_slot(
                eye, ghost_buf[at, (NG + g) * BS : (NG + g + 1) * BS], ghost_buf[at, g * BS : (g + 1) * BS]
            )[0]


def make_lists(parity, labels, slots, ghosts):
    return pl.pallas_call(
        lists_kernel,
        out_shape=[
            jax.ShapeDtypeStruct((10, 4 * NB + CHUNK), jnp.int32),
            jax.ShapeDtypeStruct((10,), jnp.int32),
            jax.ShapeDtypeStruct((4 * NB + 1, BS, BS), BF),
            jax.ShapeDtypeStruct((4 * NG, BS, BS), BF),
        ],
        in_specs=[spec(SMEM)] * 2 + [spec(pltpu.VMEM)] + [spec(ANY)] * 4,
        out_specs=[spec(SMEM)] * 2 + [spec(pltpu.VMEM)] * 2,
        scratch_shapes=[pltpu.VMEM((4, 2 * NG * BS, BS), BF), pltpu.SemaphoreType.DMA((4,))],
        compiler_params=pltpu.CompilerParams(vmem_limit_bytes=12 * 1024 * 1024),
        cost_estimate=pl.CostEstimate(flops=10**8, bytes_accessed=6 * 10**6, transcendentals=0),
        name="lists",
    )(parity, labels, slots, *ghosts)


def coarse_rows(t, at, lists, counts, blocks, applied, coarse):
    def chunk(q, carry):
        entries = [lists[t, q * CHUNK + u] for u in range(CHUNK)]
        left = jnp.concatenate([blocks[e] for e in entries], axis=1)
        rows = [jnp.minimum(lax.div(e, 4), NB - 1) for e in entries]
        for cols in TILES:
            right = jnp.concatenate([applied[r, :, cols] for r in rows], axis=0)
            res = jnp.dot(left, right, preferred_element_type=F32)
            coarse[at, :, cols] = coarse[at, :, cols] + res
        return carry

    coarse[at] = jnp.zeros((BS, WIDE), F32)
    lax.fori_loop(0, counts[t], chunk, 0)


def rows_of(level, lists, counts, blocks, applied, coarse):
    def one(b, carry):
        coarse_rows(2 * level + b, b, lists, counts, blocks, applied, coarse)
        return carry

    lax.fori_loop(0, 2, one, 0)


def chip_frame(odd):
    into = pl.ds(pl.multiple_of(odd * (2 * BS), BS), WIDE)
    return into, pl.ds(pl.multiple_of((1 - odd) * WIDE, BS), 2 * BS)


def far_kernel(
    parity, off_columns, labels, lists, counts, diag, off, slots, blocks, first_slots, g0, g1, g2, g3,
    applied, direct, relay,
    table, labels_vmem, label_smem, total_a, total_b, coarse, sem,
):
    ghosts = (g0, g1, g2, g3)
    arrivals = came_from(parity[0], SLOT_ORDER)
    for at, (n, offset) in enumerate(arrivals):
        row = ghosts[at][NG * BS :, :BS].astype(F32).astype(jnp.int32)[:8]
        labels_vmem[n] = row - 2 * offset
    to_smem = pltpu.make_async_copy(labels_vmem, label_smem, sem.at[0])
    to_smem.start()

    def keep(i, carry):
        table[i] = slots[i]
        table[NB + i, :, :BS] = first_slots[i]
        return carry

    lax.fori_loop(0, NB, keep, 0)
    for at, (n, _) in enumerate(arrivals):
        for g in range(NG):
            table[NB + n * NG + g, :, BS:] = ghosts[at][g * BS : (g + 1) * BS, :]
    to_smem.wait()

    def label_of(j, m):
        ghost = jnp.maximum(j - NB, 0)
        remote = label_smem[lax.div(ghost, NG), 0, lax.rem(ghost, NG) * 4 + m]
        local = labels[jnp.minimum(j, NB - 1), m]
        return jnp.clip(jnp.where(j < NB, local, remote), 0, FRAME - 1)

    def row_pair(q, carry):
        pair = ((2 * q, total_a), (2 * q + 1, total_b))
        for _, total in pair:
            total[...] = jnp.zeros_like(total)
        for k in range(4):
            prods = []
            for i, _ in pair:
                j = i if k == 0 else off_columns[k - 1, i]
                block = diag[i] if k == 0 else off[i, k - 1]
                prods.append(jnp.dot(block, table[j], preferred_element_type=F32))
            for (i, total), prod in zip(pair, prods):
                j = i if k == 0 else off_columns[k - 1, i]
                for m in range(4):
                    at = label_of(j, m)
                    total[at] = total[at] + prod[:, m * BS : (m + 1) * BS]
        for i, total in pair:
            for at in range(FRAME):
                applied[i, :, at * BS : (at + 1) * BS] = total[at].astype(BF)
        return carry

    lax.fori_loop(0, NB // 2, row_pair, 0)
    rows_of(4 * parity[0], lists, counts, blocks, applied, coarse)
    direct[...] = coarse[...].astype(BF)
    rows_of(1 + 2 * parity[0], lists, counts, blocks, applied, coarse)
    into, rest = chip_frame(parity[0])
    relay[:, :, rest] = jnp.zeros((2, BS, 2 * BS), BF)
    relay[:, :, into] = coarse[...].astype(BF)


def make_far(parity, off_columns, labels, lists, counts, diag, off, slots, blocks, first_slots, ghosts):
    return pl.pallas_call(
        far_kernel,
        out_shape=[
            jax.ShapeDtypeStruct((NB, BS, WIDE), BF),
            jax.ShapeDtypeStruct((2, BS, WIDE), BF),
            jax.ShapeDtypeStruct((2, BS, CHIPWIDE), BF),
        ],
        in_specs=[spec(SMEM)] * 5 + [spec(pltpu.VMEM)] * 9,
        out_specs=[spec(pltpu.VMEM)] * 3,
        scratch_shapes=[
            pltpu.VMEM((NT, BS, SLOTW), BF),
            pltpu.VMEM((4, 8, BS), jnp.int32),
            pltpu.SMEM((4, 8, BS), jnp.int32),
            pltpu.VMEM((FRAME, BS, BS), F32),
            pltpu.VMEM((FRAME, BS, BS), F32),
            pltpu.VMEM((2, BS, WIDE), F32),
            pltpu.SemaphoreType.DMA((1,)),
        ],
        compiler_params=pltpu.CompilerParams(vmem_limit_bytes=FAR_MB * 1024 * 1024),
        cost_estimate=pl.CostEstimate(flops=4 * 10**9, bytes_accessed=20 * 10**6, transcendentals=0),
        name="far_rows",
    )(parity, off_columns, labels, lists, counts, diag, off, slots, blocks, first_slots, *ghosts)


def pair_kernel(parity, lists, counts, blocks, applied, relay, pair, coarse):
    rows_of(4 - 4 * parity[0], lists, counts, blocks, applied, coarse)
    into, rest = chip_frame(parity[0])
    pair[:, :, rest] = relay[:, :, rest]
    pair[:, :, into] = (coarse[...] + relay[:, :, into].astype(F32)).astype(BF)


def make_pair(parity, lists, counts, blocks, applied, relay):
    return pl.pallas_call(
        pair_kernel,
        out_shape=jax.ShapeDtypeStruct((2, BS, CHIPWIDE), BF),
        in_specs=[spec(SMEM)] * 3 + [spec(pltpu.VMEM)] * 3,
        out_specs=spec(pltpu.VMEM),
        scratch_shapes=[pltpu.VMEM((2, BS, WIDE), F32)],
        compiler_params=pltpu.CompilerParams(vmem_limit_bytes=22 * 1024 * 1024),
        cost_estimate=pl.CostEstimate(flops=2 * 10**9, bytes_accessed=10 * 10**6, transcendentals=0),
        name="pair_rows",
    )(parity, lists, counts, blocks, applied, relay)


def near_kernel(parity, lists, counts, blocks, applied, own, mate, coarse):
    mate_level = jnp.where(parity[0] == 1, 1, 3)

    def one(b, carry):
        t = jnp.where(b < 2, 2 * mate_level + b, b + 2)
        coarse_rows(t, b, lists, counts, blocks, applied, coarse)
        return carry

    lax.fori_loop(0, 4, one, 0)
    own[...] = coarse[2:4]
    mate[...] = coarse[0:2].astype(BF)


def make_near(parity, lists, counts, blocks, applied):
    return pl.pallas_call(
        near_kernel,
        out_shape=[
            jax.ShapeDtypeStruct((2, BS, WIDE), F32),
            jax.ShapeDtypeStruct((2, BS, WIDE), BF),
        ],
        in_specs=[spec(SMEM)] * 3 + [spec(pltpu.VMEM)] * 2,
        out_specs=[spec(pltpu.VMEM)] * 2,
        scratch_shapes=[pltpu.VMEM((4, BS, WIDE), F32)],
        compiler_params=pltpu.CompilerParams(vmem_limit_bytes=26 * 1024 * 1024),
        cost_estimate=pl.CostEstimate(flops=4 * 10**9, bytes_accessed=20 * 10**6, transcendentals=0),
        name="near_rows",
    )(parity, lists, counts, blocks, applied)


def add_near_kernel(parity, own, mate, direct, out):
    edge = 4 * BS
    out[:, :, :edge] = jnp.zeros((2, own.shape[1], edge), F32)
    out[:, :, edge + WIDE :] = jnp.zeros((2, own.shape[1], edge), F32)
    out[:, :, edge : edge + WIDE] = own[...]
    for start, piece in ((3 - 2 * parity[0], mate), (4 - 4 * parity[0], direct)):
        cols = pl.ds(pl.multiple_of(start * (2 * BS), BS), WIDE)
        out[:, :, cols] = out[:, :, cols] + piece[...].astype(F32)


def add_near(parity, own, mate, direct):
    rows = 32

    def block(width):
        return pl.BlockSpec((2, rows, width), lambda r: (0, r, 0))

    return pl.pallas_call(
        add_near_kernel,
        grid=(BS // rows,),
        out_shape=jax.ShapeDtypeStruct((2, BS, BANDWIDE), F32),
        in_specs=[spec(SMEM)] + [block(WIDE)] * 3,
        out_specs=block(BANDWIDE),
        compiler_params=pltpu.CompilerParams(vmem_limit_bytes=16 * 1024 * 1024),
        cost_estimate=pl.CostEstimate(flops=10**6, bytes_accessed=9 * 10**6, transcendentals=0),
        name="add_near",
    )(parity, own, mate, direct)


def add_pair_kernel(parity, band, pair, out, buf, sem):
    rows = BS // 4
    cols = pl.ds(pl.multiple_of(parity[0] * (6 * BS), BS), CHIPWIDE)
    stores = []
    for b in range(2):
        for r in range(4):
            part = pl.ds(r * rows, rows)
            buf[b, part] = band[b, part]
            buf[b, part, cols] = band[b, part, cols] + pair[b, part].astype(F32)
            stores.append(pltpu.make_async_copy(buf.at[b, part], out.at[b, part], sem.at[b, r]))
            stores[-1].start()
    for copy in stores:
        copy.wait()


def add_pair(parity, band, pair):
    return pl.pallas_call(
        add_pair_kernel,
        out_shape=jax.ShapeDtypeStruct((2, BS, BANDWIDE), F32),
        in_specs=[spec(SMEM)] + [spec(pltpu.VMEM)] * 2,
        out_specs=spec(ANY),
        scratch_shapes=[pltpu.VMEM((2, BS, BANDWIDE), F32), pltpu.SemaphoreType.DMA((2, 4))],
        compiler_params=pltpu.CompilerParams(vmem_limit_bytes=12 * 1024 * 1024),
        name="add_pair",
    )(parity, band, pair)


def permute_by(value, even_step, odd_step):
    count = lax.axis_size(AXES)
    pairs = [(s, s + (odd_step if s % 2 else even_step)) for s in range(count)]
    return lax.ppermute(value, AXES, [(s, t) for s, t in pairs if 0 <= t < count])


def exchange(sends, order):
    return [permute_by(value, *STEPS[at]) for value, at in zip(sends, order)]


def local(diag_blocks, off_blocks, off_columns, tentative, aggregate, send_rows):
    off_columns = off_columns.T
    odd = lax.rem(lax.axis_index(AXES), 2)
    parity = odd.reshape(1)
    ghosts = exchange(pack(parity, send_rows, aggregate, tentative, diag_blocks), TENT_ORDER)
    labels, ghost_list, ghost_count, slots, scales = local_slots(
        off_columns, aggregate, diag_blocks, off_blocks, tentative
    )
    labels, slots, *sends = ghost_slots(
        parity, send_rows, off_columns, labels, ghost_list, ghost_count, off_blocks, slots, scales, ghosts
    )
    lists, counts, blocks, first_slots = make_lists(parity, labels, slots, ghosts)
    ghosts = exchange(sends, SLOT_ORDER)
    applied, direct, relay = make_far(
        parity, off_columns, labels, lists, counts, diag_blocks, off_blocks, slots, blocks, first_slots, ghosts
    )
    direct_in = permute_by(direct, -2, 2)
    relay_in = permute_by(relay, 1, -1)
    pair_sum = make_pair(parity, lists, counts, blocks, applied, relay_in)
    pair_in = permute_by(pair_sum, 2, -2)
    applied, pair_sum = lax.optimization_barrier((applied, pair_sum))
    own, mate = make_near(parity, lists, counts, blocks, applied)
    mate_in = permute_by(mate, 1, -1)
    band = add_near(parity, own, mate_in, direct_in)
    return add_pair(parity, band, pair_in)


def solution(mesh):
    in_specs = (
        P(AXES, None, None),
        P(AXES, None, None, None),
        P(AXES, None),
        P(AXES, None, None),
        P(AXES),
        P(AXES, None),
    )
    return jax.shard_map(
        local, mesh=mesh, in_specs=in_specs, out_specs=P(AXES, None, None), check_vma=False
    )
```

```python
import jax
import jax.numpy as jnp
from jax import lax
from jax.experimental import pallas as pl
from jax.experimental.pallas import tpu as pltpu
from jax.sharding import PartitionSpec as P

AXES = ("bulk", "coarse")
STEPS = ((-2, 2), (2, -2), (-1, 1), (1, -1))
TENT_ORDER = (0, 1, 2, 3)
SLOT_ORDER = (0, 2, 1, 3)
BS = 128
NB = 16
NG = 4
NT = NB + 4 * NG
FRAME = 18
WIDE = FRAME * BS
SLOTW = 4 * BS
SENDW = 3 * BS
CHIPWIDE = 20 * BS
BANDWIDE = 26 * BS
TILES = [slice(t * 2 * BS, (t + 1) * 2 * BS) for t in range(FRAME // 2)]
FAR_MB = 26
GROUP = 16
CHUNK = 4
EXTRA = 16
BF = jnp.bfloat16
F32 = jnp.float32
SMEM = pltpu.SMEM
ANY = pl.ANY
VMEM_LIMIT = 56 * 1024 * 1024


def spec(space):
    return pl.BlockSpec(memory_space=space)


def sent_to(odd, order):
    all_four = (3 - odd, 2 + odd, 1 - odd, odd)
    return [all_four[at] for at in order]


def came_from(odd, order):
    all_four = (
        (3 - odd, 4 * odd - 2),
        (2 + odd, 2 - 4 * odd),
        (odd, 1 - 2 * odd),
        (1 - odd, 2 * odd - 1),
    )
    return [all_four[at] for at in order]


def label_rows(values, width):
    lane = lax.broadcasted_iota(jnp.int32, (EXTRA, width), 1)
    total = jnp.zeros((EXTRA, width), jnp.int32)
    for at, value in enumerate(values):
        total = jnp.where(lane == at, value, total)
    return total.astype(F32).astype(BF)


def pack_kernel(parity, send_rows, aggregate, tent, diag, *refs):
    outs, labels, sem = refs[:4], refs[4], refs[5]
    targets = sent_to(parity[0], TENT_ORDER)
    copies = []
    for at, n in enumerate(targets):
        for g in range(NG):
            row = send_rows[n, g]
            copies.append(
                pltpu.make_async_copy(tent.at[row], outs[at].at[pl.ds(g * BS, BS)], sem.at[at, g])
            )
            copies.append(
                pltpu.make_async_copy(
                    diag.at[row], outs[at].at[pl.ds((NG + g) * BS, BS)], sem.at[at, NG + g]
                )
            )
    for copy in copies:
        copy.start()
    for at, n in enumerate(targets):
        labels[at] = label_rows([aggregate[send_rows[n, g]] for g in range(NG)], BS)
        copy = pltpu.make_async_copy(
            labels.at[at], outs[at].at[pl.ds(2 * NG * BS, EXTRA)], sem.at[at, 2 * NG]
        )
        copy.start()
        copies.append(copy)
    for copy in copies:
        copy.wait()


def pack(parity, send_rows, aggregate, tent, diag):
    shape = jax.ShapeDtypeStruct((2 * NG * BS + EXTRA, BS), BF)
    return pl.pallas_call(
        pack_kernel,
        out_shape=[shape] * 4,
        in_specs=[spec(SMEM)] * 3 + [spec(pltpu.VMEM)] * 2,
        out_specs=[spec(ANY)] * 4,
        scratch_shapes=[pltpu.VMEM((4, EXTRA, BS), BF), pltpu.SemaphoreType.DMA((4, 2 * NG + 1))],
        name="pack",
    )(parity, send_rows, aggregate, tent, diag)


def first_slot(eye, block, own):
    diagonal = jnp.sum(jnp.where(eye, block.astype(F32), 0.0), axis=1, keepdims=True)
    scale = 0.6 * (1.0 / jnp.where(diagonal == 0.0, 1.0, diagonal))
    first = own.astype(F32) - scale * jnp.dot(block, own, preferred_element_type=F32)
    return first.astype(BF), scale


def local_slots_kernel(off_columns, aggregate, diag, off, tent, labels, ghost_list, ghost_count, slots, scales):
    eye = lax.broadcasted_iota(jnp.int32, (BS, BS), 0) == lax.broadcasted_iota(jnp.int32, (BS, BS), 1)
    ghost_count[0] = 0

    def row(i, carry):
        slots[i, :, :BS], scale = first_slot(eye, diag[i], tent[i])
        scales[i] = jnp.broadcast_to(scale, (BS, BS))
        labels[i, 0] = aggregate[i] + 8
        for k in range(1, 4):
            c = off_columns[k - 1, i]
            near = tent[jnp.minimum(c, NB - 1)]
            part = -scale * jnp.dot(off[i, k - 1], near, preferred_element_type=F32)
            slots[i, :, k * BS : (k + 1) * BS] = part.astype(BF)
            labels[i, k] = aggregate[jnp.minimum(c, NB - 1)] + 8
            at = ghost_count[0]
            ghost_list[at] = i * 4 + k
            ghost_count[0] = at + jnp.where(c < NB, 0, 1)
        return carry

    lax.fori_loop(0, NB, row, 0, unroll=4)
    at = ghost_count[0]
    for d in range(GROUP):
        ghost_list[at + d] = NB * 4 + 1


def local_slots(off_columns, aggregate, diag, off, tent):
    return pl.pallas_call(
        local_slots_kernel,
        out_shape=[
            jax.ShapeDtypeStruct((NB, 4), jnp.int32),
            jax.ShapeDtypeStruct((3 * NB + GROUP,), jnp.int32),
            jax.ShapeDtypeStruct((1,), jnp.int32),
            jax.ShapeDtypeStruct((NB, BS, SLOTW), BF),
            jax.ShapeDtypeStruct((NB, BS, BS), F32),
        ],
        in_specs=[spec(SMEM)] * 2 + [spec(pltpu.VMEM)] * 3,
        out_specs=[spec(SMEM)] * 3 + [spec(pltpu.VMEM)] * 2,
        compiler_params=pltpu.CompilerParams(vmem_limit_bytes=10 * 1024 * 1024),
        cost_estimate=pl.CostEstimate(flops=10**9, bytes_accessed=6 * 10**6, transcendentals=0),
        name="local_slots",
    )(off_columns, aggregate, diag, off, tent)


def ghost_slots_kernel(
    parity, send_rows, off_columns, local_labels, ghost_list, ghost_count, off, slots_in, scales,
    g0, g1, g2, g3,
    labels, slots, s0, s1, s2, s3,
    table, labels_in, label_smem, sem,
):
    ghosts, sends = (g0, g1, g2, g3), (s0, s1, s2, s3)
    arrivals = came_from(parity[0], TENT_ORDER)
    for at, (n, offset) in enumerate(arrivals):
        row = ghosts[at][2 * NG * BS :, :].astype(F32).astype(jnp.int32)[:8]
        labels_in[n] = row + (8 - 2 * offset)
    to_smem = pltpu.make_async_copy(labels_in, label_smem, sem.at[0])
    to_smem.start()
    for at, (n, _) in enumerate(arrivals):
        for g in range(NG):
            table[n * NG + g] = ghosts[at][g * BS : (g + 1) * BS, :]

    def keep(i, carry):
        slots[i] = slots_in[i]
        for k in range(4):
            labels[i, k] = local_labels[i, k]
        return carry

    lax.fori_loop(0, NB, keep, 0)
    to_smem.wait()

    def group(q, carry):
        for u in range(GROUP):
            entry = ghost_list[q * GROUP + u]
            i, k = lax.div(entry, 4), lax.rem(entry, 4)
            row = jnp.minimum(i, NB - 1)
            ghost = jnp.clip(off_columns[k - 1, row] - NB, 0, 4 * NG - 1)
            part = jnp.dot(off[row, k - 1], table[ghost], preferred_element_type=F32)
            part = -scales[row] * part
            slots[i, :, pl.ds(pl.multiple_of(k * BS, BS), BS)] = part.astype(BF)
            labels[i, k] = label_smem[lax.div(ghost, NG), 0, lax.rem(ghost, NG)]
        return carry

    lax.fori_loop(0, lax.div(ghost_count[0] + GROUP - 1, GROUP), group, 0)

    for at, n in enumerate(sent_to(parity[0], SLOT_ORDER)):
        for g in range(NG):
            sends[at][g * BS : (g + 1) * BS, :] = slots[send_rows[n, g], :, BS:]
        values = [labels[send_rows[n, g], k] for g in range(NG) for k in range(4)]
        sends[at][NG * BS :, :] = label_rows(values, SENDW)


def ghost_slots(parity, send_rows, off_columns, local_labels, ghost_list, ghost_count, off, slots_in, scales, ghosts):
    send = jax.ShapeDtypeStruct((NG * BS + EXTRA, SENDW), BF)
    return pl.pallas_call(
        ghost_slots_kernel,
        out_shape=[
            jax.ShapeDtypeStruct((NB + 1, 4), jnp.int32),
            jax.ShapeDtypeStruct((NB + 1, BS, SLOTW), BF),
        ]
        + [send] * 4,
        in_specs=[spec(SMEM)] * 6 + [spec(pltpu.VMEM)] * 7,
        out_specs=[spec(SMEM)] + [spec(pltpu.VMEM)] * 5,
        scratch_shapes=[
            pltpu.VMEM((4 * NG, BS, BS), BF),
            pltpu.VMEM((4, 8, BS), jnp.int32),
            pltpu.SMEM((4, 8, BS), jnp.int32),
            pltpu.SemaphoreType.DMA((1,)),
        ],
        compiler_params=pltpu.CompilerParams(vmem_limit_bytes=16 * 1024 * 1024),
        name="ghost_slots",
    )(parity, send_rows, off_columns, local_labels, ghost_list, ghost_count, off, slots_in, scales, *ghosts)


def lists_kernel(parity, labels, slots, g0, g1, g2, g3, lists, counts, blocks, first_slots, ghost_buf, sem):
    ghosts = (g0, g1, g2, g3)
    copies = [
        pltpu.make_async_copy(ghosts[n].at[pl.ds(0, 2 * NG * BS)], ghost_buf.at[n], sem.at[n])
        for n in range(4)
    ]
    for copy in copies:
        copy.start()
    for t in range(10):
        counts[t] = 0

    def row(i, carry):
        for k in range(4):
            blocks[i * 4 + k] = slots[i, :, k * BS : (k + 1) * BS].T
            t = jnp.clip(labels[i, k] - 4, 0, 9)
            at = counts[t]
            lists[t, at] = i * 4 + k
            counts[t] = at + 1
        return carry

    lax.fori_loop(0, NB, row, 0, unroll=2)
    blocks[4 * NB] = jnp.zeros((BS, BS), BF)
    for t in range(10):
        at = counts[t]
        for d in range(CHUNK - 1):
            lists[t, at + d] = 4 * NB
        counts[t] = lax.div(at + CHUNK - 1, CHUNK)
    for copy in copies:
        copy.wait()
    eye = lax.broadcasted_iota(jnp.int32, (BS, BS), 0) == lax.broadcasted_iota(jnp.int32, (BS, BS), 1)

    for at, (n, _) in enumerate(came_from(parity[0], TENT_ORDER)):
        for g in range(NG):
            first_slots[n * NG + g] = first_slot(
                eye, ghost_buf[at, (NG + g) * BS : (NG + g + 1) * BS], ghost_buf[at, g * BS : (g + 1) * BS]
            )[0]


def make_lists(parity, labels, slots, ghosts):
    return pl.pallas_call(
        lists_kernel,
        out_shape=[
            jax.ShapeDtypeStruct((10, 4 * NB + CHUNK), jnp.int32),
            jax.ShapeDtypeStruct((10,), jnp.int32),
            jax.ShapeDtypeStruct((4 * NB + 1, BS, BS), BF),
            jax.ShapeDtypeStruct((4 * NG, BS, BS), BF),
        ],
        in_specs=[spec(SMEM)] * 2 + [spec(pltpu.VMEM)] + [spec(ANY)] * 4,
        out_specs=[spec(SMEM)] * 2 + [spec(pltpu.VMEM)] * 2,
        scratch_shapes=[pltpu.VMEM((4, 2 * NG * BS, BS), BF), pltpu.SemaphoreType.DMA((4,))],
        compiler_params=pltpu.CompilerParams(vmem_limit_bytes=12 * 1024 * 1024),
        cost_estimate=pl.CostEstimate(flops=10**8, bytes_accessed=6 * 10**6, transcendentals=0),
        name="lists",
    )(parity, labels, slots, *ghosts)


def coarse_rows(t, at, lists, counts, blocks, applied, coarse):
    def chunk(q, carry):
        entries = [lists[t, q * CHUNK + u] for u in range(CHUNK)]
        left = jnp.concatenate([blocks[e] for e in entries], axis=1)
        rows = [jnp.minimum(lax.div(e, 4), NB - 1) for e in entries]
        for cols in TILES:
            right = jnp.concatenate([applied[r, :, cols] for r in rows], axis=0)
            res = jnp.dot(left, right, preferred_element_type=F32)
            coarse[at, :, cols] = coarse[at, :, cols] + res
        return carry

    coarse[at] = jnp.zeros((BS, WIDE), F32)
    lax.fori_loop(0, counts[t], chunk, 0)


def rows_of(level, lists, counts, blocks, applied, coarse):
    def one(b, carry):
        coarse_rows(2 * level + b, b, lists, counts, blocks, applied, coarse)
        return carry

    lax.fori_loop(0, 2, one, 0)


def chip_frame(odd):
    into = pl.ds(pl.multiple_of(odd * (2 * BS), BS), WIDE)
    return into, pl.ds(pl.multiple_of((1 - odd) * WIDE, BS), 2 * BS)


def far_kernel(
    parity, off_columns, labels, lists, counts, diag, off, slots, blocks, first_slots, g0, g1, g2, g3,
    applied, direct, relay,
    table, labels_vmem, label_smem, total_a, total_b, coarse, sem,
):
    ghosts = (g0, g1, g2, g3)
    arrivals = came_from(parity[0], SLOT_ORDER)
    for at, (n, offset) in enumerate(arrivals):
        row = ghosts[at][NG * BS :, :BS].astype(F32).astype(jnp.int32)[:8]
        labels_vmem[n] = row - 2 * offset
    to_smem = pltpu.make_async_copy(labels_vmem, label_smem, sem.at[0])
    to_smem.start()

    def keep(i, carry):
        table[i] = slots[i]
        table[NB + i, :, :BS] = first_slots[i]
        return carry

    lax.fori_loop(0, NB, keep, 0)
    for at, (n, _) in enumerate(arrivals):
        for g in range(NG):
            table[NB + n * NG + g, :, BS:] = ghosts[at][g * BS : (g + 1) * BS, :]
    to_smem.wait()

    def label_of(j, m):
        ghost = jnp.maximum(j - NB, 0)
        remote = label_smem[lax.div(ghost, NG), 0, lax.rem(ghost, NG) * 4 + m]
        local = labels[jnp.minimum(j, NB - 1), m]
        return jnp.clip(jnp.where(j < NB, local, remote), 0, FRAME - 1)

    def row_pair(q, carry):
        pair = ((2 * q, total_a), (2 * q + 1, total_b))
        for _, total in pair:
            total[...] = jnp.zeros_like(total)
        for k in range(4):
            prods = []
            for i, _ in pair:
                j = i if k == 0 else off_columns[k - 1, i]
                block = diag[i] if k == 0 else off[i, k - 1]
                prods.append(jnp.dot(block, table[j], preferred_element_type=F32))
            for (i, total), prod in zip(pair, prods):
                j = i if k == 0 else off_columns[k - 1, i]
                for m in range(4):
                    at = label_of(j, m)
                    total[at] = total[at] + prod[:, m * BS : (m + 1) * BS]
        for i, total in pair:
            for at in range(FRAME):
                applied[i, :, at * BS : (at + 1) * BS] = total[at].astype(BF)
        return carry

    lax.fori_loop(0, NB // 2, row_pair, 0)
    rows_of(4 * parity[0], lists, counts, blocks, applied, coarse)
    direct[...] = coarse[...].astype(BF)
    rows_of(1 + 2 * parity[0], lists, counts, blocks, applied, coarse)
    into, rest = chip_frame(parity[0])
    relay[:, :, rest] = jnp.zeros((2, BS, 2 * BS), BF)
    relay[:, :, into] = coarse[...].astype(BF)


def make_far(parity, off_columns, labels, lists, counts, diag, off, slots, blocks, first_slots, ghosts):
    return pl.pallas_call(
        far_kernel,
        out_shape=[
            jax.ShapeDtypeStruct((NB, BS, WIDE), BF),
            jax.ShapeDtypeStruct((2, BS, WIDE), BF),
            jax.ShapeDtypeStruct((2, BS, CHIPWIDE), BF),
        ],
        in_specs=[spec(SMEM)] * 5 + [spec(pltpu.VMEM)] * 9,
        out_specs=[spec(pltpu.VMEM)] * 3,
        scratch_shapes=[
            pltpu.VMEM((NT, BS, SLOTW), BF),
            pltpu.VMEM((4, 8, BS), jnp.int32),
            pltpu.SMEM((4, 8, BS), jnp.int32),
            pltpu.VMEM((FRAME, BS, BS), F32),
            pltpu.VMEM((FRAME, BS, BS), F32),
            pltpu.VMEM((2, BS, WIDE), F32),
            pltpu.SemaphoreType.DMA((1,)),
        ],
        compiler_params=pltpu.CompilerParams(vmem_limit_bytes=FAR_MB * 1024 * 1024),
        cost_estimate=pl.CostEstimate(flops=4 * 10**9, bytes_accessed=20 * 10**6, transcendentals=0),
        name="far_rows",
    )(parity, off_columns, labels, lists, counts, diag, off, slots, blocks, first_slots, *ghosts)


def pair_kernel(parity, lists, counts, blocks, applied, relay, pair, coarse):
    rows_of(4 - 4 * parity[0], lists, counts, blocks, applied, coarse)
    into, rest = chip_frame(parity[0])
    pair[:, :, rest] = relay[:, :, rest]
    pair[:, :, into] = (coarse[...] + relay[:, :, into].astype(F32)).astype(BF)


def make_pair(parity, lists, counts, blocks, applied, relay):
    return pl.pallas_call(
        pair_kernel,
        out_shape=jax.ShapeDtypeStruct((2, BS, CHIPWIDE), BF),
        in_specs=[spec(SMEM)] * 3 + [spec(pltpu.VMEM)] * 3,
        out_specs=spec(pltpu.VMEM),
        scratch_shapes=[pltpu.VMEM((2, BS, WIDE), F32)],
        compiler_params=pltpu.CompilerParams(vmem_limit_bytes=22 * 1024 * 1024),
        cost_estimate=pl.CostEstimate(flops=2 * 10**9, bytes_accessed=10 * 10**6, transcendentals=0),
        name="pair_rows",
    )(parity, lists, counts, blocks, applied, relay)


def near_kernel(parity, lists, counts, blocks, applied, own, mate, coarse):
    mate_level = jnp.where(parity[0] == 1, 1, 3)

    def one(b, carry):
        t = jnp.where(b < 2, 2 * mate_level + b, b + 2)
        coarse_rows(t, b, lists, counts, blocks, applied, coarse)
        return carry

    lax.fori_loop(0, 4, one, 0)
    own[...] = coarse[2:4]
    mate[...] = coarse[0:2].astype(BF)


def make_near(parity, lists, counts, blocks, applied):
    return pl.pallas_call(
        near_kernel,
        out_shape=[
            jax.ShapeDtypeStruct((2, BS, WIDE), F32),
            jax.ShapeDtypeStruct((2, BS, WIDE), BF),
        ],
        in_specs=[spec(SMEM)] * 3 + [spec(pltpu.VMEM)] * 2,
        out_specs=[spec(pltpu.VMEM)] * 2,
        scratch_shapes=[pltpu.VMEM((4, BS, WIDE), F32)],
        compiler_params=pltpu.CompilerParams(vmem_limit_bytes=26 * 1024 * 1024),
        cost_estimate=pl.CostEstimate(flops=4 * 10**9, bytes_accessed=20 * 10**6, transcendentals=0),
        name="near_rows",
    )(parity, lists, counts, blocks, applied)


def add_near_kernel(parity, own, mate, direct, out):
    edge = 4 * BS
    out[:, :, :edge] = jnp.zeros((2, own.shape[1], edge), F32)
    out[:, :, edge + WIDE :] = jnp.zeros((2, own.shape[1], edge), F32)
    out[:, :, edge : edge + WIDE] = own[...]
    for start, piece in ((3 - 2 * parity[0], mate), (4 - 4 * parity[0], direct)):
        cols = pl.ds(pl.multiple_of(start * (2 * BS), BS), WIDE)
        out[:, :, cols] = out[:, :, cols] + piece[...].astype(F32)


def add_near(parity, own, mate, direct):
    rows = 32

    def block(width):
        return pl.BlockSpec((2, rows, width), lambda r: (0, r, 0))

    return pl.pallas_call(
        add_near_kernel,
        grid=(BS // rows,),
        out_shape=jax.ShapeDtypeStruct((2, BS, BANDWIDE), F32),
        in_specs=[spec(SMEM)] + [block(WIDE)] * 3,
        out_specs=block(BANDWIDE),
        compiler_params=pltpu.CompilerParams(vmem_limit_bytes=16 * 1024 * 1024),
        cost_estimate=pl.CostEstimate(flops=10**6, bytes_accessed=9 * 10**6, transcendentals=0),
        name="add_near",
    )(parity, own, mate, direct)


def add_pair_kernel(parity, band, pair, out, buf, sem):
    rows = BS // 4
    cols = pl.ds(pl.multiple_of(parity[0] * (6 * BS), BS), CHIPWIDE)
    stores = []
    for b in range(2):
        for r in range(4):
            part = pl.ds(r * rows, rows)
            buf[b, part] = band[b, part]
            buf[b, part, cols] = band[b, part, cols] + pair[b, part].astype(F32)
            stores.append(pltpu.make_async_copy(buf.at[b, part], out.at[b, part], sem.at[b, r]))
            stores[-1].start()
    for copy in stores:
        copy.wait()


def add_pair(parity, band, pair):
    return pl.pallas_call(
        add_pair_kernel,
        out_shape=jax.ShapeDtypeStruct((2, BS, BANDWIDE), F32),
        in_specs=[spec(SMEM)] + [spec(pltpu.VMEM)] * 2,
        out_specs=spec(ANY),
        scratch_shapes=[pltpu.VMEM((2, BS, BANDWIDE), F32), pltpu.SemaphoreType.DMA((2, 4))],
        compiler_params=pltpu.CompilerParams(vmem_limit_bytes=12 * 1024 * 1024),
        name="add_pair",
    )(parity, band, pair)


def permute_by(value, even_step, odd_step):
    count = lax.axis_size(AXES)
    pairs = [(s, s + (odd_step if s % 2 else even_step)) for s in range(count)]
    return lax.ppermute(value, AXES, [(s, t) for s, t in pairs if 0 <= t < count])


def exchange(sends, order):
    return [permute_by(value, *STEPS[at]) for value, at in zip(sends, order)]


def local(diag_blocks, off_blocks, off_columns, tentative, aggregate, send_rows):
    off_columns = off_columns.T
    odd = lax.rem(lax.axis_index(AXES), 2)
    parity = odd.reshape(1)
    ghosts = exchange(pack(parity, send_rows, aggregate, tentative, diag_blocks), TENT_ORDER)
    labels, ghost_list, ghost_count, slots, scales = local_slots(
        off_columns, aggregate, diag_blocks, off_blocks, tentative
    )
    labels, slots, *sends = ghost_slots(
        parity, send_rows, off_columns, labels, ghost_list, ghost_count, off_blocks, slots, scales, ghosts
    )
    lists, counts, blocks, first_slots = make_lists(parity, labels, slots, ghosts)
    ghosts = exchange(sends, SLOT_ORDER)
    applied, direct, relay = make_far(
        parity, off_columns, labels, lists, counts, diag_blocks, off_blocks, slots, blocks, first_slots, ghosts
    )
    direct_in = permute_by(direct, -2, 2)
    relay_in = permute_by(relay, 1, -1)
    pair_sum = make_pair(parity, lists, counts, blocks, applied, relay_in)
    pair_in = permute_by(pair_sum, 2, -2)
    applied, pair_sum = lax.optimization_barrier((applied, pair_sum))
    own, mate = make_near(parity, lists, counts, blocks, applied)
    mate_in = permute_by(mate, 1, -1)
    band = add_near(parity, own, mate_in, direct_in)
    return add_pair(parity, band, pair_in)


def solution(mesh):
    in_specs = (
        P(AXES, None, None),
        P(AXES, None, None, None),
        P(AXES, None),
        P(AXES, None, None),
        P(AXES),
        P(AXES, None),
    )
    return jax.shard_map(
        local, mesh=mesh, in_specs=in_specs, out_specs=P(AXES, None, None), check_vma=False
    )
```
